128 devices in a mesh: section: 2 (over y_hi), shard: 16 (over y_lo, z, core), rep: 4 (over x).
Axes of the slice: x: 4, y: 4 (y_hi: 2, y_lo: 2; y = y_hi * 2 + y_lo), z: 4, core: 2. Of those that a mesh axis runs over, the one named last changes fastest.
Arguments:
- tokens: bfloat16 [2, 7168, 1024], P(None, ('shard', 'rep')), may hold values from -6 to 6
- segment_ids: int32 [2, 64, 112], P(None, ('shard', 'rep')), may hold values from 0 to 3, never falling along the last dimension, each value on 1 to 56 neighbouring positions
- cotangent: bfloat16 [2, 7168, 1024], P(None, ('shard', 'rep')), may hold values from -6 to 6
- norm_gains: bfloat16 [2, 1024, 2], P('section', 'shard'), may hold values from 0.5 to 1.5
- w_in: bfloat16 [2, 1024, 4120], P('section', 'shard'), may hold values from -0.1875 to 0.1875
- conv_params: bfloat16 [2, 1792, 5], P('section', 'shard'), may hold values from -1.5 to 1.5
- head_params: bfloat16 [2, 24, 3], P('section'), may hold values from -6.9 to 2.77, as said below
- w_out: bfloat16 [2, 2048, 1024], P('section', 'shard'), may hold values from -0.25 to 0.25
- w_gate_up: bfloat16 [2, 1024, 4096], P('section', 'shard'), may hold values from -0.1875 to 0.1875
- w_down: bfloat16 [2, 2048, 1024], P('section', 'shard'), may hold values from -0.125 to 0.125
Outputs:
- layer_out: bfloat16 [2, 2, 7168, 1024], P('section', None, ('shard', 'rep'))
- input_grads: float32 [2, 2, 7168, 1024], P('section', None, ('shard', 'rep'))
- grad_gains: float32 [2, 1024, 2], P('section', 'shard')
- grad_w_in: float32 [2, 1024, 4120], P('section', 'shard')
- grad_conv: float32 [2, 1792, 5], P('section', 'shard')
- grad_heads: float32 [2, 24, 3], P('section')
- grad_w_out: float32 [2, 2048, 1024], P('section', 'shard')
- grad_gate_up: float32 [2, 1024, 4096], P('section', 'shard')
- grad_w_down: float32 [2, 2048, 1024], P('section', 'shard')
The draws below stay inside these ranges and needn't reach their ends.
Inputs may be any that keep to these rules, and one draw needn't show every extreme that they name: `segment_ids`: in each block of 112 slots the numbers never fall; each sequence holds 1 to 56 slots, and one holds exactly 56. `head_params`: column 0 (step bias) lies in -6.9 to -2.3, column 1 (log of the decay rate) in 0 to 2.77, column 2 (skip factor) in -1 to 1.
All inputs are finite; a program needn't handle non-finite values.
Results may differ from the reference program's by a relative error of at most 0.024.
Values may be sent and summed in bfloat16 or wider, within the bound.
A program may use at most 256 MiB of HBM per device.

```python
import math
import jax
import jax.numpy as jnp
import numpy as np
from jax import lax

D = 1024
FF = 2048
MHEADS = 24
HEAD_WIDTH = 64
STATE = 128
QUERY_HEAD_COUNT = 8
KVHEADS = 2
CONV = 4
TOK_DEV = 112
MB = 2
SSM = 1536
CH = 1792
UW = 2048
PIN = 4120
GROUPS = 64
TOKENS = 7168
N_SECTION = 2


def draw_head_params(key, part):
    key = jax.random.fold_in(key, 7)
    keys = jax.random.split(key, 3)
    shape = (2, MHEADS)
    step_bias = jax.random.uniform(keys[0], shape, jnp.float32, -6.9, -2.3)
    decay_log = jax.random.uniform(keys[1], shape, jnp.float32, 0.0, 2.77)
    skip_factor = jax.random.uniform(keys[2], shape, jnp.float32, -1.0, 1.0)
    return jnp.stack([step_bias, decay_log, skip_factor], -1).astype(jnp.bfloat16)


def steps_of(key, extent, cuts, smallest, high):
    factor_of, own = 1.0, jax.random.fold_in(key, 6)
    for position, blocks in cuts:
        heights = jnp.exp(jax.random.uniform(jax.random.fold_in(own, position), (blocks,), jnp.float32, smallest / len(cuts), high / len(cuts)))
        factor_of = factor_of * jnp.repeat(heights, extent[position] // blocks).reshape([-1 if axis == position else 1 for axis in range(len(extent))])
    return factor_of


def split_up(count, total, most, lean):
    weights = [(1 << 20) // math.isqrt(standing ** lean) + 1 for standing in range(2, count + 1)]
    surplus, counts = total - most - (count - 1), [1] * (count - 1)
    while surplus > 0:
        movable = [i for i in range(count - 1) if counts[i] < most]
        mass, budget = sum([weights[i] for i in movable]), surplus
        for i in movable:
            addition = min(most - counts[i], max(1, budget * weights[i] // mass), surplus)
            counts[i] = counts[i] + addition
            surplus = surplus - addition
    return np.array([most] + counts)


def ragged_sizes(key, count, total, bound, lean):
    if count == 2:
        one = jax.random.randint(key, (), max(1, total - bound), min(bound, total - 1) + 1)
        return jnp.stack([one, total - one])
    sizes = jnp.asarray(split_up(count, total, bound, lean), jnp.int32)
    pairs = (count - 1) // 2
    giver, receiver = sizes[1:1 + 2 * pairs:2], sizes[2:2 + 2 * pairs:2]
    slack = jnp.minimum(giver - 1, bound - receiver)
    passed = jax.random.randint(jax.random.fold_in(key, 1), (pairs,), 0, 1 << 20) % (slack + 1)
    sizes = sizes.at[1:1 + 2 * pairs:2].set(giver - passed).at[2:2 + 2 * pairs:2].set(receiver + passed)
    return sizes[jax.random.permutation(jax.random.fold_in(key, 2), count)]


def gaussian(stream_key, dims, spread, reach, cuts=(), kind=jnp.bfloat16):
    values = spread * jax.random.normal(stream_key, dims, jnp.float32)
    if cuts:
        values = values * steps_of(stream_key, dims, cuts, -0.22, 0.18)
    return jnp.clip(values, -reach, reach).astype(kind)


def setup_inputs(seed: int = 0) -> dict:
    arg_keys = jax.random.split(jax.random.key(seed), 11)
    return {
        "tokens": gaussian(arg_keys[0], (MB, TOKENS, D), 1.0, 6.0, ((1, 64),)),
        "segment_ids": jax.vmap(lambda own: jnp.searchsorted(jnp.cumsum(ragged_sizes(own, 4, TOK_DEV, TOK_DEV // 2, 2)), jnp.arange(TOK_DEV), side="right"))(jax.random.split(arg_keys[1], MB * GROUPS)).reshape((MB, GROUPS, TOK_DEV)).astype(jnp.int32),
        "cotangent": gaussian(arg_keys[2], (MB, TOKENS, D), 1.0, 6.0, ((1, 64),)),
        "norm_gains": jnp.clip(1.0 + 0.1 * jax.random.normal(arg_keys[3], (N_SECTION, D, 2), jnp.float32), 0.5, 1.5).astype(jnp.bfloat16),
        "w_in": gaussian(arg_keys[4], (N_SECTION, D, PIN), D ** -0.5, 0.1875, ((0, 2), (1, 16))),
        "conv_params": gaussian(arg_keys[5], (N_SECTION, CH, CONV + 1), 0.25, 1.5, ((0, 2), (1, 16))),
        "head_params": draw_head_params(jax.random.fold_in(arg_keys[10], 71), 0),
        "w_out": gaussian(arg_keys[7], (N_SECTION, UW, D), (UW // 4) ** -0.5, 0.25, ((0, 2), (1, 16))),
        "w_gate_up": gaussian(arg_keys[8], (N_SECTION, D, 2 * FF), D ** -0.5, 0.1875, ((0, 2), (1, 16))),
        "w_down": gaussian(arg_keys[9], (N_SECTION, FF, D), FF ** -0.5, 0.125, ((0, 2), (1, 16))),
    }


@jax.custom_vjp
def low(v):
    return lax.optimization_barrier(v.astype(jnp.bfloat16)).astype(jnp.float32)

@jax.custom_vjp
def low_back(v):
    return v

def low_keep(v):
    return (low(v), None)

def low_pass(kept, grad):
    return (grad,)

def back_keep(v):
    return (v, None)

def back_low(kept, grad):
    return (low(grad),)
low.defvjp(low_keep, low_pass)
low_back.defvjp(back_keep, back_low)

def rms_norm(values, gain):
    return values * lax.rsqrt(lax.optimization_barrier(jnp.mean(values * values, -1, keepdims=True)) + 1e-05) * gain

def mixers(projected, conv_table, head_table, segments):
    sequence_length = projected.shape[0]
    exact_result = lax.Precision.HIGHEST
    gate_z = projected[:, :SSM]
    conv_input = projected[:, SSM:SSM + CH]
    offset_qkv = SSM + CH
    query_rows = projected[:, offset_qkv:offset_qkv + QUERY_HEAD_COUNT * HEAD_WIDTH]
    key_rows = projected[:, offset_qkv + QUERY_HEAD_COUNT * HEAD_WIDTH:offset_qkv + (QUERY_HEAD_COUNT + KVHEADS) * HEAD_WIDTH]
    value_rows = projected[:, offset_qkv + (QUERY_HEAD_COUNT + KVHEADS) * HEAD_WIDTH:offset_qkv + (QUERY_HEAD_COUNT + 2 * KVHEADS) * HEAD_WIDTH]
    step_raw = projected[:, offset_qkv + (QUERY_HEAD_COUNT + 2 * KVHEADS) * HEAD_WIDTH:]
    mixed_in = conv_table[:, CONV] + conv_input * conv_table[:, 0]
    for offset in range(1, CONV):
        shifted = jnp.concatenate([jnp.zeros((offset, CH), conv_input.dtype), conv_input[:sequence_length - offset]], 0)
        linked = jnp.concatenate([jnp.zeros((offset,), bool), segments[offset:] == segments[:sequence_length - offset]])
        mixed_in = mixed_in + jnp.where(linked[:, None], shifted, 0.0) * conv_table[:, offset]
    activated = jax.nn.silu(mixed_in)
    states = activated[:, :SSM].reshape(sequence_length, MHEADS, HEAD_WIDTH)
    inputs_b = activated[:, SSM:SSM + STATE]
    outputs_c = activated[:, SSM + STATE:]
    step_size = jax.nn.softplus(step_raw + head_table[:, 0])
    decay_log = -step_size * jnp.exp(head_table[:, 1])
    running = jnp.cumsum(decay_log, 0)
    places = jnp.arange(sequence_length)
    allowed = (segments[:, None] == segments[None, :]) & (places[:, None] >= places[None, :])
    distance = running[:, None, :] - running[None, :, :]
    kernel_rows = jnp.where(allowed[:, :, None], jnp.exp(jnp.where(allowed[:, :, None], distance, 0.0)), 0.0)
    intersection = jnp.dot(outputs_c, inputs_b.T, precision=exact_result)
    kernel_rows = kernel_rows * intersection[:, :, None] * step_size[None, :, :]
    ssm_out = jnp.einsum('tsh,shp->thp', kernel_rows, states, precision=exact_result) + head_table[:, 2][None, :, None] * states
    gated_out = ssm_out.reshape(sequence_length, SSM) * jax.nn.silu(gate_z)
    group_size = QUERY_HEAD_COUNT // KVHEADS
    query_head_rows = query_rows.reshape(sequence_length, KVHEADS, group_size, HEAD_WIDTH)
    key_head_rows = key_rows.reshape(sequence_length, KVHEADS, HEAD_WIDTH)
    value_head_rows = value_rows.reshape(sequence_length, KVHEADS, HEAD_WIDTH)
    attention_scores = jnp.einsum('oxlc,mxc->xlom', query_head_rows, key_head_rows, precision=exact_result) / math.sqrt(HEAD_WIDTH)
    attention_scores = jnp.where(allowed, attention_scores, -1e+30)
    largest = lax.optimization_barrier(jnp.max(attention_scores, -1, keepdims=True))
    exponent = jnp.exp(attention_scores - largest)
    attention_probabilities = exponent / lax.optimization_barrier(jnp.sum(exponent, -1, keepdims=True))
    attended_values = jnp.einsum('cynk,kcj->ncyj', attention_probabilities, value_head_rows, precision=exact_result).reshape(sequence_length, QUERY_HEAD_COUNT * HEAD_WIDTH)
    return jnp.concatenate([gated_out, attended_values], 1)

def matmul_rows(left, right):
    return jnp.einsum('btd,df->btf', left, right, precision=lax.Precision.HIGHEST)

def layer_apply(inputs, segment_rows, gain_pair, w_in, conv_table, head_table, w_out, w_gate_up, w_down):
    normed = low(rms_norm(inputs, gain_pair[:, 0]))
    projected = low_back(matmul_rows(normed, w_in))
    core_block = jax.checkpoint(lambda block_rows, mark_rows: mixers(block_rows, conv_table, head_table, mark_rows))
    joined = lax.map(lambda block_pair: core_block(block_pair[0], block_pair[1]), (projected, segment_rows))
    branch = low_back(matmul_rows(low(joined), w_out))
    hidden = inputs + branch
    normed_two = low(rms_norm(hidden, gain_pair[:, 1]))
    gate_up = low_back(matmul_rows(normed_two, w_gate_up))
    activated = low(jax.nn.silu(gate_up[..., :FF]) * gate_up[..., FF:])
    return hidden + low_back(matmul_rows(activated, w_down))

def reference(tokens, segment_ids, cotangent, norm_gains, w_in, conv_params, head_params, w_out, w_gate_up, w_down):
    blocks = MB * GROUPS
    segment_rows = segment_ids.reshape(blocks, TOK_DEV)
    inputs = tokens.astype(jnp.float32).reshape(blocks, TOK_DEV, D)
    boundary = jnp.zeros_like(inputs)

    def forward(inputs, boundary, gains_f, w_in_f, conv_f, heads_f, w_out_f, w_gate_up_f, w_down_f):
        first_out = layer_apply(inputs, segment_rows, gains_f[0], w_in_f[0], conv_f[0], heads_f[0], w_out_f[0], w_gate_up_f[0], w_down_f[0])
        second_in = low(low_back(first_out)) + boundary
        second = layer_apply(second_in, segment_rows, gains_f[1], w_in_f[1], conv_f[1], heads_f[1], w_out_f[1], w_gate_up_f[1], w_down_f[1])
        return (first_out, second)
    outputs, pullback = jax.vjp(forward, inputs, boundary, norm_gains.astype(jnp.float32), w_in.astype(jnp.float32), conv_params.astype(jnp.float32), head_params.astype(jnp.float32), w_out.astype(jnp.float32), w_gate_up.astype(jnp.float32), w_down.astype(jnp.float32))
    gradients = pullback((jnp.zeros_like(outputs[0]), cotangent.astype(jnp.float32).reshape(blocks, TOK_DEV, D)))
    layer_out = jnp.stack([outputs[0], outputs[1]]).reshape(2, MB, TOKENS, D).astype(jnp.bfloat16)
    input_grads = jnp.stack([gradients[0], gradients[1]]).reshape(2, MB, TOKENS, D)
    return (layer_out, input_grads, gradients[2], gradients[3], gradients[4], gradients[5], gradients[6], gradients[7], gradients[8])
```

```python
import functools
import math

import jax
import jax.numpy as jnp
from jax import lax
from jax.experimental import pallas as pl
from jax.experimental.pallas import tpu as pltpu
from jax.sharding import PartitionSpec as P

FF = 2048
MHEADS = 24
HEAD_WIDTH = 64
STATE = 128
QUERY_HEAD_COUNT = 8
KVHEADS = 2
CONV = 4
SSM = 1536
CH = 1792
UW = 2048
PIN = 4120
PAD = 4224
T = 112
OFF_Q = SSM + CH
OFF_K = OFF_Q + QUERY_HEAD_COUNT * HEAD_WIDTH
OFF_V = OFF_K + KVHEADS * HEAD_WIDTH
OFF_R = OFF_V + KVHEADS * HEAD_WIDTH
F32 = jnp.float32
BF16 = jnp.bfloat16


def dot_nn(left, right):
    return jnp.dot(left.astype(BF16), right.astype(BF16), preferred_element_type=F32)


def dot_nt(left, right):
    return lax.dot_general(
        left.astype(BF16), right.astype(BF16), (((1,), (1,)), ((), ())), preferred_element_type=F32
    )


def dot_tn(left, right):
    return lax.dot_general(
        left.astype(BF16), right.astype(BF16), (((0,), (0,)), ((), ())), preferred_element_type=F32
    )


def exact_dot(left, right):
    return jnp.dot(left, right, precision=lax.Precision.HIGHEST, preferred_element_type=F32)


def iota(shape, dim):
    return lax.broadcasted_iota(jnp.int32, shape, dim)


def block_masks(segc, segr):
    rows, cols = iota((T, T), 0), iota((T, T), 1)
    allowed = (segc[:, :T] == segr[0:1, :]) & (rows >= cols)
    places = iota((T, 128), 0)
    links = [
        jnp.where((pltpu.roll(segc, j, 0) == segc) & (places >= j), 1.0, 0.0)
        for j in range(1, CONV)
    ]
    return allowed, links


def convolve(p_ref, conv_ref, links, mixed_ref, act_ref):
    for at in range(0, CH, 128):
        sl = slice(at, at + 128)
        c = p_ref[0, :, SSM + at : SSM + at + 128]
        mixed = conv_ref[4:5, sl] + c * conv_ref[0:1, sl]
        for j in range(1, CONV):
            mixed = mixed + links[j - 1] * pltpu.roll(c, j, 0) * conv_ref[j : j + 1, sl]
        if mixed_ref is not None:
            mixed_ref[:, sl] = mixed
        act_ref[:, sl] = mixed * jax.nn.sigmoid(mixed)


def softplus(v):
    return jnp.maximum(v, 0.0) + jnp.log1p(jnp.exp(-jnp.abs(v)))


def steps_and_sums(p_ref, head_ref):
    raw = p_ref[0, :, OFF_R:PAD] + head_ref[0:1, :]
    live = iota((T, 128), 1) < MHEADS
    raw = jnp.where(live, raw, 0.0)
    dt = softplus(raw)
    decay = -dt * jnp.exp(head_ref[1:2, :])
    lower = jnp.where(iota((T, T), 0) >= iota((T, T), 1), 1.0, 0.0)
    return raw, dt, decay, exact_dot(lower, decay)


def attention_probs(q_tile, keep, k_dup, allowed):
    scores = dot_nt(jnp.where(keep, q_tile, 0.0), k_dup) * (1.0 / math.sqrt(HEAD_WIDTH))
    scores = jnp.where(allowed, scores, -1e30)
    e = jnp.exp(scores - jnp.max(scores, -1, keepdims=True))
    return e / jnp.sum(e, -1, keepdims=True)


def doubled(tile, left):
    turned = pltpu.roll(tile, HEAD_WIDTH, 1)
    return jnp.where(left, tile, turned), jnp.where(left, turned, tile)


def mix_forward_kernel(p_ref, segc_ref, segr_ref, conv_ref, head_ref, skip_ref, u_ref, act_ref):
    allowed, links = block_masks(segc_ref[0], segr_ref[0])
    convolve(p_ref, conv_ref, links, None, act_ref)
    _, dt, _, cum = steps_and_sums(p_ref, head_ref)
    dt_t, cum_t = dt.T, cum.T
    left = iota((T, 128), 1) < HEAD_WIDTH
    cb = dot_nt(act_ref[:, SSM + STATE :], act_ref[:, SSM : SSM + STATE])
    for pair in range(MHEADS // 2):
        sl = slice(128 * pair, 128 * pair + 128)
        xs = act_ref[:, sl]
        ys = []
        for h in (2 * pair, 2 * pair + 1):
            decayed = jnp.exp(jnp.where(allowed, cum[:, h : h + 1] - cum_t[h : h + 1, :], -1e30))
            ys.append(dot_nn(decayed * cb * dt_t[h : h + 1, :], xs))
        y = jnp.where(left, ys[0], ys[1]) + skip_ref[0:1, sl] * xs
        z = p_ref[0, :, sl]
        u_ref[0, :, sl] = (y * (z * jax.nn.sigmoid(z))).astype(BF16)
    k_dups = doubled(p_ref[0, :, OFF_K:OFF_V], left)
    v_dups = doubled(p_ref[0, :, OFF_V:OFF_R], left)
    for pair in range(QUERY_HEAD_COUNT // 2):
        kv = pair // 2
        q_tile = p_ref[0, :, OFF_Q + 128 * pair : OFF_Q + 128 * pair + 128]
        probs = [attention_probs(q_tile, keep, k_dups[kv], allowed) for keep in (left, ~left)]
        out = [dot_nn(pr, v_dups[kv]) for pr in probs]
        u_ref[0, :, SSM + 128 * pair : SSM + 128 * pair + 128] = jnp.where(
            left, out[0], out[1]
        ).astype(BF16)


def mix_backward_kernel(
    p_ref, gu_ref, segc_ref, segr_ref, conv_ref, head_ref, skip_ref,
    gp_ref, gconv_ref, ghead_ref, gskip_ref,
    mixed_ref, act_ref, gact_ref, colq_ref,
):
    allowed, links = block_masks(segc_ref[0], segr_ref[0])
    convolve(p_ref, conv_ref, links, mixed_ref, act_ref)
    raw, dt, decay, cum = steps_and_sums(p_ref, head_ref)
    dt_t, cum_t = dt.T, cum.T
    lanes = iota((T, 128), 1)
    left = lanes < HEAD_WIDTH
    b_rows = act_ref[:, SSM : SSM + STATE]
    c_rows = act_ref[:, SSM + STATE :]
    cb = dot_nt(c_rows, b_rows)
    gcb = jnp.zeros((T, T), F32)
    row_form = jnp.zeros((T, 128), F32)
    colq_ref[...] = jnp.zeros_like(colq_ref)
    for pair in range(MHEADS // 2):
        sl = slice(128 * pair, 128 * pair + 128)
        xs = act_ref[:, sl]
        xs16 = xs.astype(BF16)
        z = p_ref[0, :, sl]
        gm = gu_ref[0, :, sl]
        sg = jax.nn.sigmoid(z)
        gy = gm * (z * sg)
        gy16 = gy.astype(BF16)
        ys, gxs = [], []
        for h, keep in ((2 * pair, left), (2 * pair + 1, ~left)):
            decayed = jnp.exp(jnp.where(allowed, cum[:, h : h + 1] - cum_t[h : h + 1, :], -1e30))
            dt_row = dt_t[h : h + 1, :]
            base = decayed * cb
            k16 = (base * dt_row).astype(BF16)
            ys.append(dot_nn(k16, xs16))
            gxs.append(dot_tn(k16, gy16))
            gk = dot_nt(jnp.where(keep, gy, 0.0), xs16)
            gcb = gcb + gk * (decayed * dt_row)
            q = gk * base
            colq_ref[h : h + 1, :] = jnp.sum(q, 0, keepdims=True)
            row_form = jnp.where(lanes == h, jnp.sum(q * dt_row, 1, keepdims=True), row_form)
        skip = skip_ref[0:1, sl]
        y = jnp.where(left, ys[0], ys[1]) + skip * xs
        gp_ref[0, :, sl] = (gm * y * (sg * (1.0 + z * (1.0 - sg)))).astype(BF16)
        gact_ref[:, sl] = jnp.where(left, gxs[0], gxs[1]) + skip * gy
        gskip_ref[0, 0:1, sl] = jnp.sum(gy * xs, 0, keepdims=True)
    gact_ref[:, SSM : SSM + STATE] = dot_tn(gcb, c_rows)
    gact_ref[:, SSM + STATE :] = dot_nn(gcb, b_rows)
    col_form = colq_ref[...].T
    gcum = row_form - col_form * dt
    upper = jnp.where(iota((T, T), 0) <= iota((T, T), 1), 1.0, 0.0)
    gdecay = exact_dot(upper, gcum)
    gdt = col_form - gdecay * jnp.exp(head_ref[1:2, :])
    graw = jnp.where(lanes < MHEADS, gdt * jax.nn.sigmoid(raw), 0.0)
    gp_ref[0, :, OFF_R:PAD] = graw.astype(BF16)
    ghead_ref[0, 0:1, :] = jnp.sum(graw, 0, keepdims=True)
    ghead_ref[0, 1:2, :] = jnp.sum(gdecay * decay, 0, keepdims=True)
    for at in range(0, CH, 128):
        sl = slice(at, at + 128)
        mixed = mixed_ref[:, sl]
        sg = jax.nn.sigmoid(mixed)
        gmix = gact_ref[:, sl] * (sg * (1.0 + mixed * (1.0 - sg)))
        c = p_ref[0, :, SSM + at : SSM + at + 128]
        gc = gmix * conv_ref[0:1, sl]
        gconv_ref[0, 0:1, sl] = jnp.sum(gmix * c, 0, keepdims=True)
        for j in range(1, CONV):
            linked = gmix * links[j - 1]
            gc = gc + pltpu.roll(linked, T - j, 0) * conv_ref[j : j + 1, sl]
            gconv_ref[0, j : j + 1, sl] = jnp.sum(linked * pltpu.roll(c, j, 0), 0, keepdims=True)
        gconv_ref[0, 4:5, sl] = jnp.sum(gmix, 0, keepdims=True)
        gp_ref[0, :, SSM + at : SSM + at + 128] = gc.astype(BF16)
    k_dups = doubled(p_ref[0, :, OFF_K:OFF_V], left)
    v_dups = doubled(p_ref[0, :, OFF_V:OFF_R], left)
    gks, gvs = [], []
    for kv in range(KVHEADS):
        gk_sum = jnp.zeros((T, 128), F32)
        gv_sum = jnp.zeros((T, 128), F32)
        for pair in (2 * kv, 2 * kv + 1):
            sl = slice(OFF_Q + 128 * pair, OFF_Q + 128 * pair + 128)
            q_tile = p_ref[0, :, sl]
            go = gu_ref[0, :, SSM + 128 * pair : SSM + 128 * pair + 128]
            gq, gk, gv = [], [], []
            for keep in (left, ~left):
                probs = attention_probs(q_tile, keep, k_dups[kv], allowed)
                gpr = dot_nt(jnp.where(keep, go, 0.0), v_dups[kv])
                gs = probs * (gpr - jnp.sum(gpr * probs, -1, keepdims=True))
                gs = (gs * (1.0 / math.sqrt(HEAD_WIDTH))).astype(BF16)
                gq.append(dot_nn(gs, k_dups[kv]))
                gk.append(dot_tn(gs, q_tile))
                gv.append(dot_tn(probs, go))
            gp_ref[0, :, sl] = jnp.where(left, gq[0], gq[1]).astype(BF16)
            gk_sum = gk_sum + jnp.where(left, gk[0], gk[1])
            gv_sum = gv_sum + jnp.where(left, gv[0], gv[1])
        gks.append(gk_sum + pltpu.roll(gk_sum, HEAD_WIDTH, 1))
        gvs.append(gv_sum + pltpu.roll(gv_sum, HEAD_WIDTH, 1))
    gp_ref[0, :, OFF_K:OFF_V] = jnp.where(left, gks[0], gks[1]).astype(BF16)
    gp_ref[0, :, OFF_V:OFF_R] = jnp.where(left, gvs[0], gvs[1]).astype(BF16)


def whole(shape):
    return pl.BlockSpec(shape, lambda m: (0,) * len(shape))


def per_block(shape):
    return pl.BlockSpec((1, *shape), lambda m: (m,) + (0,) * len(shape))


def small_specs():
    return [
        per_block((T, 128)), per_block((8, T)), whole((8, CH)), whole((8, 128)), whole((8, SSM)),
    ]


def mix_forward(projected, tables):
    blocks = projected.shape[0]
    return pl.pallas_call(
        mix_forward_kernel,
        grid=(blocks,),
        in_specs=[per_block((T, PAD)), *small_specs()],
        out_specs=per_block((T, UW)),
        out_shape=jax.ShapeDtypeStruct((blocks, T, UW), BF16),
        scratch_shapes=[pltpu.VMEM((T, CH), F32)],
        compiler_params=pltpu.CompilerParams(vmem_limit_bytes=32 * 1024 * 1024),
        name="mix_forward",
    )(projected, *tables)


def mix_backward(projected, grad_joined, tables):
    blocks = projected.shape[0]
    return pl.pallas_call(
        mix_backward_kernel,
        grid=(blocks,),
        in_specs=[per_block((T, PAD)), per_block((T, UW)), *small_specs()],
        out_specs=[per_block((T, PAD)), per_block((8, CH)), per_block((8, 128)), per_block((8, SSM))],
        out_shape=[
            jax.ShapeDtypeStruct((blocks, T, PAD), BF16),
            jax.ShapeDtypeStruct((blocks, 8, CH), F32),
            jax.ShapeDtypeStruct((blocks, 8, 128), F32),
            jax.ShapeDtypeStruct((blocks, 8, SSM), F32),
        ],
        scratch_shapes=[
            pltpu.VMEM((T, CH), F32),
            pltpu.VMEM((T, CH), F32),
            pltpu.VMEM((T, CH), F32),
            pltpu.VMEM((128, T), F32),
        ],
        compiler_params=pltpu.CompilerParams(vmem_limit_bytes=40 * 1024 * 1024),
        name="mix_backward",
    )(projected, grad_joined, *tables)


def mixer_tables(segments, conv_table, head_table):
    blocks = segments.shape[0]
    marks = segments.astype(F32)
    segc = jnp.broadcast_to(marks[:, :, None], (blocks, T, 128))
    segr = jnp.broadcast_to(marks[:, None, :], (blocks, 8, T))
    conv_rows = jnp.pad(conv_table.T, ((0, 3), (0, 0)))
    head_rows = jnp.pad(head_table.T, ((0, 5), (0, 128 - MHEADS)))
    skip_rows = jnp.broadcast_to(jnp.repeat(head_table[:, 2], HEAD_WIDTH)[None], (8, SSM))
    return segc, segr, conv_rows, head_rows, skip_rows


MESH = pl.DeviceIdType.MESH
HOPS = ("xa", "xb", "za", "zb", "y")
PARTS = (
    (3, 0, 1024, ("y", "xa", "za", "xb", "zb")),
    (2, 0, 2048, ("za", "zb", "xa", "xb", "y")),
    (2, 2048, 2048, ("zb", "za", "xb", "xa", "y")),
    (1, 0, 1024, ("xa", "xb", "za", "zb", "y")),
    (0, 0, 2176, ("xb", "xa", "zb", "za", "y")),
    (0, 2176, 2048, ("y", "zb", "xb", "za", "xa")),
)
SHARD_ROWS = (64, 128, 64, 128)
SHARD_COLS = (PAD, 1024, 2 * FF, 1024)


def pair_a(i):
    return i + 1 - 2 * (i % 2)


def pair_b(i):
    return (i + 2 * (i % 2) + 3) % 4


def place():
    shard = lax.axis_index("shard")
    return lax.axis_index("section"), shard // 8, (shard // 2) % 4, shard % 2, lax.axis_index("rep")


def neighbours(section, y, z, core, x):
    def at(y, z, core, x):
        return (section, y * 8 + z * 2 + core, x)

    return {
        "core": at(y, z, 1 - core, x),
        "xa": at(y, z, core, pair_a(x)),
        "xb": at(y, z, core, pair_b(x)),
        "za": at(y, pair_a(z), core, x),
        "zb": at(y, pair_b(z), core, x),
        "y": at(1 - y, z, core, x),
        "xo": at(y, z, core, (x + 2) % 4),
    }


def meet(devices):
    barrier = pltpu.get_barrier_semaphore()
    for device in devices:
        pl.semaphore_signal(barrier, inc=1, device_id=device, device_id_type=MESH)
    pl.semaphore_wait(barrier, len(devices))


def halve(kept, hop, me):
    near, other = (pair_a, pair_b) if hop == "a" else (pair_b, pair_a)
    if len(kept) == 4:
        return [near(me), other(near(me))], [me, other(me)]
    return [near(me)], [me]


def schedule(order, me_y, me_z, me_x):
    every = [0, 1, 2, 3]
    ys, zs, xs = None, every, every
    stages = []

    def pieces(ys, zs, xs):
        zs = [None] if len(zs) == 4 else zs
        xs = [None] if len(xs) == 4 else xs
        return [(ys, z, x) for z in zs for x in xs]

    for hop in order:
        if hop == "y":
            stages.append((pieces(1 - me_y, zs, xs), pieces(me_y, zs, xs)))
            ys = me_y
        elif hop[0] == "z":
            sent, zs_kept = halve(zs, hop[1], me_z)
            stages.append((pieces(ys, sent, xs), pieces(ys, zs_kept, xs)))
            zs = zs_kept
        else:
            sent, xs_kept = halve(xs, hop[1], me_x)
            stages.append((pieces(ys, zs, sent), pieces(ys, zs, xs_kept)))
            xs = xs_kept
    return stages


def window(piece, quarter, column, columns):
    y, z, x = piece
    return (
        slice(0, 2) if y is None else pl.ds(y, 1),
        slice(0, 4) if z is None else pl.ds(z, 1),
        slice(0, 4 * quarter) if x is None else pl.ds(pl.multiple_of(x * quarter, quarter), quarter),
        pl.ds(column, columns),
    )


def piece_dims(piece, quarter):
    y, z, x = piece
    return (2 if y is None else 1, 4 if z is None else 1, 4 * quarter if x is None else quarter)


def stage_shapes():
    shapes = []
    for array, column, columns, order in PARTS:
        for sent, _ in schedule(order, 0, 0, 0):
            dims = piece_dims(sent[0], SHARD_ROWS[array] // 4)
            shapes.append((len(sent), *dims, columns))
    return shapes


def add_into(acc, window_at, arrived):
    ny, nz, rows, columns = arrived.shape
    ys, zs, rs, cs = window_at
    y0 = 0 if isinstance(ys, slice) else ys.start
    z0 = 0 if isinstance(zs, slice) else zs.start
    r0 = 0 if isinstance(rs, slice) else rs.start
    tiles = rows // 16

    def step(i, carry):
        y, rest = i // (nz * tiles), i % (nz * tiles)
        z, t = rest // tiles, rest % tiles
        row = pl.ds(pl.multiple_of(t * 16, 16), 16)
        at = (y0 + y, z0 + z, pl.ds(pl.multiple_of(r0 + t * 16, 16), 16), cs)
        acc[at] = acc[at] + arrived[y, z, row, :]
        return carry

    lax.fori_loop(0, ny * nz * tiles, step, 0)


def scatter_kernel(*refs):
    grads, outs = refs[:4], refs[4:8]
    accs, wholes, cores = refs[8:12], refs[12:16], refs[16:22]
    n_stage = len(PARTS) * len(HOPS)
    arrivals = refs[22 : 22 + n_stage]
    local_sem, core_send, core_recv, send_sem, recv_sem, last_send, last_recv = refs[22 + n_stage :]
    section, y, z, core, x = place()
    near = neighbours(section, y, z, core, x)
    meet([near[name] for name in ("core", *HOPS, "xo")])

    loads, swaps = [], []
    for p, (array, column, columns, _) in enumerate(PARTS):
        cols = pl.ds(column, columns)
        swap = pltpu.make_async_remote_copy(
            src_ref=grads[array].at[:, :, 1 - core, :, cols],
            dst_ref=cores[p],
            send_sem=core_send.at[p],
            recv_sem=core_recv.at[p],
            device_id=near["core"],
            device_id_type=MESH,
        )
        swap.start()
        load = pltpu.make_async_copy(
            grads[array].at[:, :, core, :, cols], accs[array].at[:, :, :, cols], local_sem.at[p]
        )
        load.start()
        swaps.append(swap)
        loads.append(load)

    plans = [schedule(order, y, z, x) for _, _, _, order in PARTS]
    flying = {}
    sems = 0
    for stage in range(len(HOPS) + 1):
        for p, (array, column, columns, order) in enumerate(PARTS):
            quarter = SHARD_ROWS[array] // 4
            if stage == 0:
                loads[p].wait()
                swaps[p].wait_recv()
                add_into(accs[array], window((None, None, None), quarter, column, columns), cores[p])
            else:
                kept = plans[p][stage - 1][1]
                for k, (copy, piece) in enumerate(zip(flying[p, stage - 1], kept)):
                    copy.wait_recv()
                    add_into(
                        accs[array],
                        window(piece, quarter, column, columns),
                        arrivals[p * len(HOPS) + stage - 1].at[k],
                    )
            if stage < len(HOPS):
                copies = []
                for k, piece in enumerate(plans[p][stage][0]):
                    copy = pltpu.make_async_remote_copy(
                        src_ref=accs[array].at[window(piece, quarter, column, columns)],
                        dst_ref=arrivals[p * len(HOPS) + stage].at[k],
                        send_sem=send_sem.at[sems],
                        recv_sem=recv_sem.at[sems],
                        device_id=near[order[stage]],
                        device_id_type=MESH,
                    )
                    copy.start()
                    copies.append(copy)
                    sems += 1
                flying[p, stage] = copies

    last = []
    for array in range(4):
        quarter = SHARD_ROWS[array] // 4
        mine = pl.ds(pl.multiple_of(x * quarter, quarter), quarter)
        for k, name in enumerate(("xo", "xa", "xb")):
            copy = pltpu.make_async_remote_copy(
                src_ref=accs[array].at[y, z, mine],
                dst_ref=wholes[array].at[mine],
                send_sem=last_send.at[array, k],
                recv_sem=last_recv.at[array, k],
                device_id=near[name],
                device_id_type=MESH,
            )
            copy.start()
            last.append(copy)
        outs[array][mine, :] = accs[array][y, z, mine, :].astype(F32)
    for array in range(4):
        quarter = SHARD_ROWS[array] // 4
        for k, owner in enumerate(((x + 2) % 4, pair_a(x), pair_b(x))):
            last[array * 3 + k].wait_recv()
            theirs = pl.ds(pl.multiple_of(owner * quarter, quarter), quarter)
            outs[array][theirs, :] = wholes[array][theirs, :].astype(F32)
    for copy in last + swaps + [c for copies in flying.values() for c in copies]:
        copy.wait_send()


def scatter_sums(grads):
    n_copies = sum(shape[0] for shape in stage_shapes())
    return pl.pallas_call(
        scatter_kernel,
        in_specs=[pl.BlockSpec(memory_space=pl.ANY)] * 4,
        out_specs=[pl.BlockSpec(memory_space=pltpu.VMEM)] * 4,
        out_shape=[jax.ShapeDtypeStruct(s, F32) for s in zip(SHARD_ROWS, SHARD_COLS)],
        scratch_shapes=[
            *[pltpu.VMEM((2, 4, r, c), BF16) for r, c in zip(SHARD_ROWS, SHARD_COLS)],
            *[pltpu.VMEM((r, c), BF16) for r, c in zip(SHARD_ROWS, SHARD_COLS)],
            *[pltpu.VMEM((2, 4, SHARD_ROWS[a], cols), BF16) for a, _, cols, _ in PARTS],
            *[pltpu.VMEM(shape, BF16) for shape in stage_shapes()],
            pltpu.SemaphoreType.DMA((len(PARTS),)),
            pltpu.SemaphoreType.DMA((len(PARTS),)),
            pltpu.SemaphoreType.DMA((len(PARTS),)),
            pltpu.SemaphoreType.DMA((n_copies,)),
            pltpu.SemaphoreType.DMA((n_copies,)),
            pltpu.SemaphoreType.DMA((4, 3)),
            pltpu.SemaphoreType.DMA((4, 3)),
        ],
        compiler_params=pltpu.CompilerParams(
            collective_id=1, has_side_effects=True, vmem_limit_bytes=58 * 1024 * 1024
        ),
        name="scatter_sums",
    )(*grads)


def rms_norm(values, gain):
    return values * lax.rsqrt(jnp.mean(values * values, -1, keepdims=True) + 1e-05) * gain


def rms_back(values, gain, grad):
    scale = lax.rsqrt(jnp.mean(values * values, -1, keepdims=True) + 1e-05)
    unit = values * scale
    scaled = grad * gain
    grad_values = scale * (scaled - unit * jnp.mean(scaled * unit, -1, keepdims=True))
    return grad_values, jnp.sum(grad * unit, 0)


def forward_product(left, weight):
    return jnp.dot(left, weight, preferred_element_type=F32)


def back_product(grad_rows, weight):
    return lax.dot_general(
        grad_rows, weight, (((1,), (1,)), ((), ())), preferred_element_type=F32
    )


def outer_sum(left, right):
    return lax.dot_general(
        left, right, (((0,), (0,)), ((), ())), preferred_element_type=F32
    ).astype(BF16)


def layer_forward(inputs, weights, tables):
    gains, w_in, w_out, w_gate_up, w_down = weights
    blocks = inputs.shape[0] // T
    normed = rms_norm(inputs, gains[0]).astype(BF16)
    projected = forward_product(normed, w_in)
    joined = mix_forward(projected.reshape(blocks, T, PAD), tables).reshape(blocks * T, UW)
    hidden = inputs + forward_product(joined, w_out)
    normed_two = rms_norm(hidden, gains[1]).astype(BF16)
    gate_up = forward_product(normed_two, w_gate_up)
    activated = (jax.nn.silu(gate_up[:, :FF]) * gate_up[:, FF:]).astype(BF16)
    result = hidden + forward_product(activated, w_down)
    return result, (inputs, normed, projected, joined, hidden, normed_two, gate_up, activated)


def layer_backward(grad_out, saved, weights, tables):
    gains, w_in, w_out, w_gate_up, w_down = weights
    inputs, normed, projected, joined, hidden, normed_two, gate_up, activated = saved
    blocks = inputs.shape[0] // T
    grad_ffn = grad_out.astype(BF16)
    grad_act = back_product(grad_ffn, w_down)
    gate, up = gate_up[:, :FF], gate_up[:, FF:]
    sig = jax.nn.sigmoid(gate)
    grad_gate = (grad_act * up * (sig * (1.0 + gate * (1.0 - sig)))).astype(BF16)
    grad_up = (grad_act * (gate * sig)).astype(BF16)
    grad_gate_up = jnp.concatenate([grad_gate, grad_up], 1)
    grad_hidden, grad_gain_two = rms_back(hidden, gains[1], back_product(grad_gate_up, w_gate_up))
    grad_hidden = grad_out + grad_hidden
    grad_branch = grad_hidden.astype(BF16)
    grad_joined = back_product(grad_branch, w_out)
    grad_proj, grad_conv, grad_head, grad_skip = mix_backward(
        projected.reshape(blocks, T, PAD), grad_joined.reshape(blocks, T, UW), tables
    )
    grad_proj = grad_proj.reshape(blocks * T, PAD)
    grad_input, grad_gain_one = rms_back(inputs, gains[0], back_product(grad_proj, w_in))
    grad_input = grad_hidden + grad_input
    pairs = (
        (normed, grad_proj),
        (joined, grad_branch),
        (normed_two, grad_gate_up),
        (activated, grad_ffn),
    )
    return grad_input, pairs, (grad_gain_one, grad_gain_two, grad_conv, grad_head, grad_skip)


def across(array, by):
    return lax.ppermute(array, "section", [(0, 1)] if by > 0 else [(1, 0)])


def gather_weights(norm_gains, w_in, w_out, w_gate_up, w_down):
    filler = jnp.zeros((w_in.shape[0], PAD - PIN - 2), BF16)
    joined = jnp.concatenate([w_in, norm_gains, filler], 1)
    w_in_all, w_out_all, w_gate_up_all, w_down_all = [
        lax.all_gather(part, "shard", axis=0, tiled=True)
        for part in (joined, w_out, w_gate_up, w_down)
    ]
    gains = w_in_all[:, PIN : PIN + 2].astype(F32).T
    return gains, w_in_all, w_out_all, w_gate_up_all, w_down_all


def body(
    tokens,
    segment_ids,
    cotangent,
    norm_gains,
    w_in,
    conv_params,
    head_params,
    w_out,
    w_gate_up,
    w_down,
):
    section = lax.axis_index("section")
    blocks, _, width = tokens.shape
    rows = blocks * T
    weights = gather_weights(norm_gains[0], w_in[0], w_out[0], w_gate_up[0], w_down[0])
    conv_all = lax.all_gather(conv_params[0], "shard", axis=0, tiled=True)
    tables = mixer_tables(segment_ids[:, 0], conv_all.astype(F32), head_params[0].astype(F32))

    own = tokens.reshape(rows, width)
    first, _ = layer_forward(own.astype(F32), weights, tables)
    received = across(first.astype(BF16), 1)
    inputs = jnp.where(section == 0, own, received).astype(F32)
    result, saved = layer_forward(inputs, weights, tables)

    top = cotangent.reshape(rows, width)
    first_grad, _, _ = layer_backward(top.astype(F32), saved, weights, tables)
    coming = across(first_grad.astype(BF16), -1)
    grad_out = jnp.where(section == 1, top, coming).astype(F32)
    grad_input, pairs, smalls = layer_backward(grad_out, saved, weights, tables)

    grad_gain_one, grad_gain_two, grad_conv, grad_head, grad_skip = smalls
    sums = [outer_sum(left, right) for left, right in pairs]
    shards = lax.axis_size("shard")
    gains = jnp.stack([grad_gain_one, grad_gain_two], 1)
    conv = jnp.sum(grad_conv, 0)[: CONV + 1].T.reshape(shards, -1)
    conv = jnp.pad(conv, ((0, 0), (0, 640 - conv.shape[1]))).reshape(shards * 64, 10)
    head = jnp.sum(grad_head, 0)[:2, :MHEADS]
    skip = jnp.sum(jnp.sum(grad_skip, 0)[0].reshape(MHEADS, HEAD_WIDTH), 1)
    head = jnp.concatenate([head, skip[None]], 0).T.reshape(-1)
    head = jnp.pad(head, (0, 128 - head.shape[0])).reshape(64, 2)
    head = jnp.broadcast_to(head[None], (shards, 64, 2)).reshape(shards * 64, 2)
    extra = jnp.concatenate([gains, conv, head], 1).astype(BF16)
    sums[0] = lax.dynamic_update_slice(sums[0], extra, (0, PIN))
    out_in, out_out, out_gu, out_dn = scatter_sums(
        [g.reshape(2, 4, 2, g.shape[0] // 16, g.shape[1]) for g in sums]
    )
    out_gains = out_in[:, PIN : PIN + 2]
    out_conv = out_in[:, PIN + 2 : PIN + 12].reshape(-1)[: 112 * (CONV + 1)]
    out_head = out_in[:, PIN + 12 : PIN + 14].reshape(-1)[: MHEADS * 3]
    return (
        result.astype(BF16).reshape(1, blocks, T, width),
        grad_input.reshape(1, blocks, T, width),
        out_gains[None],
        out_in[None, :, :PIN],
        out_conv.reshape(1, 112, CONV + 1),
        out_head.reshape(1, MHEADS, 3),
        out_out[None],
        out_gu[None],
        out_dn[None],
    )


def solution(mesh):
    in_specs = (
        P(None, ("shard", "rep"), None),
        P(None, ("shard", "rep"), None),
        P(None, ("shard", "rep"), None),
        P("section", "shard", None),
        P("section", "shard", None),
        P("section", "shard", None),
        P("section", None, None),
        P("section", "shard", None),
        P("section", "shard", None),
        P("section", "shard", None),
    )
    out_specs = (
        P("section", None, ("shard", "rep"), None),
        P("section", None, ("shard", "rep"), None),
        P("section", "shard", None),
        P("section", "shard", None),
        P("section", "shard", None),
        P("section", None, None),
        P("section", "shard", None),
        P("section", "shard", None),
        P("section", "shard", None),
    )
    return jax.shard_map(body, mesh=mesh, in_specs=in_specs, out_specs=out_specs, check_vma=False)
```

```python
import functools
import math

import jax
import jax.numpy as jnp
from jax import lax
from jax.experimental import pallas as pl
from jax.experimental.pallas import tpu as pltpu
from jax.sharding import PartitionSpec as P

FF = 2048
MHEADS = 24
HEAD_WIDTH = 64
STATE = 128
QUERY_HEAD_COUNT = 8
KVHEADS = 2
CONV = 4
SSM = 1536
CH = 1792
UW = 2048
PIN = 4120
PAD = 4224
T = 112
OFF_Q = SSM + CH
OFF_K = OFF_Q + QUERY_HEAD_COUNT * HEAD_WIDTH
OFF_V = OFF_K + KVHEADS * HEAD_WIDTH
OFF_R = OFF_V + KVHEADS * HEAD_WIDTH
F32 = jnp.float32
BF16 = jnp.bfloat16


def dot_nn(left, right):
    return jnp.dot(left.astype(BF16), right.astype(BF16), preferred_element_type=F32)


def dot_nt(left, right):
    return lax.dot_general(
        left.astype(BF16), right.astype(BF16), (((1,), (1,)), ((), ())), preferred_element_type=F32
    )


def dot_tn(left, right):
    return lax.dot_general(
        left.astype(BF16), right.astype(BF16), (((0,), (0,)), ((), ())), preferred_element_type=F32
    )


def exact_dot(left, right):
    return jnp.dot(left, right, precision=lax.Precision.HIGHEST, preferred_element_type=F32)


def iota(shape, dim):
    return lax.broadcasted_iota(jnp.int32, shape, dim)


def block_masks(segc, segr):
    rows, cols = iota((T, T), 0), iota((T, T), 1)
    allowed = (segc[:, :T] == segr[0:1, :]) & (rows >= cols)
    places = iota((T, 128), 0)
    links = [
        jnp.where((pltpu.roll(segc, j, 0) == segc) & (places >= j), 1.0, 0.0)
        for j in range(1, CONV)
    ]
    return allowed, links


def convolve(p_ref, conv_ref, links, mixed_ref, act_ref):
    for at in range(0, CH, 128):
        sl = slice(at, at + 128)
        c = p_ref[0, :, SSM + at : SSM + at + 128]
        mixed = conv_ref[4:5, sl] + c * conv_ref[0:1, sl]
        for j in range(1, CONV):
            mixed = mixed + links[j - 1] * pltpu.roll(c, j, 0) * conv_ref[j : j + 1, sl]
        if mixed_ref is not None:
            mixed_ref[:, sl] = mixed
        act_ref[:, sl] = mixed * jax.nn.sigmoid(mixed)


def softplus(v):
    return jnp.maximum(v, 0.0) + jnp.log1p(jnp.exp(-jnp.abs(v)))


def steps_and_sums(p_ref, head_ref):
    raw = p_ref[0, :, OFF_R:PAD] + head_ref[0:1, :]
    live = iota((T, 128), 1) < MHEADS
    raw = jnp.where(live, raw, 0.0)
    dt = softplus(raw)
    decay = -dt * jnp.exp(head_ref[1:2, :])
    lower = jnp.where(iota((T, T), 0) >= iota((T, T), 1), 1.0, 0.0)
    return raw, dt, decay, exact_dot(lower, decay)


def attention_probs(q_tile, keep, k_dup, allowed):
    scores = dot_nt(jnp.where(keep, q_tile, 0.0), k_dup) * (1.0 / math.sqrt(HEAD_WIDTH))
    scores = jnp.where(allowed, scores, -1e30)
    e = jnp.exp(scores - jnp.max(scores, -1, keepdims=True))
    return e / jnp.sum(e, -1, keepdims=True)


def doubled(tile, left):
    turned = pltpu.roll(tile, HEAD_WIDTH, 1)
    return jnp.where(left, tile, turned), jnp.where(left, turned, tile)


def mix_forward_kernel(p_ref, segc_ref, segr_ref, conv_ref, head_ref, skip_ref, u_ref, act_ref):
    allowed, links = block_masks(segc_ref[0], segr_ref[0])
    convolve(p_ref, conv_ref, links, None, act_ref)
    _, dt, _, cum = steps_and_sums(p_ref, head_ref)
    dt_t, cum_t = dt.T, cum.T
    left = iota((T, 128), 1) < HEAD_WIDTH
    cb = dot_nt(act_ref[:, SSM + STATE :], act_ref[:, SSM : SSM + STATE])
    for pair in range(MHEADS // 2):
        sl = slice(128 * pair, 128 * pair + 128)
        xs = act_ref[:, sl]
        ys = []
        for h in (2 * pair, 2 * pair + 1):
            decayed = jnp.exp(jnp.where(allowed, cum[:, h : h + 1] - cum_t[h : h + 1, :], -1e30))
            ys.append(dot_nn(decayed * cb * dt_t[h : h + 1, :], xs))
        y = jnp.where(left, ys[0], ys[1]) + skip_ref[0:1, sl] * xs
        z = p_ref[0, :, sl]
        u_ref[0, :, sl] = (y * (z * jax.nn.sigmoid(z))).astype(BF16)
    k_dups = doubled(p_ref[0, :, OFF_K:OFF_V], left)
    v_dups = doubled(p_ref[0, :, OFF_V:OFF_R], left)
    for pair in range(QUERY_HEAD_COUNT // 2):
        kv = pair // 2
        q_tile = p_ref[0, :, OFF_Q + 128 * pair : OFF_Q + 128 * pair + 128]
        probs = [attention_probs(q_tile, keep, k_dups[kv], allowed) for keep in (left, ~left)]
        out = [dot_nn(pr, v_dups[kv]) for pr in probs]
        u_ref[0, :, SSM + 128 * pair : SSM + 128 * pair + 128] = jnp.where(
            left, out[0], out[1]
        ).astype(BF16)


def mix_backward_kernel(
    p_ref, gu_ref, segc_ref, segr_ref, conv_ref, head_ref, skip_ref,
    gp_ref, gconv_ref, ghead_ref, gskip_ref,
    mixed_ref, act_ref, gact_ref, colq_ref,
):
    allowed, links = block_masks(segc_ref[0], segr_ref[0])
    convolve(p_ref, conv_ref, links, mixed_ref, act_ref)
    raw, dt, decay, cum = steps_and_sums(p_ref, head_ref)
    dt_t, cum_t = dt.T, cum.T
    lanes = iota((T, 128), 1)
    left = lanes < HEAD_WIDTH
    b_rows = act_ref[:, SSM : SSM + STATE]
    c_rows = act_ref[:, SSM + STATE :]
    cb = dot_nt(c_rows, b_rows)
    gcb = jnp.zeros((T, T), F32)
    row_form = jnp.zeros((T, 128), F32)
    colq_ref[...] = jnp.zeros_like(colq_ref)
    for pair in range(MHEADS // 2):
        sl = slice(128 * pair, 128 * pair + 128)
        xs = act_ref[:, sl]
        xs16 = xs.astype(BF16)
        z = p_ref[0, :, sl]
        gm = gu_ref[0, :, sl]
        sg = jax.nn.sigmoid(z)
        gy = gm * (z * sg)
        gy16 = gy.astype(BF16)
        ys, gxs = [], []
        for h, keep in ((2 * pair, left), (2 * pair + 1, ~left)):
            decayed = jnp.exp(jnp.where(allowed, cum[:, h : h + 1] - cum_t[h : h + 1, :], -1e30))
            dt_row = dt_t[h : h + 1, :]
            base = decayed * cb
            k16 = (base * dt_row).astype(BF16)
            ys.append(dot_nn(k16, xs16))
            gxs.append(dot_tn(k16, gy16))
            gk = dot_nt(jnp.where(keep, gy, 0.0), xs16)
            gcb = gcb + gk * (decayed * dt_row)
            q = gk * base
            colq_ref[h : h + 1, :] = jnp.sum(q, 0, keepdims=True)
            row_form = jnp.where(lanes == h, jnp.sum(q * dt_row, 1, keepdims=True), row_form)
        skip = skip_ref[0:1, sl]
        y = jnp.where(left, ys[0], ys[1]) + skip * xs
        gp_ref[0, :, sl] = (gm * y * (sg * (1.0 + z * (1.0 - sg)))).astype(BF16)
        gact_ref[:, sl] = jnp.where(left, gxs[0], gxs[1]) + skip * gy
        gskip_ref[0, 0:1, sl] = jnp.sum(gy * xs, 0, keepdims=True)
    gact_ref[:, SSM : SSM + STATE] = dot_tn(gcb, c_rows)
    gact_ref[:, SSM + STATE :] = dot_nn(gcb, b_rows)
    col_form = colq_ref[...].T
    gcum = row_form - col_form * dt
    upper = jnp.where(iota((T, T), 0) <= iota((T, T), 1), 1.0, 0.0)
    gdecay = exact_dot(upper, gcum)
    gdt = col_form - gdecay * jnp.exp(head_ref[1:2, :])
    graw = jnp.where(lanes < MHEADS, gdt * jax.nn.sigmoid(raw), 0.0)
    gp_ref[0, :, OFF_R:PAD] = graw.astype(BF16)
    ghead_ref[0, 0:1, :] = jnp.sum(graw, 0, keepdims=True)
    ghead_ref[0, 1:2, :] = jnp.sum(gdecay * decay, 0, keepdims=True)
    for at in range(0, CH, 128):
        sl = slice(at, at + 128)
        mixed = mixed_ref[:, sl]
        sg = jax.nn.sigmoid(mixed)
        gmix = gact_ref[:, sl] * (sg * (1.0 + mixed * (1.0 - sg)))
        c = p_ref[0, :, SSM + at : SSM + at + 128]
        gc = gmix * conv_ref[0:1, sl]
        gconv_ref[0, 0:1, sl] = jnp.sum(gmix * c, 0, keepdims=True)
        for j in range(1, CONV):
            linked = gmix * links[j - 1]
            gc = gc + pltpu.roll(linked, T - j, 0) * conv_ref[j : j + 1, sl]
            gconv_ref[0, j : j + 1, sl] = jnp.sum(linked * pltpu.roll(c, j, 0), 0, keepdims=True)
        gconv_ref[0, 4:5, sl] = jnp.sum(gmix, 0, keepdims=True)
        gp_ref[0, :, SSM + at : SSM + at + 128] = gc.astype(BF16)
    k_dups = doubled(p_ref[0, :, OFF_K:OFF_V], left)
    v_dups = doubled(p_ref[0, :, OFF_V:OFF_R], left)
    gks, gvs = [], []
    for kv in range(KVHEADS):
        gk_sum = jnp.zeros((T, 128), F32)
        gv_sum = jnp.zeros((T, 128), F32)
        for pair in (2 * kv, 2 * kv + 1):
            sl = slice(OFF_Q + 128 * pair, OFF_Q + 128 * pair + 128)
            q_tile = p_ref[0, :, sl]
            go = gu_ref[0, :, SSM + 128 * pair : SSM + 128 * pair + 128]
            gq, gk, gv = [], [], []
            for keep in (left, ~left):
                probs = attention_probs(q_tile, keep, k_dups[kv], allowed)
                gpr = dot_nt(jnp.where(keep, go, 0.0), v_dups[kv])
                gs = probs * (gpr - jnp.sum(gpr * probs, -1, keepdims=True))
                gs = (gs * (1.0 / math.sqrt(HEAD_WIDTH))).astype(BF16)
                gq.append(dot_nn(gs, k_dups[kv]))
                gk.append(dot_tn(gs, q_tile))
                gv.append(dot_tn(probs, go))
            gp_ref[0, :, sl] = jnp.where(left, gq[0], gq[1]).astype(BF16)
            gk_sum = gk_sum + jnp.where(left, gk[0], gk[1])
            gv_sum = gv_sum + jnp.where(left, gv[0], gv[1])
        gks.append(gk_sum + pltpu.roll(gk_sum, HEAD_WIDTH, 1))
        gvs.append(gv_sum + pltpu.roll(gv_sum, HEAD_WIDTH, 1))
    gp_ref[0, :, OFF_K:OFF_V] = jnp.where(left, gks[0], gks[1]).astype(BF16)
    gp_ref[0, :, OFF_V:OFF_R] = jnp.where(left, gvs[0], gvs[1]).astype(BF16)


def whole(shape):
    return pl.BlockSpec(shape, lambda m: (0,) * len(shape))


def per_block(shape):
    return pl.BlockSpec((1, *shape), lambda m: (m,) + (0,) * len(shape))


def small_specs():
    return [
        per_block((T, 128)), per_block((8, T)), whole((8, CH)), whole((8, 128)), whole((8, SSM)),
    ]


def mix_forward(projected, tables):
    blocks = projected.shape[0]
    return pl.pallas_call(
        mix_forward_kernel,
        grid=(blocks,),
        in_specs=[per_block((T, PAD)), *small_specs()],
        out_specs=per_block((T, UW)),
        out_shape=jax.ShapeDtypeStruct((blocks, T, UW), BF16),
        scratch_shapes=[pltpu.VMEM((T, CH), F32)],
        compiler_params=pltpu.CompilerParams(vmem_limit_bytes=32 * 1024 * 1024),
        name="mix_forward",
    )(projected, *tables)


def mix_backward(projected, grad_joined, tables):
    blocks = projected.shape[0]
    return pl.pallas_call(
        mix_backward_kernel,
        grid=(blocks,),
        in_specs=[per_block((T, PAD)), per_block((T, UW)), *small_specs()],
        out_specs=[per_block((T, PAD)), per_block((8, CH)), per_block((8, 128)), per_block((8, SSM))],
        out_shape=[
            jax.ShapeDtypeStruct((blocks, T, PAD), BF16),
            jax.ShapeDtypeStruct((blocks, 8, CH), F32),
            jax.ShapeDtypeStruct((blocks, 8, 128), F32),
            jax.ShapeDtypeStruct((blocks, 8, SSM), F32),
        ],
        scratch_shapes=[
            pltpu.VMEM((T, CH), F32),
            pltpu.VMEM((T, CH), F32),
            pltpu.VMEM((T, CH), F32),
            pltpu.VMEM((128, T), F32),
        ],
        compiler_params=pltpu.CompilerParams(vmem_limit_bytes=40 * 1024 * 1024),
        name="mix_backward",
    )(projected, grad_joined, *tables)


def mixer_tables(segments, conv_rows, head_table):
    blocks = segments.shape[0]
    marks = segments.astype(F32)
    segc = jnp.broadcast_to(marks[:, :, None], (blocks, T, 128))
    segr = jnp.broadcast_to(marks[:, None, :], (blocks, 8, T))
    conv_rows = jnp.pad(conv_rows, ((0, 3), (0, 0)))
    head_rows = jnp.pad(head_table.T, ((0, 5), (0, 128 - MHEADS)))
    skip_rows = jnp.broadcast_to(jnp.repeat(head_table[:, 2], HEAD_WIDTH)[None], (8, SSM))
    return segc, segr, conv_rows, head_rows, skip_rows


MESH = pl.DeviceIdType.MESH
HOPS = ("xa", "xb", "za", "zb", "y")
PARTS = (
    (3, 0, 1024, ("y", "xa", "za", "xb", "zb")),
    (2, 0, 2048, ("za", "zb", "xa", "xb", "y")),
    (2, 2048, 2048, ("zb", "za", "xb", "xa", "y")),
    (1, 0, 1024, ("xa", "xb", "za", "zb", "y")),
    (0, 0, 2176, ("xb", "xa", "zb", "za", "y")),
    (0, 2176, 2048, ("y", "zb", "xb", "za", "xa")),
)
SHARD_ROWS = (64, 128, 64, 128)
SHARD_COLS = (PAD, 1024, 2 * FF, 1024)


def pair_a(i):
    return i + 1 - 2 * (i % 2)


def pair_b(i):
    return (i + 2 * (i % 2) + 3) % 4


def place():
    shard = lax.axis_index("shard")
    return lax.axis_index("section"), shard // 8, (shard // 2) % 4, shard % 2, lax.axis_index("rep")


def neighbours(section, y, z, core, x):
    def at(y, z, core, x):
        return (section, y * 8 + z * 2 + core, x)

    return {
        "core": at(y, z, 1 - core, x),
        "xa": at(y, z, core, pair_a(x)),
        "xb": at(y, z, core, pair_b(x)),
        "za": at(y, pair_a(z), core, x),
        "zb": at(y, pair_b(z), core, x),
        "y": at(1 - y, z, core, x),
        "xo": at(y, z, core, (x + 2) % 4),
    }


def meet(devices):
    barrier = pltpu.get_barrier_semaphore()
    for device in devices:
        pl.semaphore_signal(barrier, inc=1, device_id=device, device_id_type=MESH)
    pl.semaphore_wait(barrier, len(devices))


def halve(kept, hop, me):
    near, other = (pair_a, pair_b) if hop == "a" else (pair_b, pair_a)
    if len(kept) == 4:
        return [near(me), other(near(me))], [me, other(me)]
    return [near(me)], [me]


def schedule(order, me_y, me_z, me_x):
    every = [0, 1, 2, 3]
    ys, zs, xs = None, every, every
    stages = []

    def pieces(ys, zs, xs):
        zs = [None] if len(zs) == 4 else zs
        xs = [None] if len(xs) == 4 else xs
        return [(ys, z, x) for z in zs for x in xs]

    for hop in order:
        if hop == "y":
            stages.append((pieces(1 - me_y, zs, xs), pieces(me_y, zs, xs)))
            ys = me_y
        elif hop[0] == "z":
            sent, zs_kept = halve(zs, hop[1], me_z)
            stages.append((pieces(ys, sent, xs), pieces(ys, zs_kept, xs)))
            zs = zs_kept
        else:
            sent, xs_kept = halve(xs, hop[1], me_x)
            stages.append((pieces(ys, zs, sent), pieces(ys, zs, xs_kept)))
            xs = xs_kept
    return stages


def window(piece, quarter, column, columns):
    y, z, x = piece
    return (
        slice(0, 2) if y is None else pl.ds(y, 1),
        slice(0, 4) if z is None else pl.ds(z, 1),
        slice(0, 4 * quarter) if x is None else pl.ds(pl.multiple_of(x * quarter, quarter), quarter),
        pl.ds(column, columns),
    )


def piece_dims(piece, quarter):
    y, z, x = piece
    return (2 if y is None else 1, 4 if z is None else 1, 4 * quarter if x is None else quarter)


def stage_shapes():
    shapes = []
    for array, column, columns, order in PARTS:
        for sent, _ in schedule(order, 0, 0, 0):
            dims = piece_dims(sent[0], SHARD_ROWS[array] // 4)
            shapes.append((len(sent), *dims, columns))
    return shapes


def add_into(acc, window_at, arrived):
    ny, nz, rows, columns = arrived.shape
    ys, zs, rs, cs = window_at
    y0 = 0 if isinstance(ys, slice) else ys.start
    z0 = 0 if isinstance(zs, slice) else zs.start
    r0 = 0 if isinstance(rs, slice) else rs.start
    tiles = rows // 16

    def step(i, carry):
        y, rest = i // (nz * tiles), i % (nz * tiles)
        z, t = rest // tiles, rest % tiles
        row = pl.ds(pl.multiple_of(t * 16, 16), 16)
        at = (y0 + y, z0 + z, pl.ds(pl.multiple_of(r0 + t * 16, 16), 16), cs)
        acc[at] = acc[at] + arrived[y, z, row, :]
        return carry

    lax.fori_loop(0, ny * nz * tiles, step, 0)


def scatter_kernel(*refs):
    grads, outs = refs[:4], refs[4:8]
    accs, wholes, cores = refs[8:12], refs[12:16], refs[16:22]
    n_stage = len(PARTS) * len(HOPS)
    arrivals = refs[22 : 22 + n_stage]
    local_sem, core_send, core_recv, send_sem, recv_sem, last_send, last_recv = refs[22 + n_stage :]
    section, y, z, core, x = place()
    near = neighbours(section, y, z, core, x)
    meet([near[name] for name in ("core", *HOPS, "xo")])

    loads, swaps = [], []
    for p, (array, column, columns, _) in enumerate(PARTS):
        cols = pl.ds(column, columns)
        swap = pltpu.make_async_remote_copy(
            src_ref=grads[array].at[:, :, 1 - core, :, cols],
            dst_ref=cores[p],
            send_sem=core_send.at[p],
            recv_sem=core_recv.at[p],
            device_id=near["core"],
            device_id_type=MESH,
        )
        swap.start()
        load = pltpu.make_async_copy(
            grads[array].at[:, :, core, :, cols], accs[array].at[:, :, :, cols], local_sem.at[p]
        )
        load.start()
        swaps.append(swap)
        loads.append(load)

    plans = [schedule(order, y, z, x) for _, _, _, order in PARTS]
    flying = {}
    sems = 0
    for stage in range(len(HOPS) + 1):
        for p, (array, column, columns, order) in enumerate(PARTS):
            quarter = SHARD_ROWS[array] // 4
            if stage == 0:
                loads[p].wait()
                swaps[p].wait_recv()
                add_into(accs[array], window((None, None, None), quarter, column, columns), cores[p])
            else:
                kept = plans[p][stage - 1][1]
                for k, (copy, piece) in enumerate(zip(flying[p, stage - 1], kept)):
                    copy.wait_recv()
                    add_into(
                        accs[array],
                        window(piece, quarter, column, columns),
                        arrivals[p * len(HOPS) + stage - 1].at[k],
                    )
            if stage < len(HOPS):
                copies = []
                for k, piece in enumerate(plans[p][stage][0]):
                    copy = pltpu.make_async_remote_copy(
                        src_ref=accs[array].at[window(piece, quarter, column, columns)],
                        dst_ref=arrivals[p * len(HOPS) + stage].at[k],
                        send_sem=send_sem.at[sems],
                        recv_sem=recv_sem.at[sems],
                        device_id=near[order[stage]],
                        device_id_type=MESH,
                    )
                    copy.start()
                    copies.append(copy)
                    sems += 1
                flying[p, stage] = copies

    last = []
    for array in range(4):
        quarter = SHARD_ROWS[array] // 4
        mine = pl.ds(pl.multiple_of(x * quarter, quarter), quarter)
        for k, name in enumerate(("xo", "xa", "xb")):
            copy = pltpu.make_async_remote_copy(
                src_ref=accs[array].at[y, z, mine],
                dst_ref=wholes[array].at[mine],
                send_sem=last_send.at[array, k],
                recv_sem=last_recv.at[array, k],
                device_id=near[name],
                device_id_type=MESH,
            )
            copy.start()
            last.append(copy)
        outs[array][mine, :] = accs[array][y, z, mine, :].astype(F32)
    for array in range(4):
        quarter = SHARD_ROWS[array] // 4
        for k, owner in enumerate(((x + 2) % 4, pair_a(x), pair_b(x))):
            last[array * 3 + k].wait_recv()
            theirs = pl.ds(pl.multiple_of(owner * quarter, quarter), quarter)
            outs[array][theirs, :] = wholes[array][theirs, :].astype(F32)
    for copy in last + swaps + [c for copies in flying.values() for c in copies]:
        copy.wait_send()


def scatter_sums(grads):
    n_copies = sum(shape[0] for shape in stage_shapes())
    return pl.pallas_call(
        scatter_kernel,
        in_specs=[pl.BlockSpec(memory_space=pl.ANY)] * 4,
        out_specs=[pl.BlockSpec(memory_space=pltpu.VMEM)] * 4,
        out_shape=[jax.ShapeDtypeStruct(s, F32) for s in zip(SHARD_ROWS, SHARD_COLS)],
        scratch_shapes=[
            *[pltpu.VMEM((2, 4, r, c), BF16) for r, c in zip(SHARD_ROWS, SHARD_COLS)],
            *[pltpu.VMEM((r, c), BF16) for r, c in zip(SHARD_ROWS, SHARD_COLS)],
            *[pltpu.VMEM((2, 4, SHARD_ROWS[a], cols), BF16) for a, _, cols, _ in PARTS],
            *[pltpu.VMEM(shape, BF16) for shape in stage_shapes()],
            pltpu.SemaphoreType.DMA((len(PARTS),)),
            pltpu.SemaphoreType.DMA((len(PARTS),)),
            pltpu.SemaphoreType.DMA((len(PARTS),)),
            pltpu.SemaphoreType.DMA((n_copies,)),
            pltpu.SemaphoreType.DMA((n_copies,)),
            pltpu.SemaphoreType.DMA((4, 3)),
            pltpu.SemaphoreType.DMA((4, 3)),
        ],
        compiler_params=pltpu.CompilerParams(
            collective_id=1, has_side_effects=True, vmem_limit_bytes=58 * 1024 * 1024
        ),
        name="scatter_sums",
    )(*grads)


def gather_kernel(*refs):
    shards, outs = refs[:4], refs[4:8]
    local_sem, send_sem, recv_sem, core_send, core_recv = refs[8:]
    section, y, z, core, x = place()
    near = neighbours(section, y, z, core, x)
    meet([near[name] for name in ("core", *HOPS)])

    def at(array, piece, column, columns):
        ys, zs, rows, cols = window(piece, SHARD_ROWS[array] // 4, column, columns)
        return outs[array].at[ys, zs, pl.ds(core, 1), rows, cols]

    def own(array, column, columns):
        quarter = SHARD_ROWS[array] // 4
        rows = pl.ds(pl.multiple_of(x * quarter, quarter), quarter)
        return shards[array].at[:, :, :, rows, pl.ds(column, columns)]

    passed = []

    def pass_on(source, target):
        k = len(passed)
        copy = pltpu.make_async_remote_copy(
            src_ref=source,
            dst_ref=target,
            send_sem=core_send.at[k],
            recv_sem=core_recv.at[k],
            device_id=near["core"],
            device_id_type=MESH,
        )
        copy.start()
        passed.append(copy)

    locals_ = []
    for p, (array, column, columns, _) in enumerate(PARTS):
        copy = pltpu.make_async_copy(
            own(array, column, columns), at(array, (y, z, x), column, columns), local_sem.at[p]
        )
        copy.start()
        locals_.append(copy)

    plans = [schedule(order, y, z, x)[::-1] for _, _, _, order in PARTS]
    flying, sent = {}, []
    for stage in range(len(HOPS) + 1):
        for p, (array, column, columns, order) in enumerate(PARTS):
            if stage:
                for copy in flying[p, stage - 1]:
                    copy.wait_recv()
            if stage == 1:
                locals_[p].wait()
            if stage < len(HOPS):
                copies = []
                for piece in plans[p][stage][1]:
                    target = at(array, piece, column, columns)
                    copy = pltpu.make_async_remote_copy(
                        src_ref=target if stage else own(array, column, columns),
                        dst_ref=target,
                        send_sem=send_sem.at[len(sent)],
                        recv_sem=recv_sem.at[len(sent)],
                        device_id=near[order[::-1][stage]],
                        device_id_type=MESH,
                    )
                    copy.start()
                    copies.append(copy)
                    sent.append(copy)
                flying[p, stage] = copies
            if stage:
                for piece in plans[p][stage - 1][0]:
                    here = at(array, piece, column, columns)
                    pass_on(here, here)
            else:
                pass_on(own(array, column, columns), at(array, (y, z, x), column, columns))
    for copy in passed:
        copy.wait()
    for copy in sent:
        copy.wait_send()


def gather_shards(shards):
    n_copies = sum(shape[0] for shape in stage_shapes())
    n_passed = n_copies + len(PARTS)
    return pl.pallas_call(
        gather_kernel,
        in_specs=[pl.BlockSpec(memory_space=pl.ANY)] * 4,
        out_specs=[pl.BlockSpec(memory_space=pl.ANY)] * 4,
        out_shape=[
            jax.ShapeDtypeStruct((2, 4, 2, r, c), BF16) for r, c in zip(SHARD_ROWS, SHARD_COLS)
        ],
        scratch_shapes=[
            pltpu.SemaphoreType.DMA((len(PARTS),)),
            pltpu.SemaphoreType.DMA((n_copies,)),
            pltpu.SemaphoreType.DMA((n_copies,)),
            pltpu.SemaphoreType.DMA((n_passed,)),
            pltpu.SemaphoreType.DMA((n_passed,)),
        ],
        compiler_params=pltpu.CompilerParams(collective_id=2, has_side_effects=True),
        name="gather_shards",
    )(*shards)


def rms_norm(values, gain):
    return values * lax.rsqrt(jnp.mean(values * values, -1, keepdims=True) + 1e-05) * gain


def rms_back(values, gain, grad):
    scale = lax.rsqrt(jnp.mean(values * values, -1, keepdims=True) + 1e-05)
    unit = values * scale
    scaled = grad * gain
    grad_values = scale * (scaled - unit * jnp.mean(scaled * unit, -1, keepdims=True))
    return grad_values, jnp.sum(grad * unit, 0)


def forward_product(left, weight):
    return jnp.dot(left, weight, preferred_element_type=F32)


def back_product(grad_rows, weight):
    return lax.dot_general(
        grad_rows, weight, (((1,), (1,)), ((), ())), preferred_element_type=F32
    )


def outer_sum(left, right):
    return lax.dot_general(
        left, right, (((0,), (0,)), ((), ())), preferred_element_type=F32
    ).astype(BF16)


def layer_forward(inputs, weights, tables):
    gains, w_in, w_out, w_gate_up, w_down = weights
    blocks = inputs.shape[0] // T
    normed = rms_norm(inputs, gains[0]).astype(BF16)
    projected = forward_product(normed, w_in)
    joined = mix_forward(projected.reshape(blocks, T, PAD), tables).reshape(blocks * T, UW)
    hidden = inputs + forward_product(joined, w_out)
    normed_two = rms_norm(hidden, gains[1]).astype(BF16)
    gate_up = forward_product(normed_two, w_gate_up)
    activated = (jax.nn.silu(gate_up[:, :FF]) * gate_up[:, FF:]).astype(BF16)
    result = hidden + forward_product(activated, w_down)
    return result, (inputs, normed, projected, joined, hidden, normed_two, gate_up, activated)


def layer_backward(grad_out, saved, weights, tables):
    gains, w_in, w_out, w_gate_up, w_down = weights
    inputs, normed, projected, joined, hidden, normed_two, gate_up, activated = saved
    blocks = inputs.shape[0] // T
    grad_ffn = grad_out.astype(BF16)
    grad_act = back_product(grad_ffn, w_down)
    gate, up = gate_up[:, :FF], gate_up[:, FF:]
    sig = jax.nn.sigmoid(gate)
    grad_gate = (grad_act * up * (sig * (1.0 + gate * (1.0 - sig)))).astype(BF16)
    grad_up = (grad_act * (gate * sig)).astype(BF16)
    grad_gate_up = jnp.concatenate([grad_gate, grad_up], 1)
    grad_hidden, grad_gain_two = rms_back(hidden, gains[1], back_product(grad_gate_up, w_gate_up))
    grad_hidden = grad_out + grad_hidden
    grad_branch = grad_hidden.astype(BF16)
    grad_joined = back_product(grad_branch, w_out)
    grad_proj, grad_conv, grad_head, grad_skip = mix_backward(
        projected.reshape(blocks, T, PAD), grad_joined.reshape(blocks, T, UW), tables
    )
    grad_proj = grad_proj.reshape(blocks * T, PAD)
    grad_input, grad_gain_one = rms_back(inputs, gains[0], back_product(grad_proj, w_in))
    grad_input = grad_hidden + grad_input
    pairs = (
        (normed, grad_proj),
        (joined, grad_branch),
        (normed_two, grad_gate_up),
        (activated, grad_ffn),
    )
    return grad_input, pairs, (grad_gain_one, grad_gain_two, grad_conv, grad_head, grad_skip)


def across(array, by):
    return lax.ppermute(array, "section", [(0, 1)] if by > 0 else [(1, 0)])


def split_conv(rows):
    parts = rows.reshape(CONV + 1, -1, 2, 56).transpose(1, 0, 2, 3).reshape(-1, 10, 56)
    return jnp.pad(parts, ((0, 0), (0, 54), (0, 0))).reshape(-1, 56)


def join_conv(parts):
    return parts[:, :10].reshape(-1, CONV + 1, 2, 56).transpose(1, 0, 2, 3).reshape(CONV + 1, -1)


def gather_weights(norm_gains, w_in, conv_params, w_out, w_gate_up, w_down):
    filler = jnp.zeros((w_in.shape[0], PAD - PIN - 58), BF16)
    joined = jnp.concatenate([w_in, norm_gains, split_conv(conv_params.T), filler], 1)
    parts = gather_shards(
        [a.reshape(1, 1, 1, *a.shape) for a in (joined, w_out, w_gate_up, w_down)]
    )
    small = parts[0][..., PIN : PIN + 58].reshape(16, 64, 58).astype(F32)
    gains = small[:, :, :2].reshape(-1, 2).T
    return (gains, *[a.reshape(-1, a.shape[-1]) for a in parts]), join_conv(small[:, :, 2:])


def body(
    tokens,
    segment_ids,
    cotangent,
    norm_gains,
    w_in,
    conv_params,
    head_params,
    w_out,
    w_gate_up,
    w_down,
):
    section = lax.axis_index("section")
    blocks, _, width = tokens.shape
    rows = blocks * T
    weights, conv_rows = gather_weights(
        norm_gains[0], w_in[0], conv_params[0], w_out[0], w_gate_up[0], w_down[0]
    )
    tables = mixer_tables(segment_ids[:, 0], conv_rows, head_params[0].astype(F32))

    own = tokens.reshape(rows, width)
    first, _ = layer_forward(own.astype(F32), weights, tables)
    received = across(first.astype(BF16), 1)
    inputs = jnp.where(section == 0, own, received).astype(F32)
    result, saved = layer_forward(inputs, weights, tables)

    top = cotangent.reshape(rows, width)
    first_grad, _, _ = layer_backward(top.astype(F32), saved, weights, tables)
    coming = across(first_grad.astype(BF16), -1)
    grad_out = jnp.where(section == 1, top, coming).astype(F32)
    grad_input, pairs, smalls = layer_backward(grad_out, saved, weights, tables)

    grad_gain_one, grad_gain_two, grad_conv, grad_head, grad_skip = smalls
    sums = [outer_sum(left, right) for left, right in pairs]
    shards = lax.axis_size("shard")
    gains = jnp.stack([grad_gain_one, grad_gain_two], 1)
    conv = split_conv(jnp.sum(grad_conv, 0)[: CONV + 1])
    head = jnp.sum(grad_head, 0)[:2, :MHEADS]
    skip = jnp.sum(jnp.sum(grad_skip, 0)[0].reshape(MHEADS, HEAD_WIDTH), 1)
    head = jnp.concatenate([head, skip[None]], 0).T.reshape(-1)
    head = jnp.pad(head, (0, 128 - head.shape[0])).reshape(64, 2)
    head = jnp.broadcast_to(head[None], (shards, 64, 2)).reshape(shards * 64, 2)
    extra = jnp.concatenate([gains, conv, head], 1).astype(BF16)
    sums[0] = lax.dynamic_update_slice(sums[0], extra, (0, PIN))
    out_in, out_out, out_gu, out_dn = scatter_sums(
        [g.reshape(2, 4, 2, g.shape[0] // 16, g.shape[1]) for g in sums]
    )
    out_gains = out_in[:, PIN : PIN + 2]
    out_conv = join_conv(out_in[None, :, PIN + 2 : PIN + 58]).T
    out_head = out_in[:, PIN + 58 : PIN + 60].reshape(-1)[: MHEADS * 3]
    return (
        result.astype(BF16).reshape(1, blocks, T, width),
        grad_input.reshape(1, blocks, T, width),
        out_gains[None],
        out_in[None, :, :PIN],
        out_conv[None],
        out_head.reshape(1, MHEADS, 3),
        out_out[None],
        out_gu[None],
        out_dn[None],
    )


def solution(mesh):
    in_specs = (
        P(None, ("shard", "rep"), None),
        P(None, ("shard", "rep"), None),
        P(None, ("shard", "rep"), None),
        P("section", "shard", None),
        P("section", "shard", None),
        P("section", "shard", None),
        P("section", None, None),
        P("section", "shard", None),
        P("section", "shard", None),
        P("section", "shard", None),
    )
    out_specs = (
        P("section", None, ("shard", "rep"), None),
        P("section", None, ("shard", "rep"), None),
        P("section", "shard", None),
        P("section", "shard", None),
        P("section", "shard", None),
        P("section", None, None),
        P("section", "shard", None),
        P("section", "shard", None),
        P("section", "shard", None),
    )
    return jax.shard_map(body, mesh=mesh, in_specs=in_specs, out_specs=out_specs, check_vma=False)
```

```python
import itertools
import math

import jax
import jax.numpy as jnp
from jax import lax
from jax.experimental import pallas as pl
from jax.experimental.pallas import tpu as pltpu
from jax.sharding import PartitionSpec as P

FF = 2048
MHEADS = 24
HEAD_WIDTH = 64
STATE = 128
QUERY_HEAD_COUNT = 8
KVHEADS = 2
CONV = 4
SSM = 1536
CH = 1792
UW = 2048
PIN = 4120
PAD = 4224
T = 112
OFF_Q = SSM + CH
OFF_K = OFF_Q + QUERY_HEAD_COUNT * HEAD_WIDTH
OFF_V = OFF_K + KVHEADS * HEAD_WIDTH
OFF_R = OFF_V + KVHEADS * HEAD_WIDTH
F32 = jnp.float32
BF16 = jnp.bfloat16


def dot_nn(left, right):
    return jnp.dot(left.astype(BF16), right.astype(BF16), preferred_element_type=F32)


def dot_nt(left, right):
    return lax.dot_general(
        left.astype(BF16), right.astype(BF16), (((1,), (1,)), ((), ())), preferred_element_type=F32
    )


def dot_tn(left, right):
    return lax.dot_general(
        left.astype(BF16), right.astype(BF16), (((0,), (0,)), ((), ())), preferred_element_type=F32
    )


def exact_dot(left, right):
    return jnp.dot(left, right, precision=lax.Precision.HIGHEST, preferred_element_type=F32)


def iota(shape, dim):
    return lax.broadcasted_iota(jnp.int32, shape, dim)


def block_masks(segc, segr):
    rows, cols = iota((T, T), 0), iota((T, T), 1)
    allowed = (segc[:, :T] == segr[0:1, :]) & (rows >= cols)
    places = iota((T, 128), 0)
    links = [
        jnp.where((pltpu.roll(segc, j, 0) == segc) & (places >= j), 1.0, 0.0)
        for j in range(1, CONV)
    ]
    return allowed, links


def convolve(p_ref, conv_ref, links, mixed_ref, act_ref):
    for at in range(0, CH, 128):
        sl = slice(at, at + 128)
        c = p_ref[0, :, SSM + at : SSM + at + 128]
        mixed = conv_ref[4:5, sl] + c * conv_ref[0:1, sl]
        for j in range(1, CONV):
            mixed = mixed + links[j - 1] * pltpu.roll(c, j, 0) * conv_ref[j : j + 1, sl]
        if mixed_ref is not None:
            mixed_ref[:, sl] = mixed
        act_ref[:, sl] = mixed * jax.nn.sigmoid(mixed)


def softplus(v):
    return jnp.maximum(v, 0.0) + jnp.log1p(jnp.exp(-jnp.abs(v)))


def steps_and_sums(p_ref, head_ref):
    raw = p_ref[0, :, OFF_R:PAD] + head_ref[0:1, :]
    live = iota((T, 128), 1) < MHEADS
    raw = jnp.where(live, raw, 0.0)
    dt = softplus(raw)
    decay = -dt * jnp.exp(head_ref[1:2, :])
    lower = jnp.where(iota((T, T), 0) >= iota((T, T), 1), 1.0, 0.0)
    return raw, dt, decay, exact_dot(lower, decay)


def attention_probs(q_tile, keep, k_dup, allowed):
    scores = dot_nt(jnp.where(keep, q_tile, 0.0), k_dup) * (1.0 / math.sqrt(HEAD_WIDTH))
    scores = jnp.where(allowed, scores, -1e30)
    e = jnp.exp(scores - jnp.max(scores, -1, keepdims=True))
    return e / jnp.sum(e, -1, keepdims=True)


def doubled(tile, left):
    turned = pltpu.roll(tile, HEAD_WIDTH, 1)
    return jnp.where(left, tile, turned), jnp.where(left, turned, tile)


def mix_forward_kernel(p_ref, segc_ref, segr_ref, conv_ref, head_ref, skip_ref, u_ref, act_ref):
    allowed, links = block_masks(segc_ref[0], segr_ref[0])
    convolve(p_ref, conv_ref, links, None, act_ref)
    _, dt, _, cum = steps_and_sums(p_ref, head_ref)
    dt_t, cum_t = dt.T, cum.T
    left = iota((T, 128), 1) < HEAD_WIDTH
    cb = dot_nt(act_ref[:, SSM + STATE :], act_ref[:, SSM : SSM + STATE])
    for pair in range(MHEADS // 2):
        sl = slice(128 * pair, 128 * pair + 128)
        xs = act_ref[:, sl]
        ys = []
        for h in (2 * pair, 2 * pair + 1):
            decayed = jnp.exp(jnp.where(allowed, cum[:, h : h + 1] - cum_t[h : h + 1, :], -1e30))
            ys.append(dot_nn(decayed * cb * dt_t[h : h + 1, :], xs))
        y = jnp.where(left, ys[0], ys[1]) + skip_ref[0:1, sl] * xs
        z = p_ref[0, :, sl]
        u_ref[0, :, sl] = (y * (z * jax.nn.sigmoid(z))).astype(BF16)
    k_dups = doubled(p_ref[0, :, OFF_K:OFF_V], left)
    v_dups = doubled(p_ref[0, :, OFF_V:OFF_R], left)
    for pair in range(QUERY_HEAD_COUNT // 2):
        kv = pair // 2
        q_tile = p_ref[0, :, OFF_Q + 128 * pair : OFF_Q + 128 * pair + 128]
        probs = [attention_probs(q_tile, keep, k_dups[kv], allowed) for keep in (left, ~left)]
        out = [dot_nn(pr, v_dups[kv]) for pr in probs]
        u_ref[0, :, SSM + 128 * pair : SSM + 128 * pair + 128] = jnp.where(
            left, out[0], out[1]
        ).astype(BF16)


def mix_backward_kernel(
    p_ref, gu_ref, segc_ref, segr_ref, conv_ref, head_ref, skip_ref,
    gp_ref, gconv_ref, ghead_ref, gskip_ref,
    mixed_ref, act_ref, gact_ref, colq_ref,
):
    allowed, links = block_masks(segc_ref[0], segr_ref[0])
    convolve(p_ref, conv_ref, links, mixed_ref, act_ref)
    raw, dt, decay, cum = steps_and_sums(p_ref, head_ref)
    dt_t, cum_t = dt.T, cum.T
    lanes = iota((T, 128), 1)
    left = lanes < HEAD_WIDTH
    b_rows = act_ref[:, SSM : SSM + STATE]
    c_rows = act_ref[:, SSM + STATE :]
    cb = dot_nt(c_rows, b_rows)
    gcb = jnp.zeros((T, T), F32)
    row_form = jnp.zeros((T, 128), F32)
    colq_ref[...] = jnp.zeros_like(colq_ref)
    for pair in range(MHEADS // 2):
        sl = slice(128 * pair, 128 * pair + 128)
        xs = act_ref[:, sl]
        xs16 = xs.astype(BF16)
        z = p_ref[0, :, sl]
        gm = gu_ref[0, :, sl]
        sg = jax.nn.sigmoid(z)
        gy = gm * (z * sg)
        gy16 = gy.astype(BF16)
        ys, gxs = [], []
        for h, keep in ((2 * pair, left), (2 * pair + 1, ~left)):
            decayed = jnp.exp(jnp.where(allowed, cum[:, h : h + 1] - cum_t[h : h + 1, :], -1e30))
            dt_row = dt_t[h : h + 1, :]
            base = decayed * cb
            k16 = (base * dt_row).astype(BF16)
            ys.append(dot_nn(k16, xs16))
            gxs.append(dot_tn(k16, gy16))
            gk = dot_nt(jnp.where(keep, gy, 0.0), xs16)
            gcb = gcb + gk * (decayed * dt_row)
            q = gk * base
            colq_ref[h : h + 1, :] = jnp.sum(q, 0, keepdims=True)
            row_form = jnp.where(lanes == h, jnp.sum(q * dt_row, 1, keepdims=True), row_form)
        skip = skip_ref[0:1, sl]
        y = jnp.where(left, ys[0], ys[1]) + skip * xs
        gp_ref[0, :, sl] = (gm * y * (sg * (1.0 + z * (1.0 - sg)))).astype(BF16)
        gact_ref[:, sl] = jnp.where(left, gxs[0], gxs[1]) + skip * gy
        gskip_ref[0, 0:1, sl] = jnp.sum(gy * xs, 0, keepdims=True)
    gact_ref[:, SSM : SSM + STATE] = dot_tn(gcb, c_rows)
    gact_ref[:, SSM + STATE :] = dot_nn(gcb, b_rows)
    col_form = colq_ref[...].T
    gcum = row_form - col_form * dt
    upper = jnp.where(iota((T, T), 0) <= iota((T, T), 1), 1.0, 0.0)
    gdecay = exact_dot(upper, gcum)
    gdt = col_form - gdecay * jnp.exp(head_ref[1:2, :])
    graw = jnp.where(lanes < MHEADS, gdt * jax.nn.sigmoid(raw), 0.0)
    gp_ref[0, :, OFF_R:PAD] = graw.astype(BF16)
    ghead_ref[0, 0:1, :] = jnp.sum(graw, 0, keepdims=True)
    ghead_ref[0, 1:2, :] = jnp.sum(gdecay * decay, 0, keepdims=True)
    for at in range(0, CH, 128):
        sl = slice(at, at + 128)
        mixed = mixed_ref[:, sl]
        sg = jax.nn.sigmoid(mixed)
        gmix = gact_ref[:, sl] * (sg * (1.0 + mixed * (1.0 - sg)))
        c = p_ref[0, :, SSM + at : SSM + at + 128]
        gc = gmix * conv_ref[0:1, sl]
        gconv_ref[0, 0:1, sl] = jnp.sum(gmix * c, 0, keepdims=True)
        for j in range(1, CONV):
            linked = gmix * links[j - 1]
            gc = gc + pltpu.roll(linked, T - j, 0) * conv_ref[j : j + 1, sl]
            gconv_ref[0, j : j + 1, sl] = jnp.sum(linked * pltpu.roll(c, j, 0), 0, keepdims=True)
        gconv_ref[0, 4:5, sl] = jnp.sum(gmix, 0, keepdims=True)
        gp_ref[0, :, SSM + at : SSM + at + 128] = gc.astype(BF16)
    k_dups = doubled(p_ref[0, :, OFF_K:OFF_V], left)
    v_dups = doubled(p_ref[0, :, OFF_V:OFF_R], left)
    gks, gvs = [], []
    for kv in range(KVHEADS):
        gk_sum = jnp.zeros((T, 128), F32)
        gv_sum = jnp.zeros((T, 128), F32)
        for pair in (2 * kv, 2 * kv + 1):
            sl = slice(OFF_Q + 128 * pair, OFF_Q + 128 * pair + 128)
            q_tile = p_ref[0, :, sl]
            go = gu_ref[0, :, SSM + 128 * pair : SSM + 128 * pair + 128]
            gq, gk, gv = [], [], []
            for keep in (left, ~left):
                probs = attention_probs(q_tile, keep, k_dups[kv], allowed)
                gpr = dot_nt(jnp.where(keep, go, 0.0), v_dups[kv])
                gs = probs * (gpr - jnp.sum(gpr * probs, -1, keepdims=True))
                gs = (gs * (1.0 / math.sqrt(HEAD_WIDTH))).astype(BF16)
                gq.append(dot_nn(gs, k_dups[kv]))
                gk.append(dot_tn(gs, q_tile))
                gv.append(dot_tn(probs, go))
            gp_ref[0, :, sl] = jnp.where(left, gq[0], gq[1]).astype(BF16)
            gk_sum = gk_sum + jnp.where(left, gk[0], gk[1])
            gv_sum = gv_sum + jnp.where(left, gv[0], gv[1])
        gks.append(gk_sum + pltpu.roll(gk_sum, HEAD_WIDTH, 1))
        gvs.append(gv_sum + pltpu.roll(gv_sum, HEAD_WIDTH, 1))
    gp_ref[0, :, OFF_K:OFF_V] = jnp.where(left, gks[0], gks[1]).astype(BF16)
    gp_ref[0, :, OFF_V:OFF_R] = jnp.where(left, gvs[0], gvs[1]).astype(BF16)


def whole(shape):
    return pl.BlockSpec(shape, lambda m: (0,) * len(shape))


def per_block(shape):
    return pl.BlockSpec((1, *shape), lambda m: (m,) + (0,) * len(shape))


def small_specs():
    return [
        per_block((T, 128)), per_block((8, T)), whole((8, CH)), whole((8, 128)), whole((8, SSM)),
    ]


def mix_forward(projected, tables):
    blocks = projected.shape[0]
    return pl.pallas_call(
        mix_forward_kernel,
        grid=(blocks,),
        in_specs=[per_block((T, PAD)), *small_specs()],
        out_specs=per_block((T, UW)),
        out_shape=jax.ShapeDtypeStruct((blocks, T, UW), BF16),
        scratch_shapes=[pltpu.VMEM((T, CH), F32)],
        compiler_params=pltpu.CompilerParams(vmem_limit_bytes=32 * 1024 * 1024),
        name="mix_forward",
    )(projected, *tables)


def mix_backward(projected, grad_joined, tables):
    blocks = projected.shape[0]
    return pl.pallas_call(
        mix_backward_kernel,
        grid=(blocks,),
        in_specs=[per_block((T, PAD)), per_block((T, UW)), *small_specs()],
        out_specs=[per_block((T, PAD)), per_block((8, CH)), per_block((8, 128)), per_block((8, SSM))],
        out_shape=[
            jax.ShapeDtypeStruct((blocks, T, PAD), BF16),
            jax.ShapeDtypeStruct((blocks, 8, CH), F32),
            jax.ShapeDtypeStruct((blocks, 8, 128), F32),
            jax.ShapeDtypeStruct((blocks, 8, SSM), F32),
        ],
        scratch_shapes=[
            pltpu.VMEM((T, CH), F32),
            pltpu.VMEM((T, CH), F32),
            pltpu.VMEM((T, CH), F32),
            pltpu.VMEM((128, T), F32),
        ],
        compiler_params=pltpu.CompilerParams(vmem_limit_bytes=40 * 1024 * 1024),
        name="mix_backward",
    )(projected, grad_joined, *tables)


def mixer_tables(segments, conv_rows, head_table):
    blocks = segments.shape[0]
    marks = segments.astype(F32)
    segc = jnp.broadcast_to(marks[:, :, None], (blocks, T, 128))
    segr = jnp.broadcast_to(marks[:, None, :], (blocks, 8, T))
    conv_rows = jnp.pad(conv_rows, ((0, 3), (0, 0)))
    head_rows = jnp.pad(head_table.T, ((0, 5), (0, 128 - MHEADS)))
    skip_rows = jnp.broadcast_to(jnp.repeat(head_table[:, 2], HEAD_WIDTH)[None], (8, SSM))
    return segc, segr, conv_rows, head_rows, skip_rows


MESH = pl.DeviceIdType.MESH
HOPS = ("xa", "xb", "za", "zb", "y")
ORDERS = (
    ("xa", "xb", "zb", "za", "y"),
    ("xb", "xa", "y", "zb", "za"),
    ("za", "zb", "xa", "y", "xb"),
    ("zb", "y", "za", "xb", "xa"),
    ("y", "za", "xb", "xa", "zb"),
)


def cut(array, tiles, orders=(0, 1, 2, 3, 4), first=0):
    parts = []
    for width, order in zip(tiles, orders):
        parts.append((array, 128 * first, 128 * width, ORDERS[order]))
        first += width
    return parts


GATHERED = (
    *cut(0, (7, 7, 7, 6, 5)),
    *cut(0, (1,), (4,), 32),
    *cut(1, (2, 3, 3), (2, 3, 4)),
    *cut(2, (7, 7, 6, 6, 6)),
    *cut(3, (3, 3, 2)),
)
SCATTERED = (
    *cut(3, (3, 3, 2)),
    *cut(1, (2, 3, 3), (2, 3, 4)),
    *cut(2, (7, 7, 6, 6, 6)),
    *cut(0, (7, 7, 7, 6, 6)),
    *cut(0, (1,), (4,), 33),
)
TAIL = 2 * FF
EXTRA = PAD
SHARD_ROWS = (64, 128, 64, 128)
SHARD_COLS = (PAD, 1024, 2 * FF, 1024)
SUM_COLS = (PAD + 128, 1024, 2 * FF, 1024)


def pair_a(i):
    return i + 1 - 2 * (i % 2)


def pair_b(i):
    return (i + 2 * (i % 2) + 3) % 4


def place():
    shard = lax.axis_index("shard")
    return lax.axis_index("section"), shard // 8, (shard // 2) % 4, shard % 2, lax.axis_index("rep")


def neighbours(section, y, z, core, x):
    def at(y, z, core, x):
        return (section, y * 8 + z * 2 + core, x)

    return {
        "core": at(y, z, 1 - core, x),
        "xa": at(y, z, core, pair_a(x)),
        "xb": at(y, z, core, pair_b(x)),
        "za": at(y, pair_a(z), core, x),
        "zb": at(y, pair_b(z), core, x),
        "y": at(1 - y, z, core, x),
        "xo": at(y, z, core, (x + 2) % 4),
    }


def meet(devices):
    barrier = pltpu.get_barrier_semaphore()
    for device in devices:
        pl.semaphore_signal(barrier, inc=1, device_id=device, device_id_type=MESH)
    pl.semaphore_wait(barrier, len(devices))


def halve(kept, hop, me):
    near, other = (pair_a, pair_b) if hop == "a" else (pair_b, pair_a)
    if kept[0][1] != 4:
        return [(near(me), 1)], [(me, 1)]
    if hop == "b":
        return [(2 * (near(me) // 2), 2)], [(2 * (me // 2), 2)]
    return [(near(me), 1), (other(near(me)), 1)], [(me, 1), (other(me), 1)]


def schedule(order, me_y, me_z, me_x):
    ys, zs, xs = [(0, 2)], [(0, 4)], [(0, 4)]
    stages = []
    for hop in order:
        if hop == "y":
            sent, ys = [(1 - me_y, 1)], [(me_y, 1)]
            gone = sent, zs, xs
        elif hop[0] == "z":
            sent, zs = halve(zs, hop[1], me_z)
            gone = ys, sent, xs
        else:
            sent, xs = halve(xs, hop[1], me_x)
            gone = ys, zs, sent
        stages.append((list(itertools.product(*gone)), list(itertools.product(ys, zs, xs))))
    return stages


def window(piece, quarter, column, columns):
    (y, ny), (z, nz), (x, nx) = piece
    rows = 0 if nx == 4 else pl.multiple_of(x * quarter, nx * quarter)
    return pl.ds(y, ny), pl.ds(z, nz), pl.ds(rows, nx * quarter), pl.ds(column, columns)


def piece_dims(piece, quarter):
    (_, ny), (_, nz), (_, nx) = piece
    return ny, nz, nx * quarter


def stage_shapes(parts):
    shapes = []
    for array, column, columns, order in parts:
        for sent, _ in schedule(order, 0, 0, 0):
            dims = piece_dims(sent[0], SHARD_ROWS[array] // 4)
            shapes.append((len(sent), *dims, columns))
    return shapes


def add_into(acc, window_at, arrived):
    ny, nz, rows, _ = arrived.shape
    ys, zs, rs, cs = window_at

    def step(i, carry):
        y, z = i // nz, i % nz
        at = (ys.start + y, zs.start + z, rs, cs)
        acc[at] = acc[at] + arrived[y, z]
        return carry

    if ny * nz == 1:
        step(0, 0)
    else:
        lax.fori_loop(0, ny * nz, step, 0)


def scatter_kernel(*refs):
    grads, extra, outs, smalls = refs[:4], refs[4], refs[5:9], refs[9:12]
    accs, wholes, cores = refs[12:16], refs[16:20], refs[20 : 20 + len(SCATTERED)]
    arrivals = refs[20 + len(SCATTERED) : -7]
    local_sem, core_send, core_recv, send_sem, recv_sem, last_send, last_recv = refs[-7:]
    section, y, z, core, x = place()
    near = neighbours(section, y, z, core, x)
    meet([near[name] for name in ("core", *HOPS, "xo")])

    loads, swaps = [], []
    for p, (array, column, columns, _) in enumerate(SCATTERED):
        cols = pl.ds(column, columns)
        grad = extra if (array, column) == (0, EXTRA) else grads[array].at[:, :, :, :, cols]
        swap = pltpu.make_async_remote_copy(
            src_ref=grad.at[:, :, 1 - core],
            dst_ref=cores[p],
            send_sem=core_send.at[p],
            recv_sem=core_recv.at[p],
            device_id=near["core"],
            device_id_type=MESH,
        )
        swap.start()
        load = pltpu.make_async_copy(
            grad.at[:, :, core], accs[array].at[:, :, :, cols], local_sem.at[p]
        )
        load.start()
        swaps.append(swap)
        loads.append(load)

    plans = [schedule(order, y, z, x) for _, _, _, order in SCATTERED]
    flying = {}
    sems = 0
    for stage in range(len(HOPS) + 1):
        for p, (array, column, columns, order) in enumerate(SCATTERED):
            quarter = SHARD_ROWS[array] // 4
            if stage == 0:
                loads[p].wait()
                swaps[p].wait_recv()
                add_into(accs[array], window(((0, 2), (0, 4), (0, 4)), quarter, column, columns), cores[p])
            else:
                kept = plans[p][stage - 1][1]
                for k, (copy, piece) in enumerate(zip(flying[p, stage - 1], kept)):
                    copy.wait_recv()
                    add_into(
                        accs[array],
                        window(piece, quarter, column, columns),
                        arrivals[p * len(HOPS) + stage - 1].at[k],
                    )
            if stage < len(HOPS):
                copies = []
                for k, piece in enumerate(plans[p][stage][0]):
                    copy = pltpu.make_async_remote_copy(
                        src_ref=accs[array].at[window(piece, quarter, column, columns)],
                        dst_ref=arrivals[p * len(HOPS) + stage].at[k],
                        send_sem=send_sem.at[sems],
                        recv_sem=recv_sem.at[sems],
                        device_id=near[order[stage]],
                        device_id_type=MESH,
                    )
                    copy.start()
                    copies.append(copy)
                    sems += 1
                flying[p, stage] = copies

    last = []
    for array in range(4):
        quarter = SHARD_ROWS[array] // 4
        mine = pl.ds(pl.multiple_of(x * quarter, quarter), quarter)
        for k, name in enumerate(("xo", "xa", "xb")):
            copy = pltpu.make_async_remote_copy(
                src_ref=accs[array].at[y, z, mine],
                dst_ref=wholes[array].at[mine],
                send_sem=last_send.at[array, k],
                recv_sem=last_recv.at[array, k],
                device_id=near[name],
                device_id_type=MESH,
            )
            copy.start()
            last.append(copy)
        wholes[array][mine, :] = accs[array][y, z, mine, :]
    for array in range(4):
        for k in range(3):
            last[array * 3 + k].wait_recv()
        outs[array][...] = wholes[array][:, : outs[array].shape[1]].astype(F32)
    small = wholes[0][:, EXTRA:].astype(F32)
    out_gains, out_conv, out_head = smalls
    out_gains[...] = small[:, :2]
    out_conv[:56, :] = small[:56, 2 : 3 + CONV]
    out_conv[56:, :] = small[:56, 3 + CONV : 4 + 2 * CONV]
    out_head[...] = small[:MHEADS, 12:15]
    for copy in last + swaps + [c for copies in flying.values() for c in copies]:
        copy.wait_send()


def scatter_sums(grads, extra):
    n_copies = sum(shape[0] for shape in stage_shapes(SCATTERED))
    n_parts = len(SCATTERED)
    out_shapes = [
        (64, PIN), (128, 1024), (64, 2 * FF), (128, 1024), (64, 2), (112, CONV + 1), (MHEADS, 3),
    ]
    return pl.pallas_call(
        scatter_kernel,
        in_specs=[pl.BlockSpec(memory_space=pl.ANY)] * 5,
        out_specs=[pl.BlockSpec(memory_space=pltpu.VMEM)] * 7,
        out_shape=[jax.ShapeDtypeStruct(s, F32) for s in out_shapes],
        scratch_shapes=[
            *[pltpu.VMEM((2, 4, r, c), BF16) for r, c in zip(SHARD_ROWS, SUM_COLS)],
            *[pltpu.VMEM((r, c), BF16) for r, c in zip(SHARD_ROWS, SUM_COLS)],
            *[pltpu.VMEM((2, 4, SHARD_ROWS[a], cols), BF16) for a, _, cols, _ in SCATTERED],
            *[pltpu.VMEM(shape, BF16) for shape in stage_shapes(SCATTERED)],
            pltpu.SemaphoreType.DMA((n_parts,)),
            pltpu.SemaphoreType.DMA((n_parts,)),
            pltpu.SemaphoreType.DMA((n_parts,)),
            pltpu.SemaphoreType.DMA((n_copies,)),
            pltpu.SemaphoreType.DMA((n_copies,)),
            pltpu.SemaphoreType.DMA((4, 3)),
            pltpu.SemaphoreType.DMA((4, 3)),
        ],
        compiler_params=pltpu.CompilerParams(
            collective_id=1, has_side_effects=True, vmem_limit_bytes=58 * 1024 * 1024
        ),
        name="scatter_sums",
    )(*grads, extra)


def gather_kernel(*refs):
    shards, tail, outs = refs[:4], refs[4], refs[5:9]
    local_sem, send_sem, recv_sem, core_send, core_recv = refs[9:]
    section, y, z, core, x = place()
    near = neighbours(section, y, z, core, x)
    meet([near[name] for name in ("core", *HOPS)])

    def at(array, piece, column, columns):
        ys, zs, rows, cols = window(piece, SHARD_ROWS[array] // 4, column, columns)
        return outs[array].at[ys, zs, pl.ds(core, 1), rows, cols]

    def own(array, column, columns):
        quarter = SHARD_ROWS[array] // 4
        rows = pl.ds(pl.multiple_of(x * quarter, quarter), quarter)
        if (array, column) == (0, TAIL):
            return tail.at[:, :, :, rows]
        return shards[array].at[:, :, :, rows, pl.ds(column, columns)]

    passed = []

    def pass_on(source, target):
        k = len(passed)
        copy = pltpu.make_async_remote_copy(
            src_ref=source,
            dst_ref=target,
            send_sem=core_send.at[k],
            recv_sem=core_recv.at[k],
            device_id=near["core"],
            device_id_type=MESH,
        )
        copy.start()
        passed.append(copy)

    locals_ = []
    for p, (array, column, columns, _) in enumerate(GATHERED):
        copy = pltpu.make_async_copy(
            own(array, column, columns), at(array, ((y, 1), (z, 1), (x, 1)), column, columns), local_sem.at[p]
        )
        copy.start()
        locals_.append(copy)

    plans = [schedule(order, y, z, x)[::-1] for _, _, _, order in GATHERED]
    flying, sent = {}, []
    for stage in range(len(HOPS) + 1):
        for p, (array, column, columns, order) in enumerate(GATHERED):
            if stage:
                for copy in flying[p, stage - 1]:
                    copy.wait_recv()
            if stage == 1:
                locals_[p].wait()
            if stage < len(HOPS):
                copies = []
                for piece in plans[p][stage][1]:
                    target = at(array, piece, column, columns)
                    copy = pltpu.make_async_remote_copy(
                        src_ref=target if stage else own(array, column, columns),
                        dst_ref=target,
                        send_sem=send_sem.at[len(sent)],
                        recv_sem=recv_sem.at[len(sent)],
                        device_id=near[order[::-1][stage]],
                        device_id_type=MESH,
                    )
                    copy.start()
                    copies.append(copy)
                    sent.append(copy)
                flying[p, stage] = copies
            if stage:
                for piece in plans[p][stage - 1][0]:
                    here = at(array, piece, column, columns)
                    pass_on(here, here)
            else:
                pass_on(own(array, column, columns), at(array, ((y, 1), (z, 1), (x, 1)), column, columns))
    for copy in passed:
        copy.wait()
    for copy in sent:
        copy.wait_send()


def gather_shards(shards, tail):
    n_copies = sum(shape[0] for shape in stage_shapes(GATHERED))
    n_passed = n_copies + len(GATHERED)
    return pl.pallas_call(
        gather_kernel,
        in_specs=[pl.BlockSpec(memory_space=pl.ANY)] * 5,
        out_specs=[pl.BlockSpec(memory_space=pl.ANY)] * 4,
        out_shape=[
            jax.ShapeDtypeStruct((2, 4, 2, r, c), BF16) for r, c in zip(SHARD_ROWS, SHARD_COLS)
        ],
        scratch_shapes=[
            pltpu.SemaphoreType.DMA((len(GATHERED),)),
            pltpu.SemaphoreType.DMA((n_copies,)),
            pltpu.SemaphoreType.DMA((n_copies,)),
            pltpu.SemaphoreType.DMA((n_passed,)),
            pltpu.SemaphoreType.DMA((n_passed,)),
        ],
        compiler_params=pltpu.CompilerParams(collective_id=2, has_side_effects=True),
        name="gather_shards",
    )(*shards, tail)


def rms_norm(values, gain):
    return values * lax.rsqrt(jnp.mean(values * values, -1, keepdims=True) + 1e-05) * gain


def rms_back(values, gain, grad):
    scale = lax.rsqrt(jnp.mean(values * values, -1, keepdims=True) + 1e-05)
    unit = values * scale
    scaled = grad * gain
    grad_values = scale * (scaled - unit * jnp.mean(scaled * unit, -1, keepdims=True))
    return grad_values, jnp.sum(grad * unit, 0)


def forward_product(left, weight):
    return jnp.dot(left, weight, preferred_element_type=F32)


def back_product(grad_rows, weight):
    return lax.dot_general(
        grad_rows, weight, (((1,), (1,)), ((), ())), preferred_element_type=F32
    )


def outer_sum(left, right):
    return lax.dot_general(
        left, right, (((0,), (0,)), ((), ())), preferred_element_type=F32
    ).astype(BF16)


def layer_forward(inputs, weights, tables):
    gains, w_in, w_out, w_gate_up, w_down = weights
    blocks = inputs.shape[0] // T
    normed = rms_norm(inputs, gains[0]).astype(BF16)
    projected = forward_product(normed, w_in)
    joined = mix_forward(projected.reshape(blocks, T, PAD), tables).reshape(blocks * T, UW)
    hidden = inputs + forward_product(joined, w_out)
    normed_two = rms_norm(hidden, gains[1]).astype(BF16)
    gate_up = forward_product(normed_two, w_gate_up)
    activated = (jax.nn.silu(gate_up[:, :FF]) * gate_up[:, FF:]).astype(BF16)
    result = hidden + forward_product(activated, w_down)
    return result, (inputs, normed, projected, joined, hidden, normed_two, gate_up, activated)


def layer_backward(grad_out, saved, weights, tables):
    gains, w_in, w_out, w_gate_up, w_down = weights
    inputs, normed, projected, joined, hidden, normed_two, gate_up, activated = saved
    blocks = inputs.shape[0] // T
    grad_ffn = grad_out.astype(BF16)
    grad_act = back_product(grad_ffn, w_down)
    gate, up = gate_up[:, :FF], gate_up[:, FF:]
    sig = jax.nn.sigmoid(gate)
    grad_gate = (grad_act * up * (sig * (1.0 + gate * (1.0 - sig)))).astype(BF16)
    grad_up = (grad_act * (gate * sig)).astype(BF16)
    grad_gate_up = jnp.concatenate([grad_gate, grad_up], 1)
    grad_hidden, grad_gain_two = rms_back(hidden, gains[1], back_product(grad_gate_up, w_gate_up))
    grad_hidden = grad_out + grad_hidden
    grad_branch = grad_hidden.astype(BF16)
    grad_joined = back_product(grad_branch, w_out)
    grad_proj, grad_conv, grad_head, grad_skip = mix_backward(
        projected.reshape(blocks, T, PAD), grad_joined.reshape(blocks, T, UW), tables
    )
    grad_proj = grad_proj.reshape(blocks * T, PAD)
    grad_input, grad_gain_one = rms_back(inputs, gains[0], back_product(grad_proj, w_in))
    grad_input = grad_hidden + grad_input
    pairs = (
        (normed, grad_proj),
        (joined, grad_branch),
        (normed_two, grad_gate_up),
        (activated, grad_ffn),
    )
    return grad_input, pairs, (grad_gain_one, grad_gain_two, grad_conv, grad_head, grad_skip)


def across(array, by):
    return lax.ppermute(array, "section", [(0, 1)] if by > 0 else [(1, 0)])


def split_conv(table):
    parts = table.reshape(-1, 2, 56, CONV + 1).transpose(0, 2, 1, 3).reshape(-1, 56, 2 * (CONV + 1))
    return jnp.pad(parts, ((0, 0), (0, 8), (0, 0))).reshape(-1, 2 * (CONV + 1))


def join_conv(parts):
    parts = parts[:, :56].reshape(-1, 56, 2, CONV + 1)
    return parts.transpose(3, 0, 2, 1).reshape(CONV + 1, -1)


def gather_weights(norm_gains, w_in, conv_params, w_out, w_gate_up, w_down):
    filler = jnp.zeros((w_in.shape[0], PAD - PIN - 12), BF16)
    tail = jnp.concatenate([w_in[:, TAIL:], norm_gains, split_conv(conv_params), filler], 1)
    parts = gather_shards(
        [a.reshape(1, 1, 1, *a.shape) for a in (w_in, w_out, w_gate_up, w_down)],
        tail.reshape(1, 1, 1, *tail.shape),
    )
    small = parts[0][..., PIN : PIN + 12].reshape(16, 64, 12).astype(F32)
    gains = small[:, :, :2].reshape(-1, 2).T
    return (gains, *[a.reshape(-1, a.shape[-1]) for a in parts]), join_conv(small[:, :, 2:])


def body(
    tokens,
    segment_ids,
    cotangent,
    norm_gains,
    w_in,
    conv_params,
    head_params,
    w_out,
    w_gate_up,
    w_down,
):
    section = lax.axis_index("section")
    blocks, _, width = tokens.shape
    rows = blocks * T
    weights, conv_rows = gather_weights(
        norm_gains[0], w_in[0], conv_params[0], w_out[0], w_gate_up[0], w_down[0]
    )
    tables = mixer_tables(segment_ids[:, 0], conv_rows, head_params[0].astype(F32))

    own = tokens.reshape(rows, width)
    first, _ = layer_forward(own.astype(F32), weights, tables)
    received = across(first.astype(BF16), 1)
    inputs = jnp.where(section == 0, own, received).astype(F32)
    result, saved = layer_forward(inputs, weights, tables)

    top = cotangent.reshape(rows, width)
    first_grad, _, _ = layer_backward(top.astype(F32), saved, weights, tables)
    coming = across(first_grad.astype(BF16), -1)
    grad_out = jnp.where(section == 1, top, coming).astype(F32)
    grad_input, pairs, smalls = layer_backward(grad_out, saved, weights, tables)

    grad_gain_one, grad_gain_two, grad_conv, grad_head, grad_skip = smalls
    sums = [outer_sum(left, right) for left, right in pairs]
    shards = lax.axis_size("shard")
    gains = jnp.stack([grad_gain_one, grad_gain_two], 1)
    conv = split_conv(jnp.sum(grad_conv, 0)[: CONV + 1].T)
    head = jnp.sum(grad_head, 0)[:2, :MHEADS]
    skip = jnp.sum(jnp.sum(grad_skip, 0)[0].reshape(MHEADS, HEAD_WIDTH), 1)
    head = jnp.pad(jnp.concatenate([head, skip[None]], 0).T, ((0, 64 - MHEADS), (0, 0)))
    head = jnp.broadcast_to(head[None], (shards, 64, 3)).reshape(shards * 64, 3)
    extra = jnp.concatenate([gains, conv, head], 1)
    extra = jnp.pad(extra, ((0, 0), (0, 128 - extra.shape[1]))).astype(BF16)
    out_in, out_out, out_gu, out_dn, out_gains, out_conv, out_head = scatter_sums(
        [g.reshape(2, 4, 2, g.shape[0] // 16, g.shape[1]) for g in sums],
        extra.reshape(2, 4, 2, 64, 128),
    )
    return (
        result.astype(BF16).reshape(1, blocks, T, width),
        grad_input.reshape(1, blocks, T, width),
        out_gains[None],
        out_in[None],
        out_conv[None],
        out_head[None],
        out_out[None],
        out_gu[None],
        out_dn[None],
    )


def solution(mesh):
    in_specs = (
        P(None, ("shard", "rep"), None),
        P(None, ("shard", "rep"), None),
        P(None, ("shard", "rep"), None),
        P("section", "shard", None),
        P("section", "shard", None),
        P("section", "shard", None),
        P("section", None, None),
        P("section", "shard", None),
        P("section", "shard", None),
        P("section", "shard", None),
    )
    out_specs = (
        P("section", None, ("shard", "rep"), None),
        P("section", None, ("shard", "rep"), None),
        P("section", "shard", None),
        P("section", "shard", None),
        P("section", "shard", None),
        P("section", None, None),
        P("section", "shard", None),
        P("section", "shard", None),
        P("section", "shard", None),
    )
    return jax.shard_map(body, mesh=mesh, in_specs=in_specs, out_specs=out_specs, check_vma=False)
```

```python
import itertools
import math

import jax
import jax.numpy as jnp
from jax import lax
from jax.experimental import pallas as pl
from jax.experimental.pallas import tpu as pltpu
from jax.sharding import PartitionSpec as P

FF = 2048
MHEADS = 24
HEAD_WIDTH = 64
STATE = 128
QUERY_HEAD_COUNT = 8
KVHEADS = 2
CONV = 4
SSM = 1536
CH = 1792
UW = 2048
PIN = 4120
PAD = 4224
T = 112
OFF_Q = SSM + CH
OFF_K = OFF_Q + QUERY_HEAD_COUNT * HEAD_WIDTH
OFF_V = OFF_K + KVHEADS * HEAD_WIDTH
OFF_R = OFF_V + KVHEADS * HEAD_WIDTH
F32 = jnp.float32
BF16 = jnp.bfloat16


def dot_nn(left, right):
    return jnp.dot(left.astype(BF16), right.astype(BF16), preferred_element_type=F32)


def dot_nt(left, right):
    return lax.dot_general(
        left.astype(BF16), right.astype(BF16), (((1,), (1,)), ((), ())), preferred_element_type=F32
    )


def dot_tn(left, right):
    return lax.dot_general(
        left.astype(BF16), right.astype(BF16), (((0,), (0,)), ((), ())), preferred_element_type=F32
    )


def exact_dot(left, right):
    return jnp.dot(left, right, precision=lax.Precision.HIGHEST, preferred_element_type=F32)


def iota(shape, dim):
    return lax.broadcasted_iota(jnp.int32, shape, dim)


def block_masks(segc, segr):
    rows, cols = iota((T, T), 0), iota((T, T), 1)
    allowed = (segc[:, :T] == segr[0:1, :]) & (rows >= cols)
    places = iota((T, 128), 0)
    links = [
        jnp.where((pltpu.roll(segc, j, 0) == segc) & (places >= j), 1.0, 0.0)
        for j in range(1, CONV)
    ]
    return allowed, links


def convolve(p_ref, conv_ref, links, mixed_ref, act_ref):
    for at in range(0, CH, 128):
        sl = slice(at, at + 128)
        c = p_ref[0, :, SSM + at : SSM + at + 128]
        mixed = conv_ref[4:5, sl] + c * conv_ref[0:1, sl]
        for j in range(1, CONV):
            mixed = mixed + links[j - 1] * pltpu.roll(c, j, 0) * conv_ref[j : j + 1, sl]
        if mixed_ref is not None:
            mixed_ref[:, sl] = mixed
        act_ref[:, sl] = mixed * jax.nn.sigmoid(mixed)


def softplus(v):
    return jnp.maximum(v, 0.0) + jnp.log1p(jnp.exp(-jnp.abs(v)))


def steps_and_sums(p_ref, head_ref):
    raw = p_ref[0, :, OFF_R:PAD] + head_ref[0:1, :]
    live = iota((T, 128), 1) < MHEADS
    raw = jnp.where(live, raw, 0.0)
    dt = softplus(raw)
    decay = -dt * jnp.exp(head_ref[1:2, :])
    lower = jnp.where(iota((T, T), 0) >= iota((T, T), 1), 1.0, 0.0)
    return raw, dt, decay, exact_dot(lower, decay)


def stacked(tile, left):
    return jnp.concatenate([jnp.where(left, tile, 0.0), jnp.where(left, 0.0, tile)], 0).astype(BF16)


def picked(tiles, left):
    return jnp.where(left, tiles[:T], tiles[T:])


def attention_probs(q_stack, k_dup, both_allowed):
    scores = dot_nt(q_stack, k_dup) * (1.0 / math.sqrt(HEAD_WIDTH))
    scores = jnp.where(both_allowed, scores, -1e30)
    e = jnp.exp(scores - jnp.max(scores, -1, keepdims=True))
    return e / jnp.sum(e, -1, keepdims=True)


def doubled(tile, left):
    turned = pltpu.roll(tile, HEAD_WIDTH, 1)
    return jnp.where(left, tile, turned), jnp.where(left, turned, tile)


def mix_forward_kernel(p_ref, segc_ref, segr_ref, conv_ref, head_ref, skip_ref, u_ref, act_ref):
    allowed, links = block_masks(segc_ref[0], segr_ref[0])
    convolve(p_ref, conv_ref, links, None, act_ref)
    _, dt, _, cum = steps_and_sums(p_ref, head_ref)
    dt_t, cum_t = dt.T, cum.T
    left = iota((T, 128), 1) < HEAD_WIDTH
    cb = dot_nt(act_ref[:, SSM + STATE :], act_ref[:, SSM : SSM + STATE])
    for pair in range(MHEADS // 2):
        sl = slice(128 * pair, 128 * pair + 128)
        xs = act_ref[:, sl]
        parts = []
        for h in (2 * pair, 2 * pair + 1):
            decayed = jnp.exp(jnp.where(allowed, cum[:, h : h + 1] - cum_t[h : h + 1, :], -1e30))
            parts.append((decayed * cb * dt_t[h : h + 1, :]).astype(BF16))
        y = picked(dot_nn(jnp.concatenate(parts, 0), xs), left) + skip_ref[0:1, sl] * xs
        z = p_ref[0, :, sl]
        u_ref[0, :, sl] = (y * (z * jax.nn.sigmoid(z))).astype(BF16)
    k_dups = [tile.astype(BF16) for tile in doubled(p_ref[0, :, OFF_K:OFF_V], left)]
    v_dups = [tile.astype(BF16) for tile in doubled(p_ref[0, :, OFF_V:OFF_R], left)]
    places = iota((2 * T, T), 0)
    marks = jnp.concatenate([segc_ref[0], segc_ref[0]], 0)[:, :T]
    both_allowed = (marks == segr_ref[0][0:1, :]) & (
        jnp.where(places >= T, places - T, places) >= iota((2 * T, T), 1)
    )
    for pair in range(QUERY_HEAD_COUNT // 2):
        kv = pair // 2
        q_tile = p_ref[0, :, OFF_Q + 128 * pair : OFF_Q + 128 * pair + 128]
        probs = attention_probs(stacked(q_tile, left), k_dups[kv], both_allowed)
        u_ref[0, :, SSM + 128 * pair : SSM + 128 * pair + 128] = picked(
            dot_nn(probs, v_dups[kv]), left
        ).astype(BF16)


def mix_backward_kernel(
    p_ref, gu_ref, segc_ref, segr_ref, conv_ref, head_ref, skip_ref,
    gp_ref, gconv_ref, ghead_ref, gskip_ref,
    mixed_ref, act_ref, gact_ref, colq_ref,
):
    allowed, links = block_masks(segc_ref[0], segr_ref[0])
    convolve(p_ref, conv_ref, links, mixed_ref, act_ref)
    raw, dt, decay, cum = steps_and_sums(p_ref, head_ref)
    dt_t, cum_t = dt.T, cum.T
    lanes = iota((T, 128), 1)
    left = lanes < HEAD_WIDTH
    b_rows = act_ref[:, SSM : SSM + STATE]
    c_rows = act_ref[:, SSM + STATE :]
    cb = dot_nt(c_rows, b_rows)
    gcb = jnp.zeros((T, T), F32)
    row_form = jnp.zeros((T, 128), F32)
    colq_ref[...] = jnp.zeros_like(colq_ref)
    for pair in range(MHEADS // 2):
        sl = slice(128 * pair, 128 * pair + 128)
        xs = act_ref[:, sl]
        xs16 = xs.astype(BF16)
        z = p_ref[0, :, sl]
        gm = gu_ref[0, :, sl]
        sg = jax.nn.sigmoid(z)
        gy = gm * (z * sg)
        gy_stack = stacked(gy, left)
        gks = dot_nt(gy_stack, xs16)
        parts = []
        for side, h in enumerate((2 * pair, 2 * pair + 1)):
            decayed = jnp.exp(jnp.where(allowed, cum[:, h : h + 1] - cum_t[h : h + 1, :], -1e30))
            dt_row = dt_t[h : h + 1, :]
            base = decayed * cb
            parts.append((base * dt_row).astype(BF16))
            gk = gks[side * T : side * T + T]
            gcb = gcb + gk * (decayed * dt_row)
            q = gk * base
            colq_ref[h : h + 1, :] = jnp.sum(q, 0, keepdims=True)
            row_form = jnp.where(lanes == h, jnp.sum(q * dt_row, 1, keepdims=True), row_form)
        skip = skip_ref[0:1, sl]
        kernels = jnp.concatenate(parts, 0)
        y = picked(dot_nn(kernels, xs16), left) + skip * xs
        gp_ref[0, :, sl] = (gm * y * (sg * (1.0 + z * (1.0 - sg)))).astype(BF16)
        gact_ref[:, sl] = dot_tn(kernels, gy_stack) + skip * gy
        gskip_ref[0, 0:1, sl] = jnp.sum(gy * xs, 0, keepdims=True)
    gact_ref[:, SSM : SSM + STATE] = dot_tn(gcb, c_rows)
    gact_ref[:, SSM + STATE :] = dot_nn(gcb, b_rows)
    col_form = colq_ref[...].T
    gcum = row_form - col_form * dt
    upper = jnp.where(iota((T, T), 0) <= iota((T, T), 1), 1.0, 0.0)
    gdecay = exact_dot(upper, gcum)
    gdt = col_form - gdecay * jnp.exp(head_ref[1:2, :])
    graw = jnp.where(lanes < MHEADS, gdt * jax.nn.sigmoid(raw), 0.0)
    gp_ref[0, :, OFF_R:PAD] = graw.astype(BF16)
    ghead_ref[0, 0:1, :] = jnp.sum(graw, 0, keepdims=True)
    ghead_ref[0, 1:2, :] = jnp.sum(gdecay * decay, 0, keepdims=True)
    for at in range(0, CH, 128):
        sl = slice(at, at + 128)
        mixed = mixed_ref[:, sl]
        sg = jax.nn.sigmoid(mixed)
        gmix = gact_ref[:, sl] * (sg * (1.0 + mixed * (1.0 - sg)))
        c = p_ref[0, :, SSM + at : SSM + at + 128]
        gc = gmix * conv_ref[0:1, sl]
        gconv_ref[0, 0:1, sl] = jnp.sum(gmix * c, 0, keepdims=True)
        for j in range(1, CONV):
            linked = gmix * links[j - 1]
            gc = gc + pltpu.roll(linked, T - j, 0) * conv_ref[j : j + 1, sl]
            gconv_ref[0, j : j + 1, sl] = jnp.sum(linked * pltpu.roll(c, j, 0), 0, keepdims=True)
        gconv_ref[0, 4:5, sl] = jnp.sum(gmix, 0, keepdims=True)
        gconv_ref[0, 5:8, sl] = jnp.zeros((3, 128), F32)
        gp_ref[0, :, SSM + at : SSM + at + 128] = gc.astype(BF16)
    k_dups = [tile.astype(BF16) for tile in doubled(p_ref[0, :, OFF_K:OFF_V], left)]
    v_dups = [tile.astype(BF16) for tile in doubled(p_ref[0, :, OFF_V:OFF_R], left)]
    places = iota((2 * T, T), 0)
    marks = jnp.concatenate([segc_ref[0], segc_ref[0]], 0)[:, :T]
    both_allowed = (marks == segr_ref[0][0:1, :]) & (
        jnp.where(places >= T, places - T, places) >= iota((2 * T, T), 1)
    )
    gks, gvs = [], []
    for kv in range(KVHEADS):
        gk_sum = jnp.zeros((T, 128), F32)
        gv_sum = jnp.zeros((T, 128), F32)
        for pair in (2 * kv, 2 * kv + 1):
            sl = slice(OFF_Q + 128 * pair, OFF_Q + 128 * pair + 128)
            q_tile = p_ref[0, :, sl]
            go = gu_ref[0, :, SSM + 128 * pair : SSM + 128 * pair + 128]
            q_stack, go_stack = stacked(q_tile, left), stacked(go, left)
            probs = attention_probs(q_stack, k_dups[kv], both_allowed)
            gpr = dot_nt(go_stack, v_dups[kv])
            gs = probs * (gpr - jnp.sum(gpr * probs, -1, keepdims=True))
            gs = (gs * (1.0 / math.sqrt(HEAD_WIDTH))).astype(BF16)
            gp_ref[0, :, sl] = picked(dot_nn(gs, k_dups[kv]), left).astype(BF16)
            gk_sum = gk_sum + dot_tn(gs, q_stack)
            gv_sum = gv_sum + dot_tn(probs, go_stack)
        gks.append(gk_sum + pltpu.roll(gk_sum, HEAD_WIDTH, 1))
        gvs.append(gv_sum + pltpu.roll(gv_sum, HEAD_WIDTH, 1))
    gp_ref[0, :, OFF_K:OFF_V] = jnp.where(left, gks[0], gks[1]).astype(BF16)
    gp_ref[0, :, OFF_V:OFF_R] = jnp.where(left, gvs[0], gvs[1]).astype(BF16)


def whole(shape):
    return pl.BlockSpec(shape, lambda m: (0,) * len(shape))


def per_block(shape):
    return pl.BlockSpec((1, *shape), lambda m: (m,) + (0,) * len(shape))


def small_specs():
    return [
        per_block((T, 128)), per_block((8, T)), whole((8, CH)), whole((8, 128)), whole((8, SSM)),
    ]


def mix_forward(projected, tables):
    blocks = projected.shape[0]
    return pl.pallas_call(
        mix_forward_kernel,
        grid=(blocks,),
        in_specs=[per_block((T, PAD)), *small_specs()],
        out_specs=per_block((T, UW)),
        out_shape=jax.ShapeDtypeStruct((blocks, T, UW), BF16),
        scratch_shapes=[pltpu.VMEM((T, CH), F32)],
        compiler_params=pltpu.CompilerParams(vmem_limit_bytes=32 * 1024 * 1024),
        name="mix_forward",
    )(projected, *tables)


def mix_backward(projected, grad_joined, tables):
    blocks = projected.shape[0]
    return pl.pallas_call(
        mix_backward_kernel,
        grid=(blocks,),
        in_specs=[per_block((T, PAD)), per_block((T, UW)), *small_specs()],
        out_specs=[per_block((T, PAD)), per_block((8, CH)), per_block((8, 128)), per_block((8, SSM))],
        out_shape=[
            jax.ShapeDtypeStruct((blocks, T, PAD), BF16),
            jax.ShapeDtypeStruct((blocks, 8, CH), F32),
            jax.ShapeDtypeStruct((blocks, 8, 128), F32),
            jax.ShapeDtypeStruct((blocks, 8, SSM), F32),
        ],
        scratch_shapes=[
            pltpu.VMEM((T, CH), F32),
            pltpu.VMEM((T, CH), F32),
            pltpu.VMEM((T, CH), F32),
            pltpu.VMEM((128, T), F32),
        ],
        compiler_params=pltpu.CompilerParams(vmem_limit_bytes=40 * 1024 * 1024),
        name="mix_backward",
    )(projected, grad_joined, *tables)


def mixer_tables(segments, conv_rows, head_table):
    blocks = segments.shape[0]
    marks = segments.astype(F32)
    segc = jnp.broadcast_to(marks[:, :, None], (blocks, T, 128))
    segr = jnp.broadcast_to(marks[:, None, :], (blocks, 8, T))
    conv_rows = jnp.pad(conv_rows, ((0, 3), (0, 0)))
    head_rows = jnp.pad(head_table.T, ((0, 5), (0, 128 - MHEADS)))
    skip_rows = jnp.broadcast_to(jnp.repeat(head_table[:, 2], HEAD_WIDTH)[None], (8, SSM))
    return segc, segr, conv_rows, head_rows, skip_rows


MESH = pl.DeviceIdType.MESH
HOPS = ("xa", "xb", "za", "zb", "y")
ORDERS = (
    ("xa", "xb", "zb", "za", "y"),
    ("xb", "xa", "y", "zb", "za"),
    ("za", "zb", "xa", "y", "xb"),
    ("zb", "y", "za", "xb", "xa"),
    ("y", "za", "xb", "xa", "zb"),
)


def cut(array, tiles, orders=(0, 1, 2, 3, 4), first=0):
    parts = []
    for width, order in zip(tiles, orders):
        parts.append((array, 128 * first, 128 * width, ORDERS[order]))
        first += width
    return parts


GATHERED = (
    *cut(0, (7, 7, 7, 6, 5)),
    *cut(0, (1,), (4,), 32),
    *cut(1, (2, 3, 3), (2, 3, 4)),
    *cut(2, (7, 7, 6, 6, 6)),
    *cut(3, (3, 3, 2)),
)
SCATTERED = (
    *cut(3, (3, 3, 2)),
    *cut(1, (2, 3, 3), (2, 3, 4)),
    *cut(2, (7, 7, 6, 6, 6)),
    *cut(0, (7, 7, 7, 6, 6)),
    *cut(0, (1,), (4,), 33),
)
TAIL = 2 * FF
EXTRA = PAD
SHARD_ROWS = (64, 128, 64, 128)
SHARD_COLS = (PAD, 1024, 2 * FF, 1024)
SUM_COLS = (PAD + 128, 1024, 2 * FF, 1024)


def pair_a(i):
    return i + 1 - 2 * (i % 2)


def pair_b(i):
    return (i + 2 * (i % 2) + 3) % 4


def place():
    shard = lax.axis_index("shard")
    return lax.axis_index("section"), shard // 8, (shard // 2) % 4, shard % 2, lax.axis_index("rep")


def neighbours(section, y, z, core, x):
    def at(y, z, core, x):
        return (section, y * 8 + z * 2 + core, x)

    return {
        "core": at(y, z, 1 - core, x),
        "xa": at(y, z, core, pair_a(x)),
        "xb": at(y, z, core, pair_b(x)),
        "za": at(y, pair_a(z), core, x),
        "zb": at(y, pair_b(z), core, x),
        "y": at(1 - y, z, core, x),
        "xo": at(y, z, core, (x + 2) % 4),
    }


def meet(devices):
    barrier = pltpu.get_barrier_semaphore()
    for device in devices:
        pl.semaphore_signal(barrier, inc=1, device_id=device, device_id_type=MESH)
    pl.semaphore_wait(barrier, len(devices))


def halve(kept, hop, me):
    near, other = (pair_a, pair_b) if hop == "a" else (pair_b, pair_a)
    if kept[0][1] != 4:
        return [(near(me), 1)], [(me, 1)]
    if hop == "b":
        return [(2 * (near(me) // 2), 2)], [(2 * (me // 2), 2)]
    return [(near(me), 1), (other(near(me)), 1)], [(me, 1), (other(me), 1)]


def schedule(order, me_y, me_z, me_x):
    ys, zs, xs = [(0, 2)], [(0, 4)], [(0, 4)]
    stages = []
    for hop in order:
        if hop == "y":
            sent, ys = [(1 - me_y, 1)], [(me_y, 1)]
            gone = sent, zs, xs
        elif hop[0] == "z":
            sent, zs = halve(zs, hop[1], me_z)
            gone = ys, sent, xs
        else:
            sent, xs = halve(xs, hop[1], me_x)
            gone = ys, zs, sent
        stages.append((list(itertools.product(*gone)), list(itertools.product(ys, zs, xs))))
    return stages


def window(piece, quarter, column, columns):
    (y, ny), (z, nz), (x, nx) = piece
    rows = 0 if nx == 4 else pl.multiple_of(x * quarter, nx * quarter)
    return pl.ds(y, ny), pl.ds(z, nz), pl.ds(rows, nx * quarter), pl.ds(column, columns)


def piece_dims(piece, quarter):
    (_, ny), (_, nz), (_, nx) = piece
    return ny, nz, nx * quarter


def stage_shapes(parts):
    shapes = []
    for array, column, columns, order in parts:
        for sent, _ in schedule(order, 0, 0, 0):
            dims = piece_dims(sent[0], SHARD_ROWS[array] // 4)
            shapes.append((len(sent), *dims, columns))
    return shapes


def add_into(acc, window_at, arrived):
    ny, nz, rows, _ = arrived.shape
    ys, zs, rs, cs = window_at

    def step(i, carry):
        y, z = i // nz, i % nz
        at = (ys.start + y, zs.start + z, rs, cs)
        acc[at] = acc[at] + arrived[y, z]
        return carry

    if ny * nz == 1:
        step(0, 0)
    else:
        lax.fori_loop(0, ny * nz, step, 0)


def scatter_kernel(*refs):
    grads, extra, wholes, smalls = refs[:4], refs[4], refs[5:9], refs[9:12]
    accs, cores = refs[12:16], refs[16 : 16 + len(SCATTERED)]
    arrivals = refs[16 + len(SCATTERED) : -7]
    local_sem, core_send, core_recv, send_sem, recv_sem, last_send, last_recv = refs[-7:]
    section, y, z, core, x = place()
    near = neighbours(section, y, z, core, x)
    meet([near[name] for name in ("core", *HOPS, "xo")])

    loads, swaps = [], []
    for p, (array, column, columns, _) in enumerate(SCATTERED):
        cols = pl.ds(column, columns)
        grad = extra if (array, column) == (0, EXTRA) else grads[array].at[:, :, :, :, cols]
        swap = pltpu.make_async_remote_copy(
            src_ref=grad.at[:, :, 1 - core],
            dst_ref=cores[p],
            send_sem=core_send.at[p],
            recv_sem=core_recv.at[p],
            device_id=near["core"],
            device_id_type=MESH,
        )
        swap.start()
        load = pltpu.make_async_copy(
            grad.at[:, :, core], accs[array].at[:, :, :, cols], local_sem.at[p]
        )
        load.start()
        swaps.append(swap)
        loads.append(load)

    plans = [schedule(order, y, z, x) for _, _, _, order in SCATTERED]
    flying = {}
    sems = 0
    for stage in range(len(HOPS) + 1):
        for p, (array, column, columns, order) in enumerate(SCATTERED):
            quarter = SHARD_ROWS[array] // 4
            if stage == 0:
                loads[p].wait()
                swaps[p].wait_recv()
                add_into(accs[array], window(((0, 2), (0, 4), (0, 4)), quarter, column, columns), cores[p])
            else:
                kept = plans[p][stage - 1][1]
                for k, (copy, piece) in enumerate(zip(flying[p, stage - 1], kept)):
                    copy.wait_recv()
                    add_into(
                        accs[array],
                        window(piece, quarter, column, columns),
                        arrivals[p * len(HOPS) + stage - 1].at[k],
                    )
            if stage < len(HOPS):
                copies = []
                for k, piece in enumerate(plans[p][stage][0]):
                    copy = pltpu.make_async_remote_copy(
                        src_ref=accs[array].at[window(piece, quarter, column, columns)],
                        dst_ref=arrivals[p * len(HOPS) + stage].at[k],
                        send_sem=send_sem.at[sems],
                        recv_sem=recv_sem.at[sems],
                        device_id=near[order[stage]],
                        device_id_type=MESH,
                    )
                    copy.start()
                    copies.append(copy)
                    sems += 1
                flying[p, stage] = copies

    last = []
    for array in range(4):
        quarter = SHARD_ROWS[array] // 4
        mine = pl.ds(pl.multiple_of(x * quarter, quarter), quarter)
        for k, name in enumerate(("xo", "xa", "xb")):
            copy = pltpu.make_async_remote_copy(
                src_ref=accs[array].at[y, z, mine],
                dst_ref=wholes[array].at[mine],
                send_sem=last_send.at[array, k],
                recv_sem=last_recv.at[array, k],
                device_id=near[name],
                device_id_type=MESH,
            )
            copy.start()
            last.append(copy)
        wholes[array][mine, :] = accs[array][y, z, mine, :]
    for copy in last:
        copy.wait_recv()
    small = wholes[0][:, EXTRA:].astype(F32)
    out_gains, out_conv, out_head = smalls
    out_conv[:, :56] = small[: CONV + 1, :56]
    out_conv[:, 56:] = small[8 : 9 + CONV, :56]
    out_gains[...] = small[16:18, :64]
    out_head[...] = small[24:27, :MHEADS]
    for copy in last + swaps + [c for copies in flying.values() for c in copies]:
        copy.wait_send()


def scatter_sums(grads, extra):
    n_copies = sum(shape[0] for shape in stage_shapes(SCATTERED))
    n_parts = len(SCATTERED)
    out_shapes = [
        *[jax.ShapeDtypeStruct(s, BF16) for s in zip(SHARD_ROWS, SUM_COLS)],
        *[jax.ShapeDtypeStruct(s, F32) for s in ((2, 64), (CONV + 1, T), (3, MHEADS))],
    ]
    return pl.pallas_call(
        scatter_kernel,
        in_specs=[pl.BlockSpec(memory_space=pl.ANY)] * 5,
        out_specs=[pl.BlockSpec(memory_space=pltpu.VMEM)] * 7,
        out_shape=out_shapes,
        scratch_shapes=[
            *[pltpu.VMEM((2, 4, r, c), BF16) for r, c in zip(SHARD_ROWS, SUM_COLS)],
            *[pltpu.VMEM((2, 4, SHARD_ROWS[a], cols), BF16) for a, _, cols, _ in SCATTERED],
            *[pltpu.VMEM(shape, BF16) for shape in stage_shapes(SCATTERED)],
            pltpu.SemaphoreType.DMA((n_parts,)),
            pltpu.SemaphoreType.DMA((n_parts,)),
            pltpu.SemaphoreType.DMA((n_parts,)),
            pltpu.SemaphoreType.DMA((n_copies,)),
            pltpu.SemaphoreType.DMA((n_copies,)),
            pltpu.SemaphoreType.DMA((4, 3)),
            pltpu.SemaphoreType.DMA((4, 3)),
        ],
        compiler_params=pltpu.CompilerParams(
            collective_id=1, has_side_effects=True, vmem_limit_bytes=58 * 1024 * 1024
        ),
        name="scatter_sums",
    )(*grads, extra)


def gather_kernel(*refs):
    shards, tail, outs = refs[:4], refs[4], refs[5:9]
    local_sem, send_sem, recv_sem, core_send, core_recv = refs[9:]
    section, y, z, core, x = place()
    near = neighbours(section, y, z, core, x)
    meet([near[name] for name in ("core", *HOPS)])

    def at(array, piece, column, columns):
        ys, zs, rows, cols = window(piece, SHARD_ROWS[array] // 4, column, columns)
        return outs[array].at[ys, zs, pl.ds(core, 1), rows, cols]

    def own(array, column, columns):
        quarter = SHARD_ROWS[array] // 4
        rows = pl.ds(pl.multiple_of(x * quarter, quarter), quarter)
        if (array, column) == (0, TAIL):
            return tail.at[:, :, :, rows]
        return shards[array].at[:, :, :, rows, pl.ds(column, columns)]

    passed = []

    def pass_on(source, target):
        k = len(passed)
        copy = pltpu.make_async_remote_copy(
            src_ref=source,
            dst_ref=target,
            send_sem=core_send.at[k],
            recv_sem=core_recv.at[k],
            device_id=near["core"],
            device_id_type=MESH,
        )
        copy.start()
        passed.append(copy)

    locals_ = []
    for p, (array, column, columns, _) in enumerate(GATHERED):
        copy = pltpu.make_async_copy(
            own(array, column, columns), at(array, ((y, 1), (z, 1), (x, 1)), column, columns), local_sem.at[p]
        )
        copy.start()
        locals_.append(copy)

    plans = [schedule(order, y, z, x)[::-1] for _, _, _, order in GATHERED]
    flying, sent = {}, []
    for stage in range(len(HOPS) + 1):
        for p, (array, column, columns, order) in enumerate(GATHERED):
            if stage:
                for copy in flying[p, stage - 1]:
                    copy.wait_recv()
            if stage == 1:
                locals_[p].wait()
            if stage < len(HOPS):
                copies = []
                for piece in plans[p][stage][1]:
                    target = at(array, piece, column, columns)
                    copy = pltpu.make_async_remote_copy(
                        src_ref=target if stage else own(array, column, columns),
                        dst_ref=target,
                        send_sem=send_sem.at[len(sent)],
                        recv_sem=recv_sem.at[len(sent)],
                        device_id=near[order[::-1][stage]],
                        device_id_type=MESH,
                    )
                    copy.start()
                    copies.append(copy)
                    sent.append(copy)
                flying[p, stage] = copies
            if stage:
                for piece in plans[p][stage - 1][0]:
                    here = at(array, piece, column, columns)
                    pass_on(here, here)
            else:
                pass_on(own(array, column, columns), at(array, ((y, 1), (z, 1), (x, 1)), column, columns))
    for copy in passed:
        copy.wait()
    for copy in sent:
        copy.wait_send()


def gather_shards(shards, tail):
    n_copies = sum(shape[0] for shape in stage_shapes(GATHERED))
    n_passed = n_copies + len(GATHERED)
    return pl.pallas_call(
        gather_kernel,
        in_specs=[pl.BlockSpec(memory_space=pl.ANY)] * 5,
        out_specs=[pl.BlockSpec(memory_space=pl.ANY)] * 4,
        out_shape=[
            jax.ShapeDtypeStruct((2, 4, 2, r, c), BF16) for r, c in zip(SHARD_ROWS, SHARD_COLS)
        ],
        scratch_shapes=[
            pltpu.SemaphoreType.DMA((len(GATHERED),)),
            pltpu.SemaphoreType.DMA((n_copies,)),
            pltpu.SemaphoreType.DMA((n_copies,)),
            pltpu.SemaphoreType.DMA((n_passed,)),
            pltpu.SemaphoreType.DMA((n_passed,)),
        ],
        compiler_params=pltpu.CompilerParams(collective_id=2, has_side_effects=True),
        name="gather_shards",
    )(*shards, tail)


def rms_norm(values, gain):
    return values * lax.rsqrt(jnp.mean(values * values, -1, keepdims=True) + 1e-05) * gain


def rms_back(values, gain, grad):
    scale = lax.rsqrt(jnp.mean(values * values, -1, keepdims=True) + 1e-05)
    unit = values * scale
    scaled = grad * gain
    grad_values = scale * (scaled - unit * jnp.mean(scaled * unit, -1, keepdims=True))
    return grad_values, jnp.sum(grad * unit, 0)


def forward_product(left, weight):
    return jnp.dot(left, weight, preferred_element_type=F32)


def back_product(grad_rows, weight):
    return lax.dot_general(
        grad_rows, weight, (((1,), (1,)), ((), ())), preferred_element_type=F32
    )


def outer_sum(left, right):
    return lax.dot_general(
        left, right, (((0,), (0,)), ((), ())), preferred_element_type=F32
    ).astype(BF16)


def layer_forward(inputs, weights, tables):
    gains, w_in, w_out, w_gate_up, w_down = weights
    blocks = inputs.shape[0] // T
    normed = rms_norm(inputs, gains[0]).astype(BF16)
    projected = forward_product(normed, w_in)
    joined = mix_forward(projected.reshape(blocks, T, PAD), tables).reshape(blocks * T, UW)
    hidden = inputs + forward_product(joined, w_out)
    normed_two = rms_norm(hidden, gains[1]).astype(BF16)
    gate_up = forward_product(normed_two, w_gate_up)
    activated = (jax.nn.silu(gate_up[:, :FF]) * gate_up[:, FF:]).astype(BF16)
    result = hidden + forward_product(activated, w_down)
    return result, (inputs, normed, projected, joined, hidden, normed_two, gate_up, activated)


def layer_backward(grad_out, saved, weights, tables):
    gains, w_in, w_out, w_gate_up, w_down = weights
    inputs, normed, projected, joined, hidden, normed_two, gate_up, activated = saved
    blocks = inputs.shape[0] // T
    grad_ffn = grad_out.astype(BF16)
    grad_act = back_product(grad_ffn, w_down)
    gate, up = gate_up[:, :FF], gate_up[:, FF:]
    sig = jax.nn.sigmoid(gate)
    grad_gate = (grad_act * up * (sig * (1.0 + gate * (1.0 - sig)))).astype(BF16)
    grad_up = (grad_act * (gate * sig)).astype(BF16)
    grad_gate_up = jnp.concatenate([grad_gate, grad_up], 1)
    grad_hidden, grad_gain_two = rms_back(hidden, gains[1], back_product(grad_gate_up, w_gate_up))
    grad_hidden = grad_out + grad_hidden
    grad_branch = grad_hidden.astype(BF16)
    grad_joined = back_product(grad_branch, w_out)
    grad_proj, grad_conv, grad_head, grad_skip = mix_backward(
        projected.reshape(blocks, T, PAD), grad_joined.reshape(blocks, T, UW), tables
    )
    grad_proj = grad_proj.reshape(blocks * T, PAD)
    grad_input, grad_gain_one = rms_back(inputs, gains[0], back_product(grad_proj, w_in))
    grad_input = grad_hidden + grad_input
    pairs = (
        (normed, grad_proj),
        (joined, grad_branch),
        (normed_two, grad_gate_up),
        (activated, grad_ffn),
    )
    return grad_input, pairs, (grad_gain_one, grad_gain_two, grad_conv, grad_head, grad_skip)


def across(array, by):
    return lax.ppermute(array, "section", [(0, 1)] if by > 0 else [(1, 0)])


def gather_weights(norm_gains, w_in, conv_params, w_out, w_gate_up, w_down):
    rows = w_in.shape[0]
    conv_rows = conv_params.T
    small = jnp.concatenate(
        [
            jnp.pad(conv_rows[:, :56], ((0, 3), (0, 8))),
            jnp.pad(conv_rows[:, 56:], ((0, 3), (0, 8))),
            norm_gains.T,
        ],
        0,
    )
    small = jnp.pad(small, ((0, rows - small.shape[0]), (0, PAD - PIN - 64)))
    tail = jnp.concatenate([w_in[:, TAIL:], small], 1)
    parts = gather_shards(
        [a.reshape(1, 1, 1, *a.shape) for a in (w_in, w_out, w_gate_up, w_down)],
        tail.reshape(1, 1, 1, *tail.shape),
    )
    small = parts[0][..., PIN : PIN + 64].reshape(-1, rows, 64)[:, :18].astype(F32)
    gains = small[:, 16:18].transpose(1, 0, 2).reshape(2, -1)
    conv_rows = small[:, :16, :56].reshape(-1, 2, 8, 56)[:, :, : CONV + 1]
    conv_rows = conv_rows.transpose(2, 0, 1, 3).reshape(CONV + 1, -1)
    return (gains, *[a.reshape(-1, a.shape[-1]) for a in parts]), conv_rows


def body(
    tokens,
    segment_ids,
    cotangent,
    norm_gains,
    w_in,
    conv_params,
    head_params,
    w_out,
    w_gate_up,
    w_down,
):
    section = lax.axis_index("section")
    blocks, _, width = tokens.shape
    rows = blocks * T
    weights, conv_rows = gather_weights(
        norm_gains[0], w_in[0], conv_params[0], w_out[0], w_gate_up[0], w_down[0]
    )
    tables = mixer_tables(segment_ids[:, 0], conv_rows, head_params[0].astype(F32))

    own = tokens.reshape(rows, width)
    first, _ = layer_forward(own.astype(F32), weights, tables)
    received = across(first.astype(BF16), 1)
    inputs = jnp.where(section == 0, own, received).astype(F32)
    result, saved = layer_forward(inputs, weights, tables)

    top = cotangent.reshape(rows, width)
    first_grad, _, _ = layer_backward(top.astype(F32), saved, weights, tables)
    coming = across(first_grad.astype(BF16), -1)
    grad_out = jnp.where(section == 1, top, coming).astype(F32)
    grad_input, pairs, smalls = layer_backward(grad_out, saved, weights, tables)

    grad_gain_one, grad_gain_two, grad_conv, grad_head, grad_skip = smalls
    sums = [outer_sum(left, right) for left, right in pairs]
    shards = lax.axis_size("shard")
    gains = jnp.stack([grad_gain_one, grad_gain_two]).reshape(2, shards, 64).transpose(1, 0, 2)
    conv = jnp.sum(grad_conv, 0).reshape(8, shards, 2, 56).transpose(1, 2, 0, 3)
    conv = conv.reshape(shards, 16, 56)
    skip = jnp.sum(jnp.sum(grad_skip, 0)[0].reshape(MHEADS, HEAD_WIDTH), 1)
    head = jnp.concatenate([jnp.sum(grad_head, 0)[:2, :MHEADS], skip[None]], 0)
    head = jnp.broadcast_to(head[None], (shards, 3, MHEADS))
    extra = jnp.concatenate(
        [
            jnp.pad(conv, ((0, 0), (0, 0), (0, 72))),
            jnp.pad(gains, ((0, 0), (0, 6), (0, 64))),
            jnp.pad(head, ((0, 0), (0, 37), (0, 128 - MHEADS))),
        ],
        1,
    ).astype(BF16)
    out_in, out_out, out_gu, out_dn, out_gains, out_conv, out_head = scatter_sums(
        [g.reshape(2, 4, 2, g.shape[0] // 16, g.shape[1]) for g in sums],
        extra.reshape(2, 4, 2, 64, 128),
    )
    return (
        result.astype(BF16).reshape(1, blocks, T, width),
        grad_input.reshape(1, blocks, T, width),
        out_gains.T[None],
        out_in[None, :, :PIN].astype(F32),
        out_conv.T[None],
        out_head.T[None],
        out_out[None].astype(F32),
        out_gu[None].astype(F32),
        out_dn[None].astype(F32),
    )


def solution(mesh):
    in_specs = (
        P(None, ("shard", "rep"), None),
        P(None, ("shard", "rep"), None),
        P(None, ("shard", "rep"), None),
        P("section", "shard", None),
        P("section", "shard", None),
        P("section", "shard", None),
        P("section", None, None),
        P("section", "shard", None),
        P("section", "shard", None),
        P("section", "shard", None),
    )
    out_specs = (
        P("section", None, ("shard", "rep"), None),
        P("section", None, ("shard", "rep"), None),
        P("section", "shard", None),
        P("section", "shard", None),
        P("section", "shard", None),
        P("section", None, None),
        P("section", "shard", None),
        P("section", "shard", None),
        P("section", "shard", None),
    )
    return jax.shard_map(body, mesh=mesh, in_specs=in_specs, out_specs=out_specs, check_vma=False)
```

```python
import itertools
import math

import jax
import jax.numpy as jnp
from jax import lax
from jax.experimental import pallas as pl
from jax.experimental.pallas import tpu as pltpu
from jax.sharding import PartitionSpec as P

FF = 2048
MHEADS = 24
HEAD_WIDTH = 64
STATE = 128
QUERY_HEAD_COUNT = 8
KVHEADS = 2
CONV = 4
SSM = 1536
CH = 1792
UW = 2048
PIN = 4120
PAD = 4224
T = 112
OFF_Q = SSM + CH
OFF_K = OFF_Q + QUERY_HEAD_COUNT * HEAD_WIDTH
OFF_V = OFF_K + KVHEADS * HEAD_WIDTH
OFF_R = OFF_V + KVHEADS * HEAD_WIDTH
F32 = jnp.float32
BF16 = jnp.bfloat16


def dot_nn(left, right):
    return jnp.dot(left.astype(BF16), right.astype(BF16), preferred_element_type=F32)


def dot_nt(left, right):
    return lax.dot_general(
        left.astype(BF16), right.astype(BF16), (((1,), (1,)), ((), ())), preferred_element_type=F32
    )


def dot_tn(left, right):
    return lax.dot_general(
        left.astype(BF16), right.astype(BF16), (((0,), (0,)), ((), ())), preferred_element_type=F32
    )


def exact_dot(left, right):
    return jnp.dot(left, right, precision=lax.Precision.HIGHEST, preferred_element_type=F32)


def iota(shape, dim):
    return lax.broadcasted_iota(jnp.int32, shape, dim)


def block_masks(segc, segr):
    rows, cols = iota((T, T), 0), iota((T, T), 1)
    allowed = (segc[:, :T] == segr[0:1, :]) & (rows >= cols)
    places = iota((T, 128), 0)
    links = [
        jnp.where((pltpu.roll(segc, j, 0) == segc) & (places >= j), 1.0, 0.0)
        for j in range(1, CONV)
    ]
    return allowed, links


def convolve(p_ref, conv_ref, links, mixed_ref, act_ref):
    for at in range(0, CH, 128):
        sl = slice(at, at + 128)
        c = p_ref[0, :, SSM + at : SSM + at + 128]
        mixed = conv_ref[4:5, sl] + c * conv_ref[0:1, sl]
        for j in range(1, CONV):
            mixed = mixed + links[j - 1] * pltpu.roll(c, j, 0) * conv_ref[j : j + 1, sl]
        if mixed_ref is not None:
            mixed_ref[:, sl] = mixed
        act_ref[:, sl] = mixed * jax.nn.sigmoid(mixed)


def softplus(v):
    return jnp.maximum(v, 0.0) + jnp.log1p(jnp.exp(-jnp.abs(v)))


def steps_and_sums(p_ref, head_ref):
    raw = p_ref[0, :, OFF_R:PAD] + head_ref[0:1, :]
    live = iota((T, 128), 1) < MHEADS
    raw = jnp.where(live, raw, 0.0)
    dt = softplus(raw)
    decay = -dt * jnp.exp(head_ref[1:2, :])
    lower = jnp.where(iota((T, T), 0) >= iota((T, T), 1), 1.0, 0.0)
    return raw, dt, decay, exact_dot(lower, decay)


def stacked(tile, left):
    return jnp.concatenate([jnp.where(left, tile, 0.0), jnp.where(left, 0.0, tile)], 0).astype(BF16)


def picked(tiles, left):
    return jnp.where(left, tiles[:T], tiles[T:])


def attention_probs(q_stack, k_dup, both_allowed):
    scores = dot_nt(q_stack, k_dup) * (1.0 / math.sqrt(HEAD_WIDTH))
    scores = jnp.where(both_allowed, scores, -1e30)
    e = jnp.exp(scores - jnp.max(scores, -1, keepdims=True))
    return e / jnp.sum(e, -1, keepdims=True)


def doubled(tile, left):
    turned = pltpu.roll(tile, HEAD_WIDTH, 1)
    return jnp.where(left, tile, turned), jnp.where(left, turned, tile)


def mix_forward_kernel(p_ref, segc_ref, segr_ref, conv_ref, head_ref, skip_ref, u_ref, act_ref):
    allowed, links = block_masks(segc_ref[0], segr_ref[0])
    convolve(p_ref, conv_ref, links, None, act_ref)
    _, dt, _, cum = steps_and_sums(p_ref, head_ref)
    dt_t, cum_t = dt.T, cum.T
    left = iota((T, 128), 1) < HEAD_WIDTH
    cb = dot_nt(act_ref[:, SSM + STATE :], act_ref[:, SSM : SSM + STATE])
    for pair in range(MHEADS // 2):
        sl = slice(128 * pair, 128 * pair + 128)
        xs = act_ref[:, sl]
        parts = []
        for h in (2 * pair, 2 * pair + 1):
            decayed = jnp.exp(jnp.where(allowed, cum[:, h : h + 1] - cum_t[h : h + 1, :], -1e30))
            parts.append((decayed * cb * dt_t[h : h + 1, :]).astype(BF16))
        y = picked(dot_nn(jnp.concatenate(parts, 0), xs), left) + skip_ref[0:1, sl] * xs
        z = p_ref[0, :, sl]
        u_ref[0, :, sl] = (y * (z * jax.nn.sigmoid(z))).astype(BF16)
    k_dups = [tile.astype(BF16) for tile in doubled(p_ref[0, :, OFF_K:OFF_V], left)]
    v_dups = [tile.astype(BF16) for tile in doubled(p_ref[0, :, OFF_V:OFF_R], left)]
    places = iota((2 * T, T), 0)
    marks = jnp.concatenate([segc_ref[0], segc_ref[0]], 0)[:, :T]
    both_allowed = (marks == segr_ref[0][0:1, :]) & (
        jnp.where(places >= T, places - T, places) >= iota((2 * T, T), 1)
    )
    for pair in range(QUERY_HEAD_COUNT // 2):
        kv = pair // 2
        q_tile = p_ref[0, :, OFF_Q + 128 * pair : OFF_Q + 128 * pair + 128]
        probs = attention_probs(stacked(q_tile, left), k_dups[kv], both_allowed)
        u_ref[0, :, SSM + 128 * pair : SSM + 128 * pair + 128] = picked(
            dot_nn(probs, v_dups[kv]), left
        ).astype(BF16)


def mix_backward_kernel(
    p_ref, gu_ref, segc_ref, segr_ref, conv_ref, head_ref, skip_ref,
    gp_ref, gconv_ref, ghead_ref, gskip_ref,
    mixed_ref, act_ref, gact_ref, colq_ref,
):
    allowed, links = block_masks(segc_ref[0], segr_ref[0])
    convolve(p_ref, conv_ref, links, mixed_ref, act_ref)
    raw, dt, decay, cum = steps_and_sums(p_ref, head_ref)
    dt_t, cum_t = dt.T, cum.T
    lanes = iota((T, 128), 1)
    left = lanes < HEAD_WIDTH
    b_rows = act_ref[:, SSM : SSM + STATE]
    c_rows = act_ref[:, SSM + STATE :]
    cb = dot_nt(c_rows, b_rows)
    gcb = jnp.zeros((T, T), F32)
    row_form = jnp.zeros((T, 128), F32)
    colq_ref[...] = jnp.zeros_like(colq_ref)
    for pair in range(MHEADS // 2):
        sl = slice(128 * pair, 128 * pair + 128)
        xs = act_ref[:, sl]
        xs16 = xs.astype(BF16)
        z = p_ref[0, :, sl]
        gm = gu_ref[0, :, sl]
        sg = jax.nn.sigmoid(z)
        gy = gm * (z * sg)
        gy_stack = stacked(gy, left)
        gks = dot_nt(gy_stack, xs16)
        parts = []
        for side, h in enumerate((2 * pair, 2 * pair + 1)):
            decayed = jnp.exp(jnp.where(allowed, cum[:, h : h + 1] - cum_t[h : h + 1, :], -1e30))
            dt_row = dt_t[h : h + 1, :]
            base = decayed * cb
            parts.append((base * dt_row).astype(BF16))
            gk = gks[side * T : side * T + T]
            gcb = gcb + gk * (decayed * dt_row)
            q = gk * base
            colq_ref[h : h + 1, :] = jnp.sum(q, 0, keepdims=True)
            row_form = jnp.where(lanes == h, jnp.sum(q * dt_row, 1, keepdims=True), row_form)
        skip = skip_ref[0:1, sl]
        kernels = jnp.concatenate(parts, 0)
        y = picked(dot_nn(kernels, xs16), left) + skip * xs
        gp_ref[0, :, sl] = (gm * y * (sg * (1.0 + z * (1.0 - sg)))).astype(BF16)
        gact_ref[:, sl] = dot_tn(kernels, gy_stack) + skip * gy
        gskip_ref[0, 0:1, sl] = jnp.sum(gy * xs, 0, keepdims=True)
    gact_ref[:, SSM : SSM + STATE] = dot_tn(gcb, c_rows)
    gact_ref[:, SSM + STATE :] = dot_nn(gcb, b_rows)
    col_form = colq_ref[...].T
    gcum = row_form - col_form * dt
    upper = jnp.where(iota((T, T), 0) <= iota((T, T), 1), 1.0, 0.0)
    gdecay = exact_dot(upper, gcum)
    gdt = col_form - gdecay * jnp.exp(head_ref[1:2, :])
    graw = jnp.where(lanes < MHEADS, gdt * jax.nn.sigmoid(raw), 0.0)
    gp_ref[0, :, OFF_R:PAD] = graw.astype(BF16)
    ghead_ref[0, 0:1, :] = jnp.sum(graw, 0, keepdims=True)
    ghead_ref[0, 1:2, :] = jnp.sum(gdecay * decay, 0, keepdims=True)
    for at in range(0, CH, 128):
        sl = slice(at, at + 128)
        mixed = mixed_ref[:, sl]
        sg = jax.nn.sigmoid(mixed)
        gmix = gact_ref[:, sl] * (sg * (1.0 + mixed * (1.0 - sg)))
        c = p_ref[0, :, SSM + at : SSM + at + 128]
        gc = gmix * conv_ref[0:1, sl]
        gconv_ref[0, 0:1, sl] = jnp.sum(gmix * c, 0, keepdims=True)
        for j in range(1, CONV):
            linked = gmix * links[j - 1]
            gc = gc + pltpu.roll(linked, T - j, 0) * conv_ref[j : j + 1, sl]
            gconv_ref[0, j : j + 1, sl] = jnp.sum(linked * pltpu.roll(c, j, 0), 0, keepdims=True)
        gconv_ref[0, 4:5, sl] = jnp.sum(gmix, 0, keepdims=True)
        gconv_ref[0, 5:8, sl] = jnp.zeros((3, 128), F32)
        gp_ref[0, :, SSM + at : SSM + at + 128] = gc.astype(BF16)
    k_dups = [tile.astype(BF16) for tile in doubled(p_ref[0, :, OFF_K:OFF_V], left)]
    v_dups = [tile.astype(BF16) for tile in doubled(p_ref[0, :, OFF_V:OFF_R], left)]
    places = iota((2 * T, T), 0)
    marks = jnp.concatenate([segc_ref[0], segc_ref[0]], 0)[:, :T]
    both_allowed = (marks == segr_ref[0][0:1, :]) & (
        jnp.where(places >= T, places - T, places) >= iota((2 * T, T), 1)
    )
    gks, gvs = [], []
    for kv in range(KVHEADS):
        gk_sum = jnp.zeros((T, 128), F32)
        gv_sum = jnp.zeros((T, 128), F32)
        for pair in (2 * kv, 2 * kv + 1):
            sl = slice(OFF_Q + 128 * pair, OFF_Q + 128 * pair + 128)
            q_tile = p_ref[0, :, sl]
            go = gu_ref[0, :, SSM + 128 * pair : SSM + 128 * pair + 128]
            q_stack, go_stack = stacked(q_tile, left), stacked(go, left)
            probs = attention_probs(q_stack, k_dups[kv], both_allowed)
            gpr = dot_nt(go_stack, v_dups[kv])
            gs = probs * (gpr - jnp.sum(gpr * probs, -1, keepdims=True))
            gs = (gs * (1.0 / math.sqrt(HEAD_WIDTH))).astype(BF16)
            gp_ref[0, :, sl] = picked(dot_nn(gs, k_dups[kv]), left).astype(BF16)
            gk_sum = gk_sum + dot_tn(gs, q_stack)
            gv_sum = gv_sum + dot_tn(probs, go_stack)
        gks.append(gk_sum + pltpu.roll(gk_sum, HEAD_WIDTH, 1))
        gvs.append(gv_sum + pltpu.roll(gv_sum, HEAD_WIDTH, 1))
    gp_ref[0, :, OFF_K:OFF_V] = jnp.where(left, gks[0], gks[1]).astype(BF16)
    gp_ref[0, :, OFF_V:OFF_R] = jnp.where(left, gvs[0], gvs[1]).astype(BF16)


def whole(shape):
    return pl.BlockSpec(shape, lambda m: (0,) * len(shape))


def per_block(shape):
    return pl.BlockSpec((1, *shape), lambda m: (m,) + (0,) * len(shape))


def small_specs():
    return [
        per_block((T, 128)), per_block((8, T)), whole((8, CH)), whole((8, 128)), whole((8, SSM)),
    ]


def mix_forward(projected, tables):
    blocks = projected.shape[0]
    return pl.pallas_call(
        mix_forward_kernel,
        grid=(blocks,),
        in_specs=[per_block((T, PAD)), *small_specs()],
        out_specs=per_block((T, UW)),
        out_shape=jax.ShapeDtypeStruct((blocks, T, UW), BF16),
        scratch_shapes=[pltpu.VMEM((T, CH), F32)],
        compiler_params=pltpu.CompilerParams(vmem_limit_bytes=32 * 1024 * 1024),
        name="mix_forward",
    )(projected, *tables)


def mix_backward(projected, grad_joined, tables):
    blocks = projected.shape[0]
    return pl.pallas_call(
        mix_backward_kernel,
        grid=(blocks,),
        in_specs=[per_block((T, PAD)), per_block((T, UW)), *small_specs()],
        out_specs=[per_block((T, PAD)), per_block((8, CH)), per_block((8, 128)), per_block((8, SSM))],
        out_shape=[
            jax.ShapeDtypeStruct((blocks, T, PAD), BF16),
            jax.ShapeDtypeStruct((blocks, 8, CH), F32),
            jax.ShapeDtypeStruct((blocks, 8, 128), F32),
            jax.ShapeDtypeStruct((blocks, 8, SSM), F32),
        ],
        scratch_shapes=[
            pltpu.VMEM((T, CH), F32),
            pltpu.VMEM((T, CH), F32),
            pltpu.VMEM((T, CH), F32),
            pltpu.VMEM((128, T), F32),
        ],
        compiler_params=pltpu.CompilerParams(vmem_limit_bytes=40 * 1024 * 1024),
        name="mix_backward",
    )(projected, grad_joined, *tables)


def mixer_tables(segments, conv_rows, head_table):
    blocks = segments.shape[0]
    marks = segments.astype(F32)
    segc = jnp.broadcast_to(marks[:, :, None], (blocks, T, 128))
    segr = jnp.broadcast_to(marks[:, None, :], (blocks, 8, T))
    conv_rows = jnp.pad(conv_rows, ((0, 3), (0, 0)))
    head_rows = jnp.pad(head_table.T, ((0, 5), (0, 128 - MHEADS)))
    skip_rows = jnp.broadcast_to(jnp.repeat(head_table[:, 2], HEAD_WIDTH)[None], (8, SSM))
    return segc, segr, conv_rows, head_rows, skip_rows


MESH = pl.DeviceIdType.MESH
HOPS = ("xa", "xb", "za", "zb", "y")
ORDERS = (
    ("xa", "xb", "zb", "za", "y"),
    ("xb", "xa", "y", "zb", "za"),
    ("za", "zb", "xa", "y", "xb"),
    ("zb", "y", "za", "xb", "xa"),
    ("y", "za", "xb", "xa", "zb"),
)


def cut(array, tiles, orders=(0, 1, 2, 3, 4), first=0):
    parts = []
    for width, order in zip(tiles, orders):
        parts.append((array, 128 * first, 128 * width, ORDERS[order]))
        first += width
    return parts


GATHERED = (
    *cut(0, (7, 7, 7, 6, 5)),
    *cut(0, (1,), (4,), 32),
    *cut(1, (2, 3, 3), (2, 3, 4)),
    *cut(2, (7, 7, 6, 6, 6)),
    *cut(3, (3, 3, 2)),
)
SCATTERED = (
    *cut(3, (3, 3, 2)),
    *cut(1, (2, 3, 3), (2, 3, 4)),
    *cut(2, (7, 7, 6, 6, 6)),
    *cut(0, (7, 7, 7, 6, 6)),
    *cut(0, (1,), (4,), 33),
)
TAIL = 2 * FF
EXTRA = PAD
SHARD_ROWS = (64, 128, 64, 128)
SHARD_COLS = (PAD, 1024, 2 * FF, 1024)
SUM_COLS = (PAD + 128, 1024, 2 * FF, 1024)


def pair_a(i):
    return i + 1 - 2 * (i % 2)


def pair_b(i):
    return (i + 2 * (i % 2) + 3) % 4


def place():
    shard = lax.axis_index("shard")
    return lax.axis_index("section"), shard // 8, (shard // 2) % 4, shard % 2, lax.axis_index("rep")


def neighbours(section, y, z, core, x):
    def at(y, z, core, x):
        return (section, y * 8 + z * 2 + core, x)

    return {
        "core": at(y, z, 1 - core, x),
        "xa": at(y, z, core, pair_a(x)),
        "xb": at(y, z, core, pair_b(x)),
        "za": at(y, pair_a(z), core, x),
        "zb": at(y, pair_b(z), core, x),
        "y": at(1 - y, z, core, x),
        "xo": at(y, z, core, (x + 2) % 4),
    }


def meet(devices):
    barrier = pltpu.get_barrier_semaphore()
    for device in devices:
        pl.semaphore_signal(barrier, inc=1, device_id=device, device_id_type=MESH)
    pl.semaphore_wait(barrier, len(devices))


def halve(kept, hop, me):
    near, other = (pair_a, pair_b) if hop == "a" else (pair_b, pair_a)
    if kept[0][1] != 4:
        return [(near(me), 1)], [(me, 1)]
    if hop == "b":
        return [(2 * (near(me) // 2), 2)], [(2 * (me // 2), 2)]
    return [(near(me), 1), (other(near(me)), 1)], [(me, 1), (other(me), 1)]


def schedule(order, me_y, me_z, me_x):
    ys, zs, xs = [(0, 2)], [(0, 4)], [(0, 4)]
    stages = []
    for hop in order:
        if hop == "y":
            sent, ys = [(1 - me_y, 1)], [(me_y, 1)]
            gone = sent, zs, xs
        elif hop[0] == "z":
            sent, zs = halve(zs, hop[1], me_z)
            gone = ys, sent, xs
        else:
            sent, xs = halve(xs, hop[1], me_x)
            gone = ys, zs, sent
        stages.append((list(itertools.product(*gone)), list(itertools.product(ys, zs, xs))))
    return stages


def window(piece, quarter, column, columns):
    (y, ny), (z, nz), (x, nx) = piece
    rows = 0 if nx == 4 else pl.multiple_of(x * quarter, nx * quarter)
    return pl.ds(y, ny), pl.ds(z, nz), pl.ds(rows, nx * quarter), pl.ds(column, columns)


def piece_dims(piece, quarter):
    (_, ny), (_, nz), (_, nx) = piece
    return ny, nz, nx * quarter


def stage_shapes(parts):
    shapes = []
    for array, column, columns, order in parts:
        for sent, _ in schedule(order, 0, 0, 0):
            dims = piece_dims(sent[0], SHARD_ROWS[array] // 4)
            shapes.append((len(sent), *dims, columns))
    return shapes


def add_into(acc, window_at, arrived):
    ny, nz, rows, _ = arrived.shape
    ys, zs, rs, cs = window_at

    def step(i, carry):
        y, z = i // nz, i % nz
        at = (ys.start + y, zs.start + z, rs, cs)
        acc[at] = acc[at] + arrived[y, z]
        return carry

    if ny * nz == 1:
        step(0, 0)
    else:
        lax.fori_loop(0, ny * nz, step, 0)


def scatter_kernel(*refs):
    grads, extra, wholes, smalls = refs[:4], refs[4], refs[5:9], refs[9:12]
    accs, cores = refs[12:16], refs[16 : 16 + len(SCATTERED)]
    arrivals = refs[16 + len(SCATTERED) : -7]
    local_sem, core_send, core_recv, send_sem, recv_sem, last_send, last_recv = refs[-7:]
    section, y, z, core, x = place()
    near = neighbours(section, y, z, core, x)
    meet([near[name] for name in ("core", *HOPS, "xo")])

    loads, swaps = [], []
    for p, (array, column, columns, _) in enumerate(SCATTERED):
        cols = pl.ds(column, columns)
        grad = extra if (array, column) == (0, EXTRA) else grads[array].at[:, :, :, :, cols]
        swap = pltpu.make_async_remote_copy(
            src_ref=grad.at[:, :, 1 - core],
            dst_ref=cores[p],
            send_sem=core_send.at[p],
            recv_sem=core_recv.at[p],
            device_id=near["core"],
            device_id_type=MESH,
        )
        swap.start()
        load = pltpu.make_async_copy(
            grad.at[:, :, core], accs[array].at[:, :, :, cols], local_sem.at[p]
        )
        load.start()
        swaps.append(swap)
        loads.append(load)

    plans = [schedule(order, y, z, x) for _, _, _, order in SCATTERED]
    flying, last = {}, []
    sems = 0
    for stage in range(len(HOPS) + 1):
        for p, (array, column, columns, order) in enumerate(SCATTERED):
            quarter = SHARD_ROWS[array] // 4
            if stage == 0:
                loads[p].wait()
                swaps[p].wait_recv()
                add_into(accs[array], window(((0, 2), (0, 4), (0, 4)), quarter, column, columns), cores[p])
            else:
                kept = plans[p][stage - 1][1]
                for k, (copy, piece) in enumerate(zip(flying[p, stage - 1], kept)):
                    copy.wait_recv()
                    add_into(
                        accs[array],
                        window(piece, quarter, column, columns),
                        arrivals[p * len(HOPS) + stage - 1].at[k],
                    )
            if stage < len(HOPS):
                copies = []
                for k, piece in enumerate(plans[p][stage][0]):
                    copy = pltpu.make_async_remote_copy(
                        src_ref=accs[array].at[window(piece, quarter, column, columns)],
                        dst_ref=arrivals[p * len(HOPS) + stage].at[k],
                        send_sem=send_sem.at[sems],
                        recv_sem=recv_sem.at[sems],
                        device_id=near[order[stage]],
                        device_id_type=MESH,
                    )
                    copy.start()
                    copies.append(copy)
                    sems += 1
                flying[p, stage] = copies
                continue
            if p + 1 < len(SCATTERED) and SCATTERED[p + 1][0] == array:
                continue
            mine = pl.ds(pl.multiple_of(x * quarter, quarter), quarter)
            for k, name in enumerate(("xo", "xa", "xb")):
                copy = pltpu.make_async_remote_copy(
                    src_ref=accs[array].at[y, z, mine],
                    dst_ref=wholes[array].at[mine],
                    send_sem=last_send.at[array, k],
                    recv_sem=last_recv.at[array, k],
                    device_id=near[name],
                    device_id_type=MESH,
                )
                copy.start()
                last.append(copy)
            wholes[array][mine, :] = accs[array][y, z, mine, :]

    for copy in last:
        copy.wait_recv()
    small = wholes[0][:, EXTRA:].astype(F32)
    out_gains, out_conv, out_head = smalls
    out_conv[:, :56] = small[: CONV + 1, :56]
    out_conv[:, 56:] = small[8 : 9 + CONV, :56]
    out_gains[...] = small[16:18, :64]
    out_head[...] = small[24:27, :MHEADS]
    for copy in last + swaps + [c for copies in flying.values() for c in copies]:
        copy.wait_send()


def scatter_sums(grads, extra):
    n_copies = sum(shape[0] for shape in stage_shapes(SCATTERED))
    n_parts = len(SCATTERED)
    out_shapes = [
        *[jax.ShapeDtypeStruct(s, BF16) for s in zip(SHARD_ROWS, SUM_COLS)],
        *[jax.ShapeDtypeStruct(s, F32) for s in ((2, 64), (CONV + 1, T), (3, MHEADS))],
    ]
    return pl.pallas_call(
        scatter_kernel,
        in_specs=[pl.BlockSpec(memory_space=pl.ANY)] * 5,
        out_specs=[pl.BlockSpec(memory_space=pltpu.VMEM)] * 7,
        out_shape=out_shapes,
        scratch_shapes=[
            *[pltpu.VMEM((2, 4, r, c), BF16) for r, c in zip(SHARD_ROWS, SUM_COLS)],
            *[pltpu.VMEM((2, 4, SHARD_ROWS[a], cols), BF16) for a, _, cols, _ in SCATTERED],
            *[pltpu.VMEM(shape, BF16) for shape in stage_shapes(SCATTERED)],
            pltpu.SemaphoreType.DMA((n_parts,)),
            pltpu.SemaphoreType.DMA((n_parts,)),
            pltpu.SemaphoreType.DMA((n_parts,)),
            pltpu.SemaphoreType.DMA((n_copies,)),
            pltpu.SemaphoreType.DMA((n_copies,)),
            pltpu.SemaphoreType.DMA((4, 3)),
            pltpu.SemaphoreType.DMA((4, 3)),
        ],
        compiler_params=pltpu.CompilerParams(
            collective_id=1, has_side_effects=True, vmem_limit_bytes=58 * 1024 * 1024
        ),
        name="scatter_sums",
    )(*grads, extra)


def gather_kernel(*refs):
    shards, tail, outs = refs[:4], refs[4], refs[5:9]
    local_sem, send_sem, recv_sem, core_send, core_recv = refs[9:]
    section, y, z, core, x = place()
    near = neighbours(section, y, z, core, x)
    meet([near[name] for name in ("core", *HOPS)])

    def at(array, piece, column, columns):
        ys, zs, rows, cols = window(piece, SHARD_ROWS[array] // 4, column, columns)
        return outs[array].at[ys, zs, pl.ds(core, 1), rows, cols]

    def own(array, column, columns):
        quarter = SHARD_ROWS[array] // 4
        rows = pl.ds(pl.multiple_of(x * quarter, quarter), quarter)
        if (array, column) == (0, TAIL):
            return tail.at[:, :, :, rows]
        return shards[array].at[:, :, :, rows, pl.ds(column, columns)]

    passed = []

    def pass_on(source, target):
        k = len(passed)
        copy = pltpu.make_async_remote_copy(
            src_ref=source,
            dst_ref=target,
            send_sem=core_send.at[k],
            recv_sem=core_recv.at[k],
            device_id=near["core"],
            device_id_type=MESH,
        )
        copy.start()
        passed.append(copy)

    locals_ = []
    for p, (array, column, columns, _) in enumerate(GATHERED):
        copy = pltpu.make_async_copy(
            own(array, column, columns), at(array, ((y, 1), (z, 1), (x, 1)), column, columns), local_sem.at[p]
        )
        copy.start()
        locals_.append(copy)

    plans = [schedule(order, y, z, x)[::-1] for _, _, _, order in GATHERED]
    flying, sent = {}, []
    for stage in range(len(HOPS) + 1):
        for p, (array, column, columns, order) in enumerate(GATHERED):
            if stage:
                for copy in flying[p, stage - 1]:
                    copy.wait_recv()
            if stage == 1:
                locals_[p].wait()
            if stage < len(HOPS):
                copies = []
                for piece in plans[p][stage][1]:
                    target = at(array, piece, column, columns)
                    copy = pltpu.make_async_remote_copy(
                        src_ref=target if stage else own(array, column, columns),
                        dst_ref=target,
                        send_sem=send_sem.at[len(sent)],
                        recv_sem=recv_sem.at[len(sent)],
                        device_id=near[order[::-1][stage]],
                        device_id_type=MESH,
                    )
                    copy.start()
                    copies.append(copy)
                    sent.append(copy)
                flying[p, stage] = copies
            if stage:
                for piece in plans[p][stage - 1][0]:
                    here = at(array, piece, column, columns)
                    pass_on(here, here)
            else:
                pass_on(own(array, column, columns), at(array, ((y, 1), (z, 1), (x, 1)), column, columns))
    for copy in passed:
        copy.wait()
    for copy in sent:
        copy.wait_send()


def gather_shards(shards, tail):
    n_copies = sum(shape[0] for shape in stage_shapes(GATHERED))
    n_passed = n_copies + len(GATHERED)
    return pl.pallas_call(
        gather_kernel,
        in_specs=[pl.BlockSpec(memory_space=pl.ANY)] * 5,
        out_specs=[pl.BlockSpec(memory_space=pl.ANY)] * 4,
        out_shape=[
            jax.ShapeDtypeStruct((2, 4, 2, r, c), BF16) for r, c in zip(SHARD_ROWS, SHARD_COLS)
        ],
        scratch_shapes=[
            pltpu.SemaphoreType.DMA((len(GATHERED),)),
            pltpu.SemaphoreType.DMA((n_copies,)),
            pltpu.SemaphoreType.DMA((n_copies,)),
            pltpu.SemaphoreType.DMA((n_passed,)),
            pltpu.SemaphoreType.DMA((n_passed,)),
        ],
        compiler_params=pltpu.CompilerParams(collective_id=2, has_side_effects=True),
        name="gather_shards",
    )(*shards, tail)


def rms_norm(values, gain):
    return values * lax.rsqrt(jnp.mean(values * values, -1, keepdims=True) + 1e-05) * gain


def rms_back(values, gain, grad):
    scale = lax.rsqrt(jnp.mean(values * values, -1, keepdims=True) + 1e-05)
    unit = values * scale
    scaled = grad * gain
    grad_values = scale * (scaled - unit * jnp.mean(scaled * unit, -1, keepdims=True))
    return grad_values, jnp.sum(grad * unit, 0)


def forward_product(left, weight):
    return jnp.dot(left, weight, preferred_element_type=F32)


def back_product(grad_rows, weight):
    return lax.dot_general(
        grad_rows, weight, (((1,), (1,)), ((), ())), preferred_element_type=F32
    )


def outer_sum(left, right):
    return lax.dot_general(
        left, right, (((0,), (0,)), ((), ())), preferred_element_type=F32
    ).astype(BF16)


def layer_forward(inputs, weights, tables):
    gains, w_in, w_out, w_gate_up, w_down = weights
    blocks = inputs.shape[0] // T
    normed = rms_norm(inputs, gains[0]).astype(BF16)
    projected = forward_product(normed, w_in)
    joined = mix_forward(projected.reshape(blocks, T, PAD), tables).reshape(blocks * T, UW)
    hidden = inputs + forward_product(joined, w_out)
    normed_two = rms_norm(hidden, gains[1]).astype(BF16)
    gate_up = forward_product(normed_two, w_gate_up)
    activated = (jax.nn.silu(gate_up[:, :FF]) * gate_up[:, FF:]).astype(BF16)
    result = hidden + forward_product(activated, w_down)
    return result, (inputs, normed, projected, joined, hidden, normed_two, gate_up, activated)


def layer_backward(grad_out, saved, weights, tables):
    gains, w_in, w_out, w_gate_up, w_down = weights
    inputs, normed, projected, joined, hidden, normed_two, gate_up, activated = saved
    blocks = inputs.shape[0] // T
    grad_ffn = grad_out.astype(BF16)
    grad_act = back_product(grad_ffn, w_down)
    gate, up = gate_up[:, :FF], gate_up[:, FF:]
    sig = jax.nn.sigmoid(gate)
    grad_gate = (grad_act * up * (sig * (1.0 + gate * (1.0 - sig)))).astype(BF16)
    grad_up = (grad_act * (gate * sig)).astype(BF16)
    grad_gate_up = jnp.concatenate([grad_gate, grad_up], 1)
    grad_hidden, grad_gain_two = rms_back(hidden, gains[1], back_product(grad_gate_up, w_gate_up))
    grad_hidden = grad_out + grad_hidden
    grad_branch = grad_hidden.astype(BF16)
    grad_joined = back_product(grad_branch, w_out)
    grad_proj, grad_conv, grad_head, grad_skip = mix_backward(
        projected.reshape(blocks, T, PAD), grad_joined.reshape(blocks, T, UW), tables
    )
    grad_proj = grad_proj.reshape(blocks * T, PAD)
    grad_input, grad_gain_one = rms_back(inputs, gains[0], back_product(grad_proj, w_in))
    grad_input = grad_hidden + grad_input
    pairs = (
        (normed, grad_proj),
        (joined, grad_branch),
        (normed_two, grad_gate_up),
        (activated, grad_ffn),
    )
    return grad_input, pairs, (grad_gain_one, grad_gain_two, grad_conv, grad_head, grad_skip)


def across(array, by):
    return lax.ppermute(array, "section", [(0, 1)] if by > 0 else [(1, 0)])


def gather_weights(norm_gains, w_in, conv_params, w_out, w_gate_up, w_down):
    rows = w_in.shape[0]
    conv_rows = conv_params.T
    small = jnp.concatenate(
        [
            jnp.pad(conv_rows[:, :56], ((0, 3), (0, 8))),
            jnp.pad(conv_rows[:, 56:], ((0, 3), (0, 8))),
            norm_gains.T,
        ],
        0,
    )
    small = jnp.pad(small, ((0, rows - small.shape[0]), (0, PAD - PIN - 64)))
    tail = jnp.concatenate([w_in[:, TAIL:], small], 1)
    parts = gather_shards(
        [a.reshape(1, 1, 1, *a.shape) for a in (w_in, w_out, w_gate_up, w_down)],
        tail.reshape(1, 1, 1, *tail.shape),
    )
    small = parts[0][..., PIN : PIN + 64].reshape(-1, rows, 64)[:, :18].astype(F32)
    gains = small[:, 16:18].transpose(1, 0, 2).reshape(2, -1)
    conv_rows = small[:, :16, :56].reshape(-1, 2, 8, 56)[:, :, : CONV + 1]
    conv_rows = conv_rows.transpose(2, 0, 1, 3).reshape(CONV + 1, -1)
    return (gains, *[a.reshape(-1, a.shape[-1]) for a in parts]), conv_rows


def body(
    tokens,
    segment_ids,
    cotangent,
    norm_gains,
    w_in,
    conv_params,
    head_params,
    w_out,
    w_gate_up,
    w_down,
):
    section = lax.axis_index("section")
    blocks, _, width = tokens.shape
    rows = blocks * T
    weights, conv_rows = gather_weights(
        norm_gains[0], w_in[0], conv_params[0], w_out[0], w_gate_up[0], w_down[0]
    )
    tables = mixer_tables(segment_ids[:, 0], conv_rows, head_params[0].astype(F32))

    own = tokens.reshape(rows, width)
    first, _ = layer_forward(own.astype(F32), weights, tables)
    received = across(first.astype(BF16), 1)
    inputs = jnp.where(section == 0, own, received).astype(F32)
    result, saved = layer_forward(inputs, weights, tables)

    top = cotangent.reshape(rows, width)
    first_grad, _, _ = layer_backward(top.astype(F32), saved, weights, tables)
    coming = across(first_grad.astype(BF16), -1)
    grad_out = jnp.where(section == 1, top, coming).astype(F32)
    grad_input, pairs, smalls = layer_backward(grad_out, saved, weights, tables)

    grad_gain_one, grad_gain_two, grad_conv, grad_head, grad_skip = smalls
    sums = [outer_sum(left, right) for left, right in pairs]
    shards = lax.axis_size("shard")
    gains = jnp.stack([grad_gain_one, grad_gain_two]).reshape(2, shards, 64).transpose(1, 0, 2)
    conv = jnp.sum(grad_conv, 0).reshape(8, shards, 2, 56).transpose(1, 2, 0, 3)
    conv = conv.reshape(shards, 16, 56)
    skip = jnp.sum(jnp.sum(grad_skip, 0)[0].reshape(MHEADS, HEAD_WIDTH), 1)
    head = jnp.concatenate([jnp.sum(grad_head, 0)[:2, :MHEADS], skip[None]], 0)
    head = jnp.broadcast_to(head[None], (shards, 3, MHEADS))
    extra = jnp.concatenate(
        [
            jnp.pad(conv, ((0, 0), (0, 0), (0, 72))),
            jnp.pad(gains, ((0, 0), (0, 6), (0, 64))),
            jnp.pad(head, ((0, 0), (0, 37), (0, 128 - MHEADS))),
        ],
        1,
    ).astype(BF16)
    out_in, out_out, out_gu, out_dn, out_gains, out_conv, out_head = scatter_sums(
        [g.reshape(2, 4, 2, g.shape[0] // 16, g.shape[1]) for g in sums],
        extra.reshape(2, 4, 2, 64, 128),
    )
    return (
        result.astype(BF16).reshape(1, blocks, T, width),
        grad_input.reshape(1, blocks, T, width),
        out_gains.T[None],
        out_in[None, :, :PIN].astype(F32),
        out_conv.T[None],
        out_head.T[None],
        out_out[None].astype(F32),
        out_gu[None].astype(F32),
        out_dn[None].astype(F32),
    )


def solution(mesh):
    in_specs = (
        P(None, ("shard", "rep"), None),
        P(None, ("shard", "rep"), None),
        P(None, ("shard", "rep"), None),
        P("section", "shard", None),
        P("section", "shard", None),
        P("section", "shard", None),
        P("section", None, None),
        P("section", "shard", None),
        P("section", "shard", None),
        P("section", "shard", None),
    )
    out_specs = (
        P("section", None, ("shard", "rep"), None),
        P("section", None, ("shard", "rep"), None),
        P("section", "shard", None),
        P("section", "shard", None),
        P("section", "shard", None),
        P("section", None, None),
        P("section", "shard", None),
        P("section", "shard", None),
        P("section", "shard", None),
    )
    return jax.shard_map(body, mesh=mesh, in_specs=in_specs, out_specs=out_specs, check_vma=False)
```

```python
import itertools
import math

import jax
import jax.numpy as jnp
from jax import lax
from jax.experimental import pallas as pl
from jax.experimental.pallas import tpu as pltpu
from jax.sharding import PartitionSpec as P

FF = 2048
MHEADS = 24
HEAD_WIDTH = 64
STATE = 128
QUERY_HEAD_COUNT = 8
KVHEADS = 2
CONV = 4
SSM = 1536
CH = 1792
UW = 2048
PIN = 4120
PAD = 4224
T = 112
OFF_Q = SSM + CH
OFF_K = OFF_Q + QUERY_HEAD_COUNT * HEAD_WIDTH
OFF_V = OFF_K + KVHEADS * HEAD_WIDTH
OFF_R = OFF_V + KVHEADS * HEAD_WIDTH
F32 = jnp.float32
BF16 = jnp.bfloat16


def dot_nn(left, right):
    return jnp.dot(left.astype(BF16), right.astype(BF16), preferred_element_type=F32)


def dot_nt(left, right):
    return lax.dot_general(
        left.astype(BF16), right.astype(BF16), (((1,), (1,)), ((), ())), preferred_element_type=F32
    )


def dot_tn(left, right):
    return lax.dot_general(
        left.astype(BF16), right.astype(BF16), (((0,), (0,)), ((), ())), preferred_element_type=F32
    )


def exact_dot(left, right):
    return jnp.dot(left, right, precision=lax.Precision.HIGHEST, preferred_element_type=F32)


def iota(shape, dim):
    return lax.broadcasted_iota(jnp.int32, shape, dim)


def block_masks(segc, segr):
    rows, cols = iota((T, T), 0), iota((T, T), 1)
    allowed = (segc[:, :T] == segr[0:1, :]) & (rows >= cols)
    places = iota((T, 128), 0)
    links = [
        jnp.where((pltpu.roll(segc, j, 0) == segc) & (places >= j), 1.0, 0.0)
        for j in range(1, CONV)
    ]
    return allowed, links


def convolve(p_ref, conv_ref, links, mixed_ref, act_ref):
    for at in range(0, CH, 128):
        sl = slice(at, at + 128)
        c = p_ref[0, :, SSM + at : SSM + at + 128]
        mixed = conv_ref[4:5, sl] + c * conv_ref[0:1, sl]
        for j in range(1, CONV):
            mixed = mixed + links[j - 1] * pltpu.roll(c, j, 0) * conv_ref[j : j + 1, sl]
        if mixed_ref is not None:
            mixed_ref[:, sl] = mixed
        act_ref[:, sl] = mixed * jax.nn.sigmoid(mixed)


def softplus(v):
    return jnp.maximum(v, 0.0) + jnp.log1p(jnp.exp(-jnp.abs(v)))


def steps_and_sums(p_ref, head_ref):
    raw = p_ref[0, :, OFF_R:PAD] + head_ref[0:1, :]
    live = iota((T, 128), 1) < MHEADS
    raw = jnp.where(live, raw, 0.0)
    dt = softplus(raw)
    decay = -dt * jnp.exp(head_ref[1:2, :])
    lower = jnp.where(iota((T, T), 0) >= iota((T, T), 1), 1.0, 0.0)
    return raw, dt, decay, exact_dot(lower, decay)


def stacked(tile, left):
    return jnp.concatenate([jnp.where(left, tile, 0.0), jnp.where(left, 0.0, tile)], 0).astype(BF16)


def picked(tiles, left):
    return jnp.where(left, tiles[:T], tiles[T:])


def attention_probs(q_stack, k_dup, both_allowed):
    scores = dot_nt(q_stack, k_dup) * (1.0 / math.sqrt(HEAD_WIDTH))
    scores = jnp.where(both_allowed, scores, -1e30)
    e = jnp.exp(scores - jnp.max(scores, -1, keepdims=True))
    return e / jnp.sum(e, -1, keepdims=True)


def doubled(tile, left):
    turned = pltpu.roll(tile, HEAD_WIDTH, 1)
    return jnp.where(left, tile, turned), jnp.where(left, turned, tile)


def mix_forward_kernel(p_ref, segc_ref, segr_ref, conv_ref, head_ref, skip_ref, u_ref, *rest):
    y_ref, act_ref = rest if len(rest) == 2 else (None, *rest)
    allowed, links = block_masks(segc_ref[0], segr_ref[0])
    convolve(p_ref, conv_ref, links, None, act_ref)
    _, dt, _, cum = steps_and_sums(p_ref, head_ref)
    dt_t, cum_t = dt.T, cum.T
    left = iota((T, 128), 1) < HEAD_WIDTH
    cb = dot_nt(act_ref[:, SSM + STATE :], act_ref[:, SSM : SSM + STATE])
    for pair in range(MHEADS // 2):
        sl = slice(128 * pair, 128 * pair + 128)
        xs = act_ref[:, sl]
        parts = []
        for h in (2 * pair, 2 * pair + 1):
            decayed = jnp.exp(jnp.where(allowed, cum[:, h : h + 1] - cum_t[h : h + 1, :], -1e30))
            parts.append((decayed * cb * dt_t[h : h + 1, :]).astype(BF16))
        y = picked(dot_nn(jnp.concatenate(parts, 0), xs), left) + skip_ref[0:1, sl] * xs
        if y_ref is not None:
            y_ref[0, :, sl] = y
        z = p_ref[0, :, sl]
        u_ref[0, :, sl] = (y * (z * jax.nn.sigmoid(z))).astype(BF16)
    k_dups = [tile.astype(BF16) for tile in doubled(p_ref[0, :, OFF_K:OFF_V], left)]
    v_dups = [tile.astype(BF16) for tile in doubled(p_ref[0, :, OFF_V:OFF_R], left)]
    places = iota((2 * T, T), 0)
    marks = jnp.concatenate([segc_ref[0], segc_ref[0]], 0)[:, :T]
    both_allowed = (marks == segr_ref[0][0:1, :]) & (
        jnp.where(places >= T, places - T, places) >= iota((2 * T, T), 1)
    )
    for pair in range(QUERY_HEAD_COUNT // 2):
        kv = pair // 2
        q_tile = p_ref[0, :, OFF_Q + 128 * pair : OFF_Q + 128 * pair + 128]
        probs = attention_probs(stacked(q_tile, left), k_dups[kv], both_allowed)
        u_ref[0, :, SSM + 128 * pair : SSM + 128 * pair + 128] = picked(
            dot_nn(probs, v_dups[kv]), left
        ).astype(BF16)


def mix_backward_kernel(
    p_ref, gu_ref, y_ref, segc_ref, segr_ref, conv_ref, head_ref, skip_ref,
    gp_ref, gconv_ref, ghead_ref, gskip_ref,
    mixed_ref, act_ref, gact_ref, colq_ref,
):
    allowed, links = block_masks(segc_ref[0], segr_ref[0])
    convolve(p_ref, conv_ref, links, mixed_ref, act_ref)
    raw, dt, decay, cum = steps_and_sums(p_ref, head_ref)
    dt_t, cum_t = dt.T, cum.T
    lanes = iota((T, 128), 1)
    left = lanes < HEAD_WIDTH
    b_rows = act_ref[:, SSM : SSM + STATE]
    c_rows = act_ref[:, SSM + STATE :]
    cb = dot_nt(c_rows, b_rows)
    gcb = jnp.zeros((T, T), F32)
    row_form = jnp.zeros((T, 128), F32)
    colq_ref[...] = jnp.zeros_like(colq_ref)
    for pair in range(MHEADS // 2):
        sl = slice(128 * pair, 128 * pair + 128)
        xs = act_ref[:, sl]
        xs16 = xs.astype(BF16)
        z = p_ref[0, :, sl]
        gm = gu_ref[0, :, sl]
        sg = jax.nn.sigmoid(z)
        gy = gm * (z * sg)
        gy_stack = stacked(gy, left)
        gks = dot_nt(gy_stack, xs16)
        parts = []
        for side, h in enumerate((2 * pair, 2 * pair + 1)):
            decayed = jnp.exp(jnp.where(allowed, cum[:, h : h + 1] - cum_t[h : h + 1, :], -1e30))
            dt_row = dt_t[h : h + 1, :]
            base = decayed * cb
            parts.append((base * dt_row).astype(BF16))
            gk = gks[side * T : side * T + T]
            gcb = gcb + gk * (decayed * dt_row)
            q = gk * base
            colq_ref[h : h + 1, :] = jnp.sum(q, 0, keepdims=True)
            row_form = jnp.where(lanes == h, jnp.sum(q * dt_row, 1, keepdims=True), row_form)
        skip = skip_ref[0:1, sl]
        kernels = jnp.concatenate(parts, 0)
        y = y_ref[0, :, sl]
        gp_ref[0, :, sl] = (gm * y * (sg * (1.0 + z * (1.0 - sg)))).astype(BF16)
        gact_ref[:, sl] = dot_tn(kernels, gy_stack) + skip * gy
        gskip_ref[0, 0:1, sl] = jnp.sum(gy * xs, 0, keepdims=True)
    gact_ref[:, SSM : SSM + STATE] = dot_tn(gcb, c_rows)
    gact_ref[:, SSM + STATE :] = dot_nn(gcb, b_rows)
    col_form = colq_ref[...].T
    gcum = row_form - col_form * dt
    upper = jnp.where(iota((T, T), 0) <= iota((T, T), 1), 1.0, 0.0)
    gdecay = exact_dot(upper, gcum)
    gdt = col_form - gdecay * jnp.exp(head_ref[1:2, :])
    graw = jnp.where(lanes < MHEADS, gdt * jax.nn.sigmoid(raw), 0.0)
    gp_ref[0, :, OFF_R:PAD] = graw.astype(BF16)
    ghead_ref[0, 0:1, :] = jnp.sum(graw, 0, keepdims=True)
    ghead_ref[0, 1:2, :] = jnp.sum(gdecay * decay, 0, keepdims=True)
    for at in range(0, CH, 128):
        sl = slice(at, at + 128)
        mixed = mixed_ref[:, sl]
        sg = jax.nn.sigmoid(mixed)
        gmix = gact_ref[:, sl] * (sg * (1.0 + mixed * (1.0 - sg)))
        c = p_ref[0, :, SSM + at : SSM + at + 128]
        gc = gmix * conv_ref[0:1, sl]
        gconv_ref[0, 0:1, sl] = jnp.sum(gmix * c, 0, keepdims=True)
        for j in range(1, CONV):
            linked = gmix * links[j - 1]
            gc = gc + pltpu.roll(linked, T - j, 0) * conv_ref[j : j + 1, sl]
            gconv_ref[0, j : j + 1, sl] = jnp.sum(linked * pltpu.roll(c, j, 0), 0, keepdims=True)
        gconv_ref[0, 4:5, sl] = jnp.sum(gmix, 0, keepdims=True)
        gconv_ref[0, 5:8, sl] = jnp.zeros((3, 128), F32)
        gp_ref[0, :, SSM + at : SSM + at + 128] = gc.astype(BF16)
    k_dups = [tile.astype(BF16) for tile in doubled(p_ref[0, :, OFF_K:OFF_V], left)]
    v_dups = [tile.astype(BF16) for tile in doubled(p_ref[0, :, OFF_V:OFF_R], left)]
    places = iota((2 * T, T), 0)
    marks = jnp.concatenate([segc_ref[0], segc_ref[0]], 0)[:, :T]
    both_allowed = (marks == segr_ref[0][0:1, :]) & (
        jnp.where(places >= T, places - T, places) >= iota((2 * T, T), 1)
    )
    gks, gvs = [], []
    for kv in range(KVHEADS):
        gk_sum = jnp.zeros((T, 128), F32)
        gv_sum = jnp.zeros((T, 128), F32)
        for pair in (2 * kv, 2 * kv + 1):
            sl = slice(OFF_Q + 128 * pair, OFF_Q + 128 * pair + 128)
            q_tile = p_ref[0, :, sl]
            go = gu_ref[0, :, SSM + 128 * pair : SSM + 128 * pair + 128]
            q_stack, go_stack = stacked(q_tile, left), stacked(go, left)
            probs = attention_probs(q_stack, k_dups[kv], both_allowed)
            gpr = dot_nt(go_stack, v_dups[kv])
            gs = probs * (gpr - jnp.sum(gpr * probs, -1, keepdims=True))
            gs = (gs * (1.0 / math.sqrt(HEAD_WIDTH))).astype(BF16)
            gp_ref[0, :, sl] = picked(dot_nn(gs, k_dups[kv]), left).astype(BF16)
            gk_sum = gk_sum + dot_tn(gs, q_stack)
            gv_sum = gv_sum + dot_tn(probs, go_stack)
        gks.append(gk_sum + pltpu.roll(gk_sum, HEAD_WIDTH, 1))
        gvs.append(gv_sum + pltpu.roll(gv_sum, HEAD_WIDTH, 1))
    gp_ref[0, :, OFF_K:OFF_V] = jnp.where(left, gks[0], gks[1]).astype(BF16)
    gp_ref[0, :, OFF_V:OFF_R] = jnp.where(left, gvs[0], gvs[1]).astype(BF16)


def whole(shape):
    return pl.BlockSpec(shape, lambda m: (0,) * len(shape))


def per_block(shape):
    return pl.BlockSpec((1, *shape), lambda m: (m,) + (0,) * len(shape))


def small_specs():
    return [
        per_block((T, 128)), per_block((8, T)), whole((8, CH)), whole((8, 128)), whole((8, SSM)),
    ]


def mix_forward(projected, tables, keep):
    blocks = projected.shape[0]
    widths = ((UW, BF16), (SSM, F32))[: 1 + keep]
    return pl.pallas_call(
        mix_forward_kernel,
        grid=(blocks,),
        in_specs=[per_block((T, PAD)), *small_specs()],
        out_specs=[per_block((T, width)) for width, _ in widths],
        out_shape=[jax.ShapeDtypeStruct((blocks, T, width), kind) for width, kind in widths],
        scratch_shapes=[pltpu.VMEM((T, CH), F32)],
        compiler_params=pltpu.CompilerParams(vmem_limit_bytes=32 * 1024 * 1024),
        name="mix_forward",
    )(projected, *tables)


def mix_backward(projected, grad_joined, kept, tables):
    blocks = projected.shape[0]
    return pl.pallas_call(
        mix_backward_kernel,
        grid=(blocks,),
        in_specs=[per_block((T, PAD)), per_block((T, UW)), per_block((T, SSM)), *small_specs()],
        out_specs=[per_block((T, PAD)), per_block((8, CH)), per_block((8, 128)), per_block((8, SSM))],
        out_shape=[
            jax.ShapeDtypeStruct((blocks, T, PAD), BF16),
            jax.ShapeDtypeStruct((blocks, 8, CH), F32),
            jax.ShapeDtypeStruct((blocks, 8, 128), F32),
            jax.ShapeDtypeStruct((blocks, 8, SSM), F32),
        ],
        scratch_shapes=[
            pltpu.VMEM((T, CH), F32),
            pltpu.VMEM((T, CH), F32),
            pltpu.VMEM((T, CH), F32),
            pltpu.VMEM((128, T), F32),
        ],
        compiler_params=pltpu.CompilerParams(vmem_limit_bytes=40 * 1024 * 1024),
        name="mix_backward",
    )(projected, grad_joined, kept, *tables)


def mixer_tables(segments, conv_rows, head_table):
    blocks = segments.shape[0]
    marks = segments.astype(F32)
    segc = jnp.broadcast_to(marks[:, :, None], (blocks, T, 128))
    segr = jnp.broadcast_to(marks[:, None, :], (blocks, 8, T))
    conv_rows = jnp.pad(conv_rows, ((0, 3), (0, 0)))
    head_rows = jnp.pad(head_table.T, ((0, 5), (0, 128 - MHEADS)))
    skip_rows = jnp.broadcast_to(jnp.repeat(head_table[:, 2], HEAD_WIDTH)[None], (8, SSM))
    return segc, segr, conv_rows, head_rows, skip_rows


MESH = pl.DeviceIdType.MESH
HOPS = ("xa", "xb", "za", "zb", "y")
ORDERS = (
    ("xa", "xb", "zb", "za", "y"),
    ("xb", "xa", "y", "zb", "za"),
    ("za", "zb", "xa", "y", "xb"),
    ("zb", "y", "za", "xb", "xa"),
    ("y", "za", "xb", "xa", "zb"),
)


def cut(array, tiles, orders=(0, 1, 2, 3, 4), first=0):
    parts = []
    for width, order in zip(tiles, orders):
        parts.append((array, 128 * first, 128 * width, ORDERS[order]))
        first += width
    return parts


GATHERED = (
    *cut(0, (7, 7, 7, 6, 5)),
    *cut(0, (1,), (4,), 32),
    *cut(1, (2, 3, 3), (2, 3, 4)),
    *cut(2, (7, 7, 6, 6, 6)),
    *cut(3, (3, 3, 2)),
)
SCATTERED = (
    *cut(3, (3, 3, 2)),
    *cut(1, (2, 3, 3), (2, 3, 4)),
    *cut(2, (7, 7, 6, 6, 6)),
    *cut(0, (7, 7, 7, 6, 6)),
    *cut(0, (1,), (4,), 33),
)
TAIL = 2 * FF
EXTRA = PAD
SHARD_ROWS = (64, 128, 64, 128)
SHARD_COLS = (PAD, 1024, 2 * FF, 1024)
SUM_COLS = (PAD + 128, 1024, 2 * FF, 1024)


def pair_a(i):
    return i + 1 - 2 * (i % 2)


def pair_b(i):
    return (i + 2 * (i % 2) + 3) % 4


def place():
    shard = lax.axis_index("shard")
    return lax.axis_index("section"), shard // 8, (shard // 2) % 4, shard % 2, lax.axis_index("rep")


def neighbours(section, y, z, core, x):
    def at(y, z, core, x):
        return (section, y * 8 + z * 2 + core, x)

    return {
        "core": at(y, z, 1 - core, x),
        "xa": at(y, z, core, pair_a(x)),
        "xb": at(y, z, core, pair_b(x)),
        "za": at(y, pair_a(z), core, x),
        "zb": at(y, pair_b(z), core, x),
        "y": at(1 - y, z, core, x),
        "xo": at(y, z, core, (x + 2) % 4),
    }


def meet(devices):
    barrier = pltpu.get_barrier_semaphore()
    for device in devices:
        pl.semaphore_signal(barrier, inc=1, device_id=device, device_id_type=MESH)
    pl.semaphore_wait(barrier, len(devices))


def halve(kept, hop, me):
    near, other = (pair_a, pair_b) if hop == "a" else (pair_b, pair_a)
    if kept[0][1] != 4:
        return [(near(me), 1)], [(me, 1)]
    if hop == "b":
        return [(2 * (near(me) // 2), 2)], [(2 * (me // 2), 2)]
    return [(near(me), 1), (other(near(me)), 1)], [(me, 1), (other(me), 1)]


def schedule(order, me_y, me_z, me_x):
    ys, zs, xs = [(0, 2)], [(0, 4)], [(0, 4)]
    stages = []
    for hop in order:
        if hop == "y":
            sent, ys = [(1 - me_y, 1)], [(me_y, 1)]
            gone = sent, zs, xs
        elif hop[0] == "z":
            sent, zs = halve(zs, hop[1], me_z)
            gone = ys, sent, xs
        else:
            sent, xs = halve(xs, hop[1], me_x)
            gone = ys, zs, sent
        stages.append((list(itertools.product(*gone)), list(itertools.product(ys, zs, xs))))
    return stages


def window(piece, quarter, column, columns):
    (y, ny), (z, nz), (x, nx) = piece
    rows = 0 if nx == 4 else pl.multiple_of(x * quarter, nx * quarter)
    return pl.ds(y, ny), pl.ds(z, nz), pl.ds(rows, nx * quarter), pl.ds(column, columns)


def piece_dims(piece, quarter):
    (_, ny), (_, nz), (_, nx) = piece
    return ny, nz, nx * quarter


def stage_shapes(parts):
    shapes = []
    for array, column, columns, order in parts:
        for sent, _ in schedule(order, 0, 0, 0):
            dims = piece_dims(sent[0], SHARD_ROWS[array] // 4)
            shapes.append((len(sent), *dims, columns))
    return shapes


def add_into(acc, window_at, arrived):
    ny, nz, rows, _ = arrived.shape
    ys, zs, rs, cs = window_at

    def step(i, carry):
        y, z = i // nz, i % nz
        at = (ys.start + y, zs.start + z, rs, cs)
        acc[at] = acc[at] + arrived[y, z]
        return carry

    if ny * nz == 1:
        step(0, 0)
    else:
        lax.fori_loop(0, ny * nz, step, 0)


def scatter_kernel(*refs):
    grads, extra, wholes, smalls = refs[:4], refs[4], refs[5:9], refs[9:12]
    accs, cores = refs[12:16], refs[16 : 16 + len(SCATTERED)]
    arrivals = refs[16 + len(SCATTERED) : -7]
    local_sem, core_send, core_recv, send_sem, recv_sem, last_send, last_recv = refs[-7:]
    section, y, z, core, x = place()
    near = neighbours(section, y, z, core, x)
    meet([near[name] for name in ("core", *HOPS, "xo")])

    loads, swaps = [], []
    for p, (array, column, columns, _) in enumerate(SCATTERED):
        cols = pl.ds(column, columns)
        grad = extra if (array, column) == (0, EXTRA) else grads[array].at[:, :, :, :, cols]
        swap = pltpu.make_async_remote_copy(
            src_ref=grad.at[:, :, 1 - core],
            dst_ref=cores[p],
            send_sem=core_send.at[p],
            recv_sem=core_recv.at[p],
            device_id=near["core"],
            device_id_type=MESH,
        )
        swap.start()
        load = pltpu.make_async_copy(
            grad.at[:, :, core], accs[array].at[:, :, :, cols], local_sem.at[p]
        )
        load.start()
        swaps.append(swap)
        loads.append(load)

    plans = [schedule(order, y, z, x) for _, _, _, order in SCATTERED]
    flying, last = {}, []
    sems = 0
    for stage in range(len(HOPS) + 1):
        for p, (array, column, columns, order) in enumerate(SCATTERED):
            quarter = SHARD_ROWS[array] // 4
            if stage == 0:
                loads[p].wait()
                swaps[p].wait_recv()
                add_into(accs[array], window(((0, 2), (0, 4), (0, 4)), quarter, column, columns), cores[p])
            else:
                kept = plans[p][stage - 1][1]
                for k, (copy, piece) in enumerate(zip(flying[p, stage - 1], kept)):
                    copy.wait_recv()
                    add_into(
                        accs[array],
                        window(piece, quarter, column, columns),
                        arrivals[p * len(HOPS) + stage - 1].at[k],
                    )
            if stage < len(HOPS):
                copies = []
                for k, piece in enumerate(plans[p][stage][0]):
                    copy = pltpu.make_async_remote_copy(
                        src_ref=accs[array].at[window(piece, quarter, column, columns)],
                        dst_ref=arrivals[p * len(HOPS) + stage].at[k],
                        send_sem=send_sem.at[sems],
                        recv_sem=recv_sem.at[sems],
                        device_id=near[order[stage]],
                        device_id_type=MESH,
                    )
                    copy.start()
                    copies.append(copy)
                    sems += 1
                flying[p, stage] = copies
                continue
            if p + 1 < len(SCATTERED) and SCATTERED[p + 1][0] == array:
                continue
            mine = pl.ds(pl.multiple_of(x * quarter, quarter), quarter)
            for k, name in enumerate(("xo", "xa", "xb")):
                copy = pltpu.make_async_remote_copy(
                    src_ref=accs[array].at[y, z, mine],
                    dst_ref=wholes[array].at[mine],
                    send_sem=last_send.at[array, k],
                    recv_sem=last_recv.at[array, k],
                    device_id=near[name],
                    device_id_type=MESH,
                )
                copy.start()
                last.append(copy)
            wholes[array][mine, :] = accs[array][y, z, mine, :]

    for copy in last:
        copy.wait_recv()
    small = wholes[0][:, EXTRA:].astype(F32)
    out_gains, out_conv, out_head = smalls
    out_conv[:, :56] = small[: CONV + 1, :56]
    out_conv[:, 56:] = small[8 : 9 + CONV, :56]
    out_gains[...] = small[16:18, :64]
    out_head[...] = small[24:27, :MHEADS]
    for copy in last + swaps + [c for copies in flying.values() for c in copies]:
        copy.wait_send()


def scatter_sums(grads, extra):
    n_copies = sum(shape[0] for shape in stage_shapes(SCATTERED))
    n_parts = len(SCATTERED)
    out_shapes = [
        *[jax.ShapeDtypeStruct(s, BF16) for s in zip(SHARD_ROWS, SUM_COLS)],
        *[jax.ShapeDtypeStruct(s, F32) for s in ((2, 64), (CONV + 1, T), (3, MHEADS))],
    ]
    return pl.pallas_call(
        scatter_kernel,
        in_specs=[pl.BlockSpec(memory_space=pl.ANY)] * 5,
        out_specs=[pl.BlockSpec(memory_space=pltpu.VMEM)] * 7,
        out_shape=out_shapes,
        scratch_shapes=[
            *[pltpu.VMEM((2, 4, r, c), BF16) for r, c in zip(SHARD_ROWS, SUM_COLS)],
            *[pltpu.VMEM((2, 4, SHARD_ROWS[a], cols), BF16) for a, _, cols, _ in SCATTERED],
            *[pltpu.VMEM(shape, BF16) for shape in stage_shapes(SCATTERED)],
            pltpu.SemaphoreType.DMA((n_parts,)),
            pltpu.SemaphoreType.DMA((n_parts,)),
            pltpu.SemaphoreType.DMA((n_parts,)),
            pltpu.SemaphoreType.DMA((n_copies,)),
            pltpu.SemaphoreType.DMA((n_copies,)),
            pltpu.SemaphoreType.DMA((4, 3)),
            pltpu.SemaphoreType.DMA((4, 3)),
        ],
        compiler_params=pltpu.CompilerParams(
            collective_id=1, has_side_effects=True, vmem_limit_bytes=58 * 1024 * 1024
        ),
        name="scatter_sums",
    )(*grads, extra)


def gather_kernel(*refs):
    shards, tail, outs = refs[:4], refs[4], refs[5:9]
    local_sem, send_sem, recv_sem, core_send, core_recv = refs[9:]
    section, y, z, core, x = place()
    near = neighbours(section, y, z, core, x)
    meet([near[name] for name in ("core", *HOPS)])

    def at(array, piece, column, columns):
        ys, zs, rows, cols = window(piece, SHARD_ROWS[array] // 4, column, columns)
        return outs[array].at[ys, zs, pl.ds(core, 1), rows, cols]

    def own(array, column, columns):
        quarter = SHARD_ROWS[array] // 4
        rows = pl.ds(pl.multiple_of(x * quarter, quarter), quarter)
        if (array, column) == (0, TAIL):
            return tail.at[:, :, :, rows]
        return shards[array].at[:, :, :, rows, pl.ds(column, columns)]

    passed = []

    def pass_on(source, target):
        k = len(passed)
        copy = pltpu.make_async_remote_copy(
            src_ref=source,
            dst_ref=target,
            send_sem=core_send.at[k],
            recv_sem=core_recv.at[k],
            device_id=near["core"],
            device_id_type=MESH,
        )
        copy.start()
        passed.append(copy)

    locals_ = []
    for p, (array, column, columns, _) in enumerate(GATHERED):
        copy = pltpu.make_async_copy(
            own(array, column, columns), at(array, ((y, 1), (z, 1), (x, 1)), column, columns), local_sem.at[p]
        )
        copy.start()
        locals_.append(copy)

    plans = [schedule(order, y, z, x)[::-1] for _, _, _, order in GATHERED]
    flying, sent = {}, []
    for stage in range(len(HOPS) + 1):
        for p, (array, column, columns, order) in enumerate(GATHERED):
            if stage:
                for copy in flying[p, stage - 1]:
                    copy.wait_recv()
            if stage == 1:
                locals_[p].wait()
            if stage < len(HOPS):
                copies = []
                for piece in plans[p][stage][1]:
                    target = at(array, piece, column, columns)
                    copy = pltpu.make_async_remote_copy(
                        src_ref=target if stage else own(array, column, columns),
                        dst_ref=target,
                        send_sem=send_sem.at[len(sent)],
                        recv_sem=recv_sem.at[len(sent)],
                        device_id=near[order[::-1][stage]],
                        device_id_type=MESH,
                    )
                    copy.start()
                    copies.append(copy)
                    sent.append(copy)
                flying[p, stage] = copies
            if stage:
                for piece in plans[p][stage - 1][0]:
                    here = at(array, piece, column, columns)
                    pass_on(here, here)
            else:
                pass_on(own(array, column, columns), at(array, ((y, 1), (z, 1), (x, 1)), column, columns))
    for copy in passed:
        copy.wait()
    for copy in sent:
        copy.wait_send()


def gather_shards(shards, tail):
    n_copies = sum(shape[0] for shape in stage_shapes(GATHERED))
    n_passed = n_copies + len(GATHERED)
    return pl.pallas_call(
        gather_kernel,
        in_specs=[pl.BlockSpec(memory_space=pl.ANY)] * 5,
        out_specs=[pl.BlockSpec(memory_space=pl.ANY)] * 4,
        out_shape=[
            jax.ShapeDtypeStruct((2, 4, 2, r, c), BF16) for r, c in zip(SHARD_ROWS, SHARD_COLS)
        ],
        scratch_shapes=[
            pltpu.SemaphoreType.DMA((len(GATHERED),)),
            pltpu.SemaphoreType.DMA((n_copies,)),
            pltpu.SemaphoreType.DMA((n_copies,)),
            pltpu.SemaphoreType.DMA((n_passed,)),
            pltpu.SemaphoreType.DMA((n_passed,)),
        ],
        compiler_params=pltpu.CompilerParams(collective_id=2, has_side_effects=True),
        name="gather_shards",
    )(*shards, tail)


def rms_norm(values, gain):
    return values * lax.rsqrt(jnp.mean(values * values, -1, keepdims=True) + 1e-05) * gain


def rms_back(values, gain, grad):
    scale = lax.rsqrt(jnp.mean(values * values, -1, keepdims=True) + 1e-05)
    unit = values * scale
    scaled = grad * gain
    grad_values = scale * (scaled - unit * jnp.mean(scaled * unit, -1, keepdims=True))
    return grad_values, jnp.sum(grad * unit, 0)


def forward_product(left, weight):
    return jnp.dot(left, weight, preferred_element_type=F32)


def back_product(grad_rows, weight):
    return lax.dot_general(
        grad_rows, weight, (((1,), (1,)), ((), ())), preferred_element_type=F32
    )


def outer_sum(left, right):
    return lax.dot_general(
        left, right, (((0,), (0,)), ((), ())), preferred_element_type=F32
    ).astype(BF16)


def layer_forward(inputs, weights, tables, keep):
    gains, w_in, w_out, w_gate_up, w_down = weights
    blocks = inputs.shape[0] // T
    normed = rms_norm(inputs, gains[0]).astype(BF16)
    projected = forward_product(normed, w_in)
    joined, *kept = mix_forward(projected.reshape(blocks, T, PAD), tables, keep)
    joined = joined.reshape(blocks * T, UW)
    hidden = inputs + forward_product(joined, w_out)
    normed_two = rms_norm(hidden, gains[1]).astype(BF16)
    gate_up = forward_product(normed_two, w_gate_up)
    activated = (jax.nn.silu(gate_up[:, :FF]) * gate_up[:, FF:]).astype(BF16)
    result = hidden + forward_product(activated, w_down)
    return result, (inputs, normed, projected, joined, hidden, normed_two, gate_up, activated, *kept)


def layer_backward(grad_out, saved, weights, tables):
    gains, w_in, w_out, w_gate_up, w_down = weights
    inputs, normed, projected, joined, hidden, normed_two, gate_up, activated, kept = saved
    blocks = inputs.shape[0] // T
    grad_ffn = grad_out.astype(BF16)
    grad_act = back_product(grad_ffn, w_down)
    gate, up = gate_up[:, :FF], gate_up[:, FF:]
    sig = jax.nn.sigmoid(gate)
    grad_gate = (grad_act * up * (sig * (1.0 + gate * (1.0 - sig)))).astype(BF16)
    grad_up = (grad_act * (gate * sig)).astype(BF16)
    grad_gate_up = jnp.concatenate([grad_gate, grad_up], 1)
    grad_hidden, grad_gain_two = rms_back(hidden, gains[1], back_product(grad_gate_up, w_gate_up))
    grad_hidden = grad_out + grad_hidden
    grad_branch = grad_hidden.astype(BF16)
    grad_joined = back_product(grad_branch, w_out)
    grad_proj, grad_conv, grad_head, grad_skip = mix_backward(
        projected.reshape(blocks, T, PAD), grad_joined.reshape(blocks, T, UW), kept, tables
    )
    grad_proj = grad_proj.reshape(blocks * T, PAD)
    grad_input, grad_gain_one = rms_back(inputs, gains[0], back_product(grad_proj, w_in))
    grad_input = grad_hidden + grad_input
    pairs = (
        (normed, grad_proj),
        (joined, grad_branch),
        (normed_two, grad_gate_up),
        (activated, grad_ffn),
    )
    return grad_input, pairs, (grad_gain_one, grad_gain_two, grad_conv, grad_head, grad_skip)


def across(array, by):
    return lax.ppermute(array, "section", [(0, 1)] if by > 0 else [(1, 0)])


def gather_weights(norm_gains, w_in, conv_params, w_out, w_gate_up, w_down):
    rows = w_in.shape[0]
    conv_rows = conv_params.T
    small = jnp.concatenate(
        [
            jnp.pad(conv_rows[:, :56], ((0, 3), (0, 8))),
            jnp.pad(conv_rows[:, 56:], ((0, 3), (0, 8))),
            norm_gains.T,
        ],
        0,
    )
    small = jnp.pad(small, ((0, rows - small.shape[0]), (0, PAD - PIN - 64)))
    tail = jnp.concatenate([w_in[:, TAIL:], small], 1)
    parts = gather_shards(
        [a.reshape(1, 1, 1, *a.shape) for a in (w_in, w_out, w_gate_up, w_down)],
        tail.reshape(1, 1, 1, *tail.shape),
    )
    small = parts[0][..., PIN : PIN + 64].reshape(-1, rows, 64)[:, :18].astype(F32)
    gains = small[:, 16:18].transpose(1, 0, 2).reshape(2, -1)
    conv_rows = small[:, :16, :56].reshape(-1, 2, 8, 56)[:, :, : CONV + 1]
    conv_rows = conv_rows.transpose(2, 0, 1, 3).reshape(CONV + 1, -1)
    return (gains, *[a.reshape(-1, a.shape[-1]) for a in parts]), conv_rows


def body(
    tokens,
    segment_ids,
    cotangent,
    norm_gains,
    w_in,
    conv_params,
    head_params,
    w_out,
    w_gate_up,
    w_down,
):
    section = lax.axis_index("section")
    blocks, _, width = tokens.shape
    rows = blocks * T
    weights, conv_rows = gather_weights(
        norm_gains[0], w_in[0], conv_params[0], w_out[0], w_gate_up[0], w_down[0]
    )
    tables = mixer_tables(segment_ids[:, 0], conv_rows, head_params[0].astype(F32))

    own = tokens.reshape(rows, width)
    first, _ = layer_forward(own.astype(F32), weights, tables, False)
    received = across(first.astype(BF16), 1)
    inputs = jnp.where(section == 0, own, received).astype(F32)
    result, saved = layer_forward(inputs, weights, tables, True)

    top = cotangent.reshape(rows, width)
    first_grad, _, _ = layer_backward(top.astype(F32), saved, weights, tables)
    coming = across(first_grad.astype(BF16), -1)
    grad_out = jnp.where(section == 1, top, coming).astype(F32)
    grad_input, pairs, smalls = layer_backward(grad_out, saved, weights, tables)

    grad_gain_one, grad_gain_two, grad_conv, grad_head, grad_skip = smalls
    sums = [outer_sum(left, right) for left, right in pairs]
    shards = lax.axis_size("shard")
    gains = jnp.stack([grad_gain_one, grad_gain_two]).reshape(2, shards, 64).transpose(1, 0, 2)
    conv = jnp.sum(grad_conv, 0).reshape(8, shards, 2, 56).transpose(1, 2, 0, 3)
    conv = conv.reshape(shards, 16, 56)
    skip = jnp.sum(jnp.sum(grad_skip, 0)[0].reshape(MHEADS, HEAD_WIDTH), 1)
    head = jnp.concatenate([jnp.sum(grad_head, 0)[:2, :MHEADS], skip[None]], 0)
    head = jnp.broadcast_to(head[None], (shards, 3, MHEADS))
    extra = jnp.concatenate(
        [
            jnp.pad(conv, ((0, 0), (0, 0), (0, 72))),
            jnp.pad(gains, ((0, 0), (0, 6), (0, 64))),
            jnp.pad(head, ((0, 0), (0, 37), (0, 128 - MHEADS))),
        ],
        1,
    ).astype(BF16)
    out_in, out_out, out_gu, out_dn, out_gains, out_conv, out_head = scatter_sums(
        [g.reshape(2, 4, 2, g.shape[0] // 16, g.shape[1]) for g in sums],
        extra.reshape(2, 4, 2, 64, 128),
    )
    return (
        result.astype(BF16).reshape(1, blocks, T, width),
        grad_input.reshape(1, blocks, T, width),
        out_gains.T[None],
        out_in[None, :, :PIN].astype(F32),
        out_conv.T[None],
        out_head.T[None],
        out_out[None].astype(F32),
        out_gu[None].astype(F32),
        out_dn[None].astype(F32),
    )


def solution(mesh):
    in_specs = (
        P(None, ("shard", "rep"), None),
        P(None, ("shard", "rep"), None),
        P(None, ("shard", "rep"), None),
        P("section", "shard", None),
        P("section", "shard", None),
        P("section", "shard", None),
        P("section", None, None),
        P("section", "shard", None),
        P("section", "shard", None),
        P("section", "shard", None),
    )
    out_specs = (
        P("section", None, ("shard", "rep"), None),
        P("section", None, ("shard", "rep"), None),
        P("section", "shard", None),
        P("section", "shard", None),
        P("section", "shard", None),
        P("section", None, None),
        P("section", "shard", None),
        P("section", "shard", None),
        P("section", "shard", None),
    )
    return jax.shard_map(body, mesh=mesh, in_specs=in_specs, out_specs=out_specs, check_vma=False)
```
